32 devices in a mesh: dp: 8 (over y, x, core), tensor: 4 (over z).
Axes of the slice: x: 2, y: 2, z: 4, core: 2. Of those that a mesh axis runs over, the one named last changes fastest.
Arguments:
- inputs: bfloat16 [8192, 2048], P(('dp', 'tensor')), may hold values from -6 to 6
- gain_attn: bfloat16 [2048], P('dp'), may hold values from 0.5 to 1.5
- w_query: bfloat16 [2048, 2048], P('dp', 'tensor'), may hold values from -0.125 to 0.125
- w_key: bfloat16 [2048, 2048], P('dp', 'tensor'), may hold values from -0.125 to 0.125
- w_value: bfloat16 [2048, 4096], P('dp', 'tensor'), may hold values from -0.125 to 0.125
- w_gate: bfloat16 [2048, 4096], P('dp', 'tensor'), may hold values from -0.125 to 0.125
- w_out: bfloat16 [4096, 2048], P('tensor', 'dp'), may hold values from -0.125 to 0.125
- gain_mlp: bfloat16 [2048], P('dp'), may hold values from 0.5 to 1.5
- w_act: bfloat16 [2048, 4096], P('dp', 'tensor'), may hold values from -0.125 to 0.125
- w_lin: bfloat16 [2048, 4096], P('dp', 'tensor'), may hold values from -0.125 to 0.125
- w_down: bfloat16 [4096, 2048], P('tensor', 'dp'), may hold values from -0.125 to 0.125
- cotangent: bfloat16 [8192, 2048], P(('dp', 'tensor')), may hold values from -6 to 6
- lengths: int32 [8, 3], P('dp'), may hold values from 1 to 896, as said below
- offsets: int32 [8, 3], P('dp'), may hold values from 0 to 960, as said below
Outputs:
- outputs: bfloat16 [8192, 2048], P(('dp', 'tensor'))
- grad_inputs: float32 [8192, 2048], P(('dp', 'tensor'))
- grad_gain_attn: float32 [2048], P('dp')
- grad_w_query: float32 [2048, 2048], P('dp', 'tensor')
- grad_w_key: float32 [2048, 2048], P('dp', 'tensor')
- grad_w_value: float32 [2048, 4096], P('dp', 'tensor')
- grad_w_gate: float32 [2048, 4096], P('dp', 'tensor')
- grad_w_out: float32 [4096, 2048], P('tensor', 'dp')
- grad_gain_mlp: float32 [2048], P('dp')
- grad_w_act: float32 [2048, 4096], P('dp', 'tensor')
- grad_w_lin: float32 [2048, 4096], P('dp', 'tensor')
- grad_w_down: float32 [4096, 2048], P('tensor', 'dp')
The draws below stay inside these ranges and needn't reach their ends.
Inputs may be any that keep to these rules, and one draw needn't show every extreme that they name: `lengths`: each group holds 3 sequences; the first is the longest. `offsets`: multiples of 64; in each group the first sequence starts at 0, later ones start after the earlier ones end, and the last ends at most at 1024.
All inputs are finite; a program needn't handle non-finite values.
Results may differ from the reference program's by a relative error of at most 0.024.
Values may be sent and summed in bfloat16 or wider, within the bound.
No kernel may reach another device: no remote copies, remote signals or barrier semaphores. Data moves between devices by JAX's collectives and lax.ppermute only.
A program may use at most 192 MiB of HBM per device.

```python
import functools
import math
import jax
import jax.numpy as jnp
from jax import lax

D = 2048
HEADS = 8
KD = 256
VD = 512
FF = 4096
CAP = 1024
SLOTS = 3
BLOCK = 512
ALIGN = 64
TOKENS = 8192
N_DP = 8


def sequence_plan(key):
    blocks_total = CAP // ALIGN
    subkeys = jax.random.split(key, 4)
    filled = jax.random.randint(subkeys[0], (N_DP,), blocks_total // 2, blocks_total + 1)
    fullest = jax.random.randint(subkeys[1], (), 0, N_DP)
    is_fullest = jnp.arange(N_DP) == fullest
    filled = jnp.where(is_fullest, blocks_total, filled)
    drawn = jax.random.randint(subkeys[2], (N_DP, SLOTS - 1), 0, 1 << 20)
    bounds = jnp.maximum(filled // (2 * (SLOTS - 1)), 1)
    shorter = 1 + jnp.remainder(drawn, bounds[:, None])
    shorter = jnp.where(is_fullest[:, None], 1, shorter)
    longest = filled - jnp.sum(shorter, axis=1)
    blocks = jnp.concatenate([longest[:, None], shorter], axis=1)
    leftover = blocks_total - filled
    finishes = jnp.cumsum(blocks, axis=1)
    starts = finishes - blocks + jnp.where(jnp.arange(SLOTS)[None, :] > 0, leftover[:, None], 0)
    trimmed = jax.random.randint(subkeys[3], (N_DP, SLOTS), 0, ALIGN)
    keep_whole = is_fullest[:, None] & (jnp.arange(SLOTS)[None, :] == 0)
    trimmed = jnp.where(keep_whole, 0, trimmed)
    return ((blocks * ALIGN - trimmed).astype(jnp.int32), (starts * ALIGN).astype(jnp.int32))


def draw_lengths(key, part):
    return sequence_plan(key)[0]


def draw_offsets(key, part):
    return sequence_plan(key)[1]


def block_scale(stream_key, dims, shards, least, high):
    def one(dim, parts):
        draws = jax.random.uniform(jax.random.fold_in(jax.random.fold_in(stream_key, 6), dim), (parts,), jnp.float32, least / len(shards), high / len(shards))
        return jnp.repeat(jnp.exp(draws), dims[dim] // parts).reshape((-1,) + (1,) * (len(dims) - dim - 1))

    factor_of = one(*shards[0])
    for cut in shards[1:]:
        factor_of = factor_of * one(*cut)
    return factor_of


def bell_draw(rng, extent, deviation, limit, pieces=(), held_as=jnp.bfloat16):
    entries = jax.random.normal(rng, extent, jnp.float32) * deviation
    if len(pieces) > 0:
        entries = block_scale(rng, extent, pieces, -0.22, 0.18) * entries
    return jnp.clip(entries, min=-limit, max=limit).astype(held_as)


def setup_inputs(seed: int = 0) -> dict:
    splits = jax.random.split(jax.random.key(seed), 15)
    return {
        "inputs": bell_draw(splits[0], (TOKENS, D), 1.0, 6.0, ((0, 32),)),
        "gain_attn": jnp.clip(1.0 + 0.1 * jax.random.normal(splits[1], (D,), jnp.float32), 0.5, 1.5).astype(jnp.bfloat16),
        "w_query": bell_draw(splits[2], (D, HEADS * KD), D ** -0.5, 0.125, ((0, 8), (1, 4))),
        "w_key": bell_draw(splits[3], (D, HEADS * KD), D ** -0.5, 0.125, ((0, 8), (1, 4))),
        "w_value": bell_draw(splits[4], (D, HEADS * VD), D ** -0.5, 0.125, ((0, 8), (1, 4))),
        "w_gate": bell_draw(splits[5], (D, HEADS * VD), D ** -0.5, 0.125, ((0, 8), (1, 4))),
        "w_out": bell_draw(splits[6], (HEADS * VD, D), D ** -0.5, 0.125, ((0, 4), (1, 8))),
        "gain_mlp": jnp.clip(1.0 + 0.1 * jax.random.normal(splits[7], (D,), jnp.float32), 0.5, 1.5).astype(jnp.bfloat16),
        "w_act": bell_draw(splits[8], (D, FF), D ** -0.5, 0.125, ((0, 8), (1, 4))),
        "w_lin": bell_draw(splits[9], (D, FF), D ** -0.5, 0.125, ((0, 8), (1, 4))),
        "w_down": bell_draw(splits[10], (FF, D), (FF // 2) ** -0.5, 0.125, ((0, 4), (1, 8))),
        "cotangent": bell_draw(splits[11], (TOKENS, D), 1.0, 6.0, ((0, 32),)),
        "lengths": draw_lengths(jax.random.fold_in(splits[14], 71), 0),
        "offsets": draw_offsets(jax.random.fold_in(splits[14], 71), 0),
    }


highest_precision = lax.Precision.HIGHEST
epsilon = 1e-05
group_floor = 1.0

@jax.custom_vjp
def low(v):
    return lax.optimization_barrier(v.astype(jnp.bfloat16)).astype(jnp.float32)

@jax.custom_vjp
def low_back(v):
    return v

def low_keep(v):
    return (low(v), None)

def low_pass(kept, grad):
    return (grad,)

def back_keep(v):
    return (v, None)

def back_low(kept, grad):
    return (low(grad),)
low.defvjp(low_keep, low_pass)
low_back.defvjp(back_keep, back_low)

def layer_norm(values, floor_value=epsilon):
    center = values - lax.optimization_barrier(jnp.mean(values, axis=-1, keepdims=True))
    scale_inv = lax.rsqrt(lax.optimization_barrier(jnp.mean(center * center, axis=-1, keepdims=True)) + floor_value)
    return center * scale_inv

def sequence_layout(lengths, offsets, total):
    places = jnp.arange(total, dtype=jnp.int32)[:, None]
    inside = (places >= offsets[None, :]) & (places < offsets[None, :] + lengths[None, :])
    numbers = jnp.arange(1, offsets.shape[0] + 1, dtype=jnp.int32)
    segment = (lax.optimization_barrier(jnp.sum(jnp.where(inside, numbers[None, :], 0), axis=1)) - 1).astype(jnp.int32)
    position = places[:, 0] - lax.optimization_barrier(jnp.sum(jnp.where(inside, offsets[None, :], 0), axis=1))
    return (segment, position.astype(jnp.float32))

def rotate(values, position, direction):
    half = values.shape[-1] // 2
    frequency = jnp.exp(-math.log(10000.0) * jnp.arange(half, dtype=jnp.float32) * 2.0 / values.shape[-1])
    angles = position[:, None] * frequency[None, :]
    cosine = jnp.cos(angles)
    sine = jnp.sin(angles) * direction
    first = values[..., :half]
    second = values[..., half:]
    return jnp.concatenate([first * cosine - second * sine, first * sine + second * cosine], axis=-1)

def block_consts(segment, start, log_decay, size):
    seg_block = lax.dynamic_slice_in_dim(segment, start, size)
    before = lax.dynamic_slice_in_dim(segment, jnp.maximum(start - 1, 0).astype(jnp.int32), 1)[0]
    before = jnp.where(start > 0, before, -2)
    final = seg_block[size - 1]
    places = jnp.arange(size, dtype=jnp.int32)
    living = seg_block >= 0
    same = (seg_block[:, None] == seg_block[None, :]) & living[:, None] & (places[None, :] <= places[:, None])
    spacing = jnp.maximum(places[:, None] - places[None, :], 0).astype(jnp.float32)
    decay = jnp.where(same[None], jnp.exp(spacing[None] * log_decay[:, None, None]), 0.0)
    inward_state = ((seg_block == before) & living).astype(jnp.float32)[None, :] * jnp.exp((places + 1).astype(jnp.float32)[None, :] * log_decay[:, None])
    outward_state = ((seg_block == final) & living).astype(jnp.float32)[None, :] * jnp.exp((size - 1 - places).astype(jnp.float32)[None, :] * log_decay[:, None])
    carried_state = jnp.where((final == before) & (final >= 0), jnp.exp(size * log_decay), 0.0)
    return (decay, inward_state, outward_state, carried_state)

def block_step(log_decay, segment, recurrent_state, item):
    index, query_block_rows, key_block_rows, value_block_rows = item
    decay, inward_state, outward_state, carried_state = block_consts(segment, index * BLOCK, log_decay, BLOCK)
    scores = low_back(jnp.einsum('hik,hjk->hij', query_block_rows, key_block_rows, precision=highest_precision))
    weights = low(decay * scores)
    inner = jnp.einsum('hij,hjv->hiv', weights, value_block_rows, precision=highest_precision)
    cross_scores = inward_state[..., None] * jnp.einsum('zpu,zud->zpd', query_block_rows, recurrent_state, precision=highest_precision)
    updated_state = carried_state[:, None, None] * recurrent_state + jnp.einsum('eaw,eag->ewg', key_block_rows * outward_state[..., None], value_block_rows, precision=highest_precision)
    return (updated_state, inner + cross_scores)

def retain(query_rot, key_rot, values, segment, log_decay):
    heads, total, key_size = query_rot.shape
    value_size = values.shape[2]
    count = total // BLOCK

    def to_blocks(tensor):
        return tensor.reshape(heads, count, BLOCK, tensor.shape[2]).transpose(1, 0, 2, 3)
    start_state = jnp.zeros((heads, key_size, value_size), jnp.float32)
    step = jax.checkpoint(functools.partial(block_step, log_decay, segment))
    _, blocks = lax.scan(step, start_state, (jnp.arange(count, dtype=jnp.int32), to_blocks(query_rot), to_blocks(key_rot), to_blocks(values)))
    return blocks.transpose(1, 0, 2, 3).reshape(heads, total, value_size)

def split_heads(matrix, heads):
    return matrix.reshape(matrix.shape[0], heads, -1).transpose(1, 0, 2)

def join_heads(tensor):
    return tensor.transpose(1, 0, 2).reshape(tensor.shape[1], -1)

def group_layer(rows, lengths, offsets, params):
    gain_one, w_query, w_key, w_value, w_gate, w_out, gain_two, w_act, w_lin, w_down = params
    segment, position = sequence_layout(lengths, offsets, CAP)
    log_decay = jnp.log(1.0 - jnp.exp2(-5.0 - jnp.arange(HEADS, dtype=jnp.float32)))
    h_attn = low(layer_norm(rows) * gain_one)
    query = low_back(split_heads(jnp.dot(h_attn, w_query, precision=highest_precision), HEADS))
    keys = low_back(split_heads(jnp.dot(h_attn, w_key, precision=highest_precision), HEADS))
    query_rot = low(rotate(query, position, 1.0) * KD ** (-0.5))
    key_rot = low(rotate(keys, position, 1.0))
    values = low(low_back(split_heads(jnp.dot(h_attn, w_value, precision=highest_precision), HEADS)))
    gate_pre = low_back(split_heads(jnp.dot(h_attn, w_gate, precision=highest_precision), HEADS))
    retained = low_back(retain(query_rot, key_rot, values, segment, log_decay))
    grouped = layer_norm(retained, group_floor)
    mixed = low(join_heads(jax.nn.silu(gate_pre) * grouped))
    middle = rows + low_back(jnp.dot(mixed, w_out, precision=highest_precision))
    h_mlp = low(layer_norm(middle) * gain_two)
    act = low_back(jnp.dot(h_mlp, w_act, precision=highest_precision))
    lin = low_back(jnp.dot(h_mlp, w_lin, precision=highest_precision))
    hidden = low(jax.nn.gelu(act) * lin)
    return middle + low_back(jnp.dot(hidden, w_down, precision=highest_precision))

def reference(inputs, gain_attn, w_query, w_key, w_value, w_gate, w_out, gain_mlp, w_act, w_lin, w_down, cotangent, lengths, offsets):
    floats = tuple((a.astype(jnp.float32) for a in (inputs, gain_attn, w_query, w_key, w_value, w_gate, w_out, gain_mlp, w_act, w_lin, w_down)))

    def forward(rows_all, *params):
        groups = rows_all.reshape(N_DP, CAP, rows_all.shape[1])

        def one_group(item):
            return group_layer(item[0], item[1], item[2], params)
        result = lax.map(jax.checkpoint(one_group), (groups, lengths, offsets))
        return result.reshape(N_DP * CAP, rows_all.shape[1])
    result, backward = jax.vjp(forward, *floats)
    grads = backward(cotangent.astype(jnp.float32))
    return (result.astype(jnp.bfloat16), grads[0], grads[1], grads[2], grads[3], grads[4], grads[5], grads[6], grads[7], grads[8], grads[9], grads[10])
```

```python
import functools
import math

import jax
import jax.numpy as jnp
from jax import lax
from jax.experimental import pallas as pl
from jax.experimental.pallas import tpu as pltpu
from jax.sharding import PartitionSpec as P

KD = 256
VD = 512
TILE = 256

epsilon = 1e-05
group_floor = 1.0
f32 = jnp.float32
low = jnp.bfloat16
gelu_slope = math.sqrt(2.0 / math.pi)
gelu_cubic = 0.044715


def layer_norm(values, floor_value=epsilon):
    center = values - jnp.mean(values, axis=-1, keepdims=True)
    scale_inv = lax.rsqrt(jnp.mean(center * center, axis=-1, keepdims=True) + floor_value)
    return (center * scale_inv, scale_inv)


def norm_back(grad_norm, normed, scale_inv):
    mean_grad = jnp.mean(grad_norm, axis=-1, keepdims=True)
    mean_cross = jnp.mean(grad_norm * normed, axis=-1, keepdims=True)
    return (grad_norm - mean_grad - normed * mean_cross) * scale_inv


def sequence_layout(lengths, offsets, total):
    places = jnp.arange(total, dtype=jnp.int32)[:, None]
    inside = (places >= offsets[None, :]) & (places < offsets[None, :] + lengths[None, :])
    numbers = jnp.arange(1, offsets.shape[0] + 1, dtype=jnp.int32)
    segment = jnp.sum(jnp.where(inside, numbers[None, :], 0), axis=1) - 1
    position = places[:, 0] - jnp.sum(jnp.where(inside, offsets[None, :], 0), axis=1)
    return (segment, position.astype(f32))


def rotation(position, size):
    half = size // 2
    frequency = jnp.exp(-math.log(10000.0) * jnp.arange(half, dtype=f32) * 2.0 / size)
    angles = position[:, None] * frequency[None, :]
    return (jnp.cos(angles), jnp.sin(angles))


def dot(left, right):
    return jnp.dot(left, right, preferred_element_type=f32)


def dot_nt(left, right):
    return lax.dot_general(left, right, (((1,), (1,)), ((), ())), preferred_element_type=f32)


def dot_tn(left, right):
    return lax.dot_general(left, right, (((0,), (0,)), ((), ())), preferred_element_type=f32)


def add_low(left, right):
    return (left.astype(f32) + right.astype(f32)).astype(low)


def swap(values, axis, bits, name="swap"):
    size = lax.axis_size(axis)
    with jax.named_scope(f"{name}_{axis}{bits}"):
        return lax.ppermute(values, axis, [(i, i ^ bits) for i in range(size)])


def shift(values, axis, step, name="shift"):
    size = lax.axis_size(axis)
    with jax.named_scope(name):
        return lax.ppermute(values, axis, [(i, (i + step) % size) for i in range(size)])


def tie(values, token):
    return values if token is None else lax.optimization_barrier((values, token))[0]


def pick(tokens, stage):
    return tokens[min(stage, len(tokens) - 1)] if tokens else None


def dp_bits(size):
    bits = [1 << b for b in range(1, size.bit_length() - 1)]
    return list(zip(bits, bits[1:] + bits[:1]))


def feature_order(size):
    same = []
    for half in (0, 1):
        held = [0]
        for bits in dp_bits(size):
            held += [k ^ bits[half] for k in held]
        same += [(k, half) for k in held]
    return same + [(k ^ 1, half) for k, half in same]


def gather_start(block):
    half = block.shape[0] // 2
    return [block[:half], block[half:]]


def gather_step(parts, stage, name):
    bits = dp_bits(lax.axis_size("dp"))[stage]
    return [
        jnp.concatenate([part, swap(part, "dp", bit, name)], axis=0)
        for part, bit in zip(sync(*parts), bits)
    ]


def gather_rest(parts, stage, name):
    for step in range(stage, len(dp_bits(lax.axis_size("dp")))):
        parts = gather_step(parts, step, name)
    return jnp.concatenate(parts, axis=0)


def scatter_step(parts, stage, name):
    bits = dp_bits(lax.axis_size("dp"))[-1 - stage]
    sums = []
    for (kept, sent), bit in zip(sync(*parts), bits):
        came = swap(sent, "dp", bit, name)
        half = kept.shape[0] // 2
        sums.append([add_low(kept[i : i + half], came[i : i + half]) for i in (0, half)])
    return sums


def scatter_rest(parts, stage, name):
    for step in range(stage, len(dp_bits(lax.axis_size("dp")))):
        parts = scatter_step(parts, step, name)
    return jnp.concatenate([half for part in parts for half in part], axis=0)


def sync(*values):
    return lax.optimization_barrier(values)


def gather_ring(rows, name, beside):
    pieces = [rows]
    for step in range(1, lax.axis_size("tensor")):
        came = shift(pieces[-1], "tensor", 1, f"{name}_{step}")
        pieces.append(beside(step, came))
    return pieces


def call(kernel, grid, in_specs, out_specs, out_shape, flops, scratch=(), scalars=0, aliases=None, moved=0, exps=0):
    return pl.pallas_call(
        kernel,
        grid_spec=pltpu.PrefetchScalarGridSpec(
            num_scalar_prefetch=scalars,
            grid=grid,
            in_specs=in_specs,
            out_specs=out_specs,
            scratch_shapes=scratch,
        ),
        out_shape=out_shape,
        input_output_aliases=aliases or {},
        compiler_params=pltpu.CompilerParams(
            dimension_semantics=("arbitrary",) * len(grid), vmem_limit_bytes=48 * 1024 * 1024
        ),
        cost_estimate=pl.CostEstimate(flops=0, bytes_accessed=0, transcendentals=0),
    )


def reorder_kernel(table, values, out):
    count = table.shape[0]
    width = values.shape[1] // count
    for place in range(count):
        start = pl.multiple_of(table[place] * width, width)
        out[:, place * width : (place + 1) * width] = values[:, pl.ds(start, width)]


def reorder(values, table):
    count, (rows, width) = table.shape[0], values.shape
    size = width // count
    if size % 128:
        blocks = [
            lax.dynamic_slice_in_dim(values, table[i] * size, size, axis=1) for i in range(count)
        ]
        return jnp.concatenate(blocks, axis=1)
    part = min(rows, 64)
    spec = pl.BlockSpec((part, width), lambda i, _: (i, 0))
    return call(
        reorder_kernel,
        (rows // part,),
        [spec],
        spec,
        jax.ShapeDtypeStruct(values.shape, values.dtype),
        0,
        scalars=1,
        moved=2 * values.size * values.dtype.itemsize,
    )(table, values)


def project_kernel(count, places, *refs):
    own, other, out = refs[count], refs[count + 1], refs[-1]
    half = own.shape[0]
    for i in range(count):
        rows = refs[i]
        size = rows.shape[0]
        start = pl.multiple_of(places[i] * size, size) if out.shape[0] > size else 0
        out[pl.ds(start, size), :] = dot(rows[:, :half], own[...]) + dot(rows[:, half:], other[...])


def project(pieces, weight, whole, places, chunks):
    own, other = weight
    (count, width), columns = pieces[0].shape, own.shape[1]
    size = 512 if columns % 512 == 0 else TILE
    spec = pl.BlockSpec((width // 2, size), lambda j, _: (0, j))
    rows = pl.BlockSpec((count, width), lambda j, _: (0, 0))
    number = len(pieces)
    if whole is None:
        held, out = [], pl.BlockSpec((count * chunks, size), lambda j, _: (0, j))
    else:
        held, out = [whole], pl.BlockSpec((count, size), lambda j, at: (at[0], j))
    return call(
        functools.partial(project_kernel, number),
        (columns // size,),
        [rows] * number + [spec, spec] + [pl.BlockSpec(memory_space=pl.ANY)] * len(held),
        out,
        jax.ShapeDtypeStruct((count * chunks, columns), f32),
        2 * number * count * width * columns,
        scalars=1,
        aliases={number + 3: 0} if held else None,
        moved=2 * width * columns + 4 * number * count * columns,
    )(jnp.stack(places), *pieces, own, other, *held)


def terms_kernel(count, paired, places, *refs):
    own, other, outs = refs[count], refs[count + 1], refs[count + 2 :]
    pairs, outs = outs[: count * paired], outs[count * paired :]

    def give(weight):
        sums = 0.0
        for i, rows in enumerate(refs[:count]):
            result = dot_nt(rows[...], weight[...])
            outs[i][...] = result.astype(outs[i].dtype)
            if paired:
                sums = sums + jnp.sum(result * pairs[i][...].astype(f32), axis=0, keepdims=True)
        if paired:
            outs[count][...] = sums

    pl.when(pl.program_id(0) == 0)(lambda: give(own))
    pl.when(pl.program_id(0) == 1)(lambda: give(other))


def terms(whole, weight, places, size, kinds, pairs):
    own, other = weight
    half, depth = own.shape
    tile = min(half, 1024 if depth <= 1024 else 512)
    steps = half // tile
    number = len(places)
    rows = [
        pl.BlockSpec((size, depth), lambda i, j, at, n=n: (at[n], 0)) for n in range(number)
    ]
    out = lambda height: pl.BlockSpec((height, tile), lambda i, j, _: (0, i * steps + j))
    paired = 1 if pairs else 0
    return call(
        functools.partial(terms_kernel, number, paired),
        (2, steps),
        rows
        + [
            pl.BlockSpec((tile, depth), lambda i, j, _: (jnp.where(i == 0, j, steps - 1), 0)),
            pl.BlockSpec((tile, depth), lambda i, j, _: (jnp.where(i == 0, 0, j), 0)),
        ]
        + [out(size)] * (number * paired),
        [out(size)] * number + [out(1)] * paired,
        [jax.ShapeDtypeStruct((size, 2 * half), kind) for kind in kinds]
        + [jax.ShapeDtypeStruct((1, 2 * half), f32)] * paired,
        4 * number * size * depth * half,
        scalars=1,
        moved=4 * depth * half + 8 * number * size * half,
    )(jnp.stack(places), *([whole] * number), own, other, *(pairs or []))


def scatter_ring(whole, weight, count, name, beside, pairs=None):
    own, size = lax.axis_index("tensor"), lax.axis_size("tensor")
    places = [(own - step) % size for step in range(1, size + 1)]
    pairs = pairs and pairs[1:] + pairs[:1]
    total, *first = terms(whole, weight, places[:1], count, [low], pairs and pairs[:1])
    late = tie(whole, total)
    rest = terms(late, weight, places[1:], count, [f32] * (size - 1), pairs and pairs[1:])
    more = first[0] + rest[-1] if pairs else None
    for step in range(1, size):
        came = shift(total, "tensor", 1, f"{name}_{step}")
        if step == 1:
            came = tie(came, (rest, more))
        came = beside(step, came, more)
        total = came.astype(f32) + rest[step - 1]
        if step < size - 1:
            total = total.astype(low)
    return total


def norm_kernel(values, added, gain, middle, out):
    rows = values[...].astype(f32) + added[...]
    middle[...] = rows
    out[...] = (layer_norm(rows)[0] * gain[...]).astype(low)


def norm_rows(values, added, gain):
    count, width = values.shape
    size = min(count, 128)
    rows = pl.BlockSpec((size, width), lambda i: (i, 0))
    return call(
        norm_kernel,
        (count // size,),
        [rows, rows, pl.BlockSpec((1, width), lambda i: (0, 0))],
        [rows, rows],
        [jax.ShapeDtypeStruct((count, width), f32), jax.ShapeDtypeStruct((count, width), low)],
        0,
        moved=count * width * 12,
    )(values, added, gain[None])


def norm_back_kernel(added, values, base, gain, grad, *refs):
    outs = refs[added:]
    given = grad[...]
    if added:
        given = given + refs[0][...].astype(f32)
    normed, scale = layer_norm(values[...].astype(f32))
    result = base[...].astype(f32) + norm_back(given * gain[...], normed, scale)
    outs[0][...] = result
    if len(outs) == 1:
        return
    term = jnp.sum(given * normed, axis=0, keepdims=True)

    @pl.when(pl.program_id(0) == 0)
    def _():
        outs[1][...] = term

    @pl.when(pl.program_id(0) != 0)
    def _():
        outs[1][...] += term

    outs[2][...] = result.astype(low)


def norm_back_rows(values, base, gain, grad, came=None):
    count, width = values.shape
    size = min(count, 128)
    rows = pl.BlockSpec((size, width), lambda i: (i, 0))
    line = pl.BlockSpec((1, width), lambda i: (0, 0))
    more = [] if came is None else [came]
    return call(
        functools.partial(norm_back_kernel, len(more)),
        (count // size,),
        [rows, rows, line, rows] + [rows] * len(more),
        [rows] + [line, rows] * len(more),
        [jax.ShapeDtypeStruct((count, width), f32)]
        + [jax.ShapeDtypeStruct((1, width), f32), jax.ShapeDtypeStruct((count, width), low)]
        * len(more),
        0,
        moved=count * width * 16,
    )(values, base, gain[None], grad, *more)


def place_masks(size):
    row = lax.broadcasted_iota(jnp.int32, (size, size), 0)
    column = lax.broadcasted_iota(jnp.int32, (size, size), 1)
    return row, column


def block_decay(powers, head, apart, base, row, column, after, before):
    kept = (after == before) & (after >= 0)
    if apart == 0:
        kept = kept & (column <= row)
        return jnp.where(kept, base, 0.0)
    return jnp.where(kept, base * powers[head, apart], 0.0)


def retain_kernel(powers, logs, pre, cosine, sine, after, before, mixed, kept, grouped, scale):
    head = pl.program_id(0)
    total = pre.shape[0]
    half = KD // 2
    cos, sin = cosine[...], sine[...]
    for first, factor in ((0, KD ** (-0.5)), (KD, 1.0)):
        a, b = pre[:, first : first + half], pre[:, first + half : first + KD]
        kept[:, first : first + half] = ((a * cos - b * sin) * factor).astype(low)
        kept[:, first + half : first + KD] = ((a * sin + b * cos) * factor).astype(low)
    kept[:, 2 * KD :] = pre[:, 2 * KD : 2 * KD + VD].astype(low)
    row, column = place_masks(TILE)
    base = jnp.exp((row - column).astype(f32) * logs[head])
    for i in range(total // TILE):
        rows = slice(i * TILE, (i + 1) * TILE)
        held = jnp.zeros((TILE, VD), f32)
        for j in range(i + 1):
            past = slice(j * TILE, (j + 1) * TILE)
            decay = block_decay(powers, head, i - j, base, row, column, after[rows, :], before[:, past])
            scores = dot_nt(kept[rows, :KD], kept[past, KD : 2 * KD])
            held = held + dot((decay * scores).astype(low), kept[past, 2 * KD :])
        normed, inverse = layer_norm(held, group_floor)
        grouped[rows, :] = normed
        scale[rows, :] = jnp.broadcast_to(inverse, (TILE, 128))
        gate = pre[rows, 2 * KD + VD :]
        mixed[rows, :] = (gate * jax.nn.sigmoid(gate) * normed).astype(low)


def retain(pre, consts, heads):
    total = pre.shape[0]
    powers, logs, cosine, sine, after, before = consts
    whole = lambda a: pl.BlockSpec(a.shape, lambda h: (0, 0))
    smem = pl.BlockSpec(memory_space=pltpu.SMEM)
    by_head = lambda width: pl.BlockSpec((total, width), lambda h: (0, h))
    shape = lambda width, kind: jax.ShapeDtypeStruct((total, heads * width), kind)
    return call(
        retain_kernel,
        (heads,),
        [smem, smem, by_head(2 * KD + 2 * VD), whole(cosine), whole(sine), whole(after), whole(before)],
        [by_head(VD), by_head(2 * KD + VD), by_head(VD), by_head(128)],
        [shape(VD, low), shape(2 * KD + VD, low), shape(VD, f32), shape(128, f32)],
        heads * total * total * (KD + VD) * 5 // 4,
        moved=heads * total * (1536 * 4 + 512 * 2 + 1024 * 2 + 512 * 4 + 512),
        exps=heads * total * 600,
    )(*consts[:2], pre, *consts[2:])


def retain_back_kernel(
    powers, logs, grad, gates, kept, grouped, scale, cosine, sine, after, before, out, grad_low, grad_q, grad_k, grad_v
):
    head = pl.program_id(0)
    total = kept.shape[0]
    half = KD // 2
    blocks = total // TILE
    for i in range(blocks):
        rows = slice(i * TILE, (i + 1) * TILE)
        gate, normed, given = gates[rows, :], grouped[rows, :], grad[rows, :]
        sigmoid = jax.nn.sigmoid(gate)
        out[rows, 2 * KD + VD :] = (
            given * normed * sigmoid * (1.0 + gate * (1.0 - sigmoid))
        ).astype(low)
        grad_low[rows, :] = norm_back(given * (gate * sigmoid), normed, scale[rows, :1]).astype(low)
    row, column = place_masks(TILE)
    base = jnp.exp((row - column).astype(f32) * logs[head])
    for i in range(blocks):
        rows = slice(i * TILE, (i + 1) * TILE)
        query, grad_rows = kept[rows, :KD], grad_low[rows, :]
        held = jnp.zeros((TILE, KD), f32)
        for j in range(i + 1):
            past = slice(j * TILE, (j + 1) * TILE)
            decay = block_decay(powers, head, i - j, base, row, column, after[rows, :], before[:, past])
            key, value = kept[past, KD : 2 * KD], kept[past, 2 * KD :]
            weights = (decay * dot_nt(query, key)).astype(low)
            grad_scores = (dot_nt(grad_rows, value) * decay).astype(low)
            held = held + dot(grad_scores, key)
            key_term, value_term = dot_tn(grad_scores, query), dot_tn(weights, grad_rows)
            if i == j:
                grad_k[past, :], grad_v[past, :] = key_term, value_term
            else:
                grad_k[past, :] += key_term
                grad_v[past, :] += value_term
        grad_q[rows, :] = held
    cos, sin = cosine[...], sine[...]
    for first, source, factor in ((0, grad_q, KD ** (-0.5)), (KD, grad_k, 1.0)):
        a, b = source[:, :half] * factor, source[:, half:] * factor
        out[:, first : first + half] = (a * cos + b * sin).astype(low)
        out[:, first + half : first + KD] = (b * cos - a * sin).astype(low)
    out[:, 2 * KD : 2 * KD + VD] = grad_v[...].astype(low)


def retain_back(grad, pre, kept, grouped, scale, consts, heads):
    total = pre.shape[0]
    powers, logs, cosine, sine, after, before = consts
    whole = lambda a: pl.BlockSpec(a.shape, lambda h: (0, 0))
    smem = pl.BlockSpec(memory_space=pltpu.SMEM)
    by_head = lambda width: pl.BlockSpec((total, width), lambda h: (0, h))
    return call(
        retain_back_kernel,
        (heads,),
        [smem, smem, by_head(VD), pl.BlockSpec((total, VD), lambda h: (0, 3 * h + 2))]
        + [by_head(2 * KD + VD), by_head(VD), by_head(128)]
        + [whole(cosine), whole(sine), whole(after), whole(before)],
        by_head(2 * KD + 2 * VD),
        jax.ShapeDtypeStruct((total, heads * (2 * KD + 2 * VD)), low),
        heads * total * total * (3 * KD + 2 * VD) * 5 // 4,
        scratch=[
            pltpu.VMEM((total, VD), low),
            pltpu.VMEM((total, KD), f32),
            pltpu.VMEM((total, KD), f32),
            pltpu.VMEM((total, VD), f32),
        ],
        moved=heads * total * (512 * 4 * 3 + 1024 * 2 + 1536 * 2),
        exps=heads * total * 600,
    )(*consts[:2], grad, pre, kept, grouped, scale, *consts[2:])


def feed_kernel(held, rows, cot, *refs):
    weights = refs[:6]
    hidden, grad_act, grad_lin, total = refs[6 + held :]
    half = rows.shape[1] // 2
    up, gate, down = ((weights[2 * i][...], weights[2 * i + 1][...]) for i in range(3))

    def into(values, weight):
        return dot(values[:, :half], weight[0]) + dot(values[:, half:], weight[1])

    act, lin, grad_hidden = into(rows, up), into(rows, gate), into(cot, down)
    curve = jnp.tanh(gelu_slope * (act + gelu_cubic * act * act * act))
    gelu = 0.5 * act * (1.0 + curve)
    slope = 0.5 * (1.0 + curve) + (0.5 * gelu_slope) * act * (1.0 - curve * curve) * (
        1.0 + (3.0 * gelu_cubic) * act * act
    )
    hidden[...] = (gelu * lin).astype(low)
    act_low = (grad_hidden * lin * slope).astype(low)
    lin_low = (grad_hidden * gelu).astype(low)
    grad_act[...] = act_low
    grad_lin[...] = lin_low

    for side in range(2):
        columns = slice(side * half, (side + 1) * half)
        add = dot_nt(act_low, up[side]) + dot_nt(lin_low, gate[side])

        @pl.when(pl.program_id(0) == 0)
        def _(add=add, columns=columns):
            total[:, columns] = add + refs[6][:, columns] if held else add

        @pl.when(pl.program_id(0) != 0)
        def _(add=add, columns=columns):
            total[:, columns] += add


def feed(rows, cot, weight, total):
    own, other = weight
    count, width = rows.shape
    columns = own.shape[1] // 3
    size = min(TILE, columns)
    steps = columns // size
    full = pl.BlockSpec((count, width), lambda t: (0, 0))
    tile = pl.BlockSpec((count, size), lambda t: (0, t))
    weights = [
        pl.BlockSpec((width // 2, size), lambda t, part=part: (0, part * steps + t))
        for part in range(3)
        for _ in range(2)
    ]
    shape = jax.ShapeDtypeStruct((count, columns), low)
    held = [] if total is None else [total]
    return call(
        functools.partial(feed_kernel, len(held)),
        (steps,),
        [full, full] + weights + [full] * len(held),
        [tile, tile, tile, full],
        [shape, shape, shape, jax.ShapeDtypeStruct((count, width), f32)],
        10 * count * width * columns,
        moved=6 * width * columns + 8 * count * width + 6 * count * columns,
        exps=count * columns,
    )(rows, cot, *([own, other] * 3), *held)


def gradient_kernel(plan, added, places, *refs):
    number = sum(pieces for pieces, _, _ in plan)
    lefts, rights = refs[:number], refs[number : number + sum(len(r) for _, r, _ in plan)]
    rest = refs[number + len(rights) :]
    came, outs, turned = rest[:added], rest[added:-1], rest[-1]
    step = pl.program_id(0)
    first = left_at = right_at = 0
    for pieces, lengths, size in plan:

        @pl.when(step == first)
        def _(left_at=left_at, pieces=pieces, size=size):
            for i in range(left_at, left_at + pieces):
                start = pl.multiple_of(places[i] * size, size) if pieces > 1 else 0
                turned[:, pl.ds(start, size)] = lefts[i][...].T

        for length in lengths:

            @pl.when((step >= first) & (step < first + length))
            def _(right=rights[right_at]):
                result = dot(turned[...], right[...])
                if added:
                    result = result + came[0][...].astype(f32)
                height = result.shape[0] // len(outs)
                for i, out in enumerate(outs):
                    out[...] = result[i * height : (i + 1) * height].astype(low)

            first, right_at = first + length, right_at + 1
        left_at += pieces


def weight_gradient(groups, side, came=None):
    width = groups[0][0][0].shape[1]
    half = width // 2
    count = groups[0][0][0].shape[0] * len(groups[0][0])
    columns = sum(right.shape[1] for _, _, rights in groups for right in rights)
    size = min(512, min(right.shape[1] for _, _, rights in groups for right in rights))
    plan, lefts, rights, left_specs, right_specs, places, first = [], [], [], [], [], [], 0
    for pieces, at, given in groups:
        plan.append((len(pieces), [right.shape[1] // size for right in given], pieces[0].shape[0]))
        lefts += pieces
        places += at
        left_specs += [pl.BlockSpec((pieces[0].shape[0], half), lambda t, _: (0, side))] * len(pieces)
        for right in given:
            steps = right.shape[1] // size
            right_specs.append(
                pl.BlockSpec(
                    (count, size),
                    lambda t, _, first=first, steps=steps: (0, jnp.clip(t - first, 0, steps - 1)),
                )
            )
            rights.append(right)
            first += steps
    parts = 1 if came is None else 4
    tile = lambda height: pl.BlockSpec((height, size), lambda t, _: (0, t))
    more = [] if came is None else [came]
    outs = call(
        functools.partial(gradient_kernel, plan, len(more)),
        (columns // size,),
        left_specs + right_specs + [tile(half)] * len(more),
        [tile(half // parts)] * parts,
        [jax.ShapeDtypeStruct((half // parts, columns), low)] * parts,
        2 * half * count * columns,
        scratch=[pltpu.VMEM((half, count), low)],
        scalars=1,
        moved=2 * (half * columns * (1 + len(more)) + count * (half + columns)),
    )(jnp.stack(places), *lefts, *rights, *more)
    return outs[0] if came is None else [outs[:2], outs[2:]]


def shards(
    inputs,
    gain_attn,
    w_query,
    w_key,
    w_value,
    w_gate,
    w_out,
    gain_mlp,
    w_act,
    w_lin,
    w_down,
    cotangent,
    lengths,
    offsets,
):
    rows, width = inputs.shape
    dp_size, tensor_size = lax.axis_size("dp"), lax.axis_size("tensor")
    dp_own, tensor_own = lax.axis_index("dp"), lax.axis_index("tensor")
    total = rows * tensor_size
    heads = w_query.shape[1] // KD
    hidden_cols = w_act.shape[1]
    half = width // 2

    order = feature_order(dp_size)
    taken = jnp.array([k for k, _ in order], jnp.int32)
    parts = jnp.array([i for _, i in order], jnp.int32)
    table = (taken ^ dp_own) * 2 + parts
    place = {pair: i for i, pair in enumerate(order)}
    places = jnp.array([[place[k, i] for i in range(2)] for k in range(dp_size)], jnp.int32)
    back = places[jnp.arange(dp_size, dtype=jnp.int32) ^ dp_own].reshape(-1)

    gains = jnp.concatenate([gain_attn.reshape(2, -1), gain_mlp.reshape(2, -1)], axis=1)
    gains = gather_rest(gather_start(gains), 0, "gains")
    gains = jnp.concatenate([gains, swap(gains, "dp", 1, "gains")], axis=0).astype(f32)
    fine = gains.shape[1] // 2
    gain_one, gain_two = gains[:, :fine].reshape(-1), gains[:, fine:].reshape(-1)
    cot_came = swap(cotangent, "tensor", 1, "rows_cot")
    x_low = reorder(inputs, table)
    cot = reorder(cotangent, table)
    h_attn = (layer_norm(x_low.astype(f32))[0] * gain_one).astype(low)

    def per_head(query, key, value, gate):
        columns = []
        for h in range(heads):
            columns += [a[:, h * KD : (h + 1) * KD] for a in (query, key)]
            columns += [a[:, h * VD : (h + 1) * VD] for a in (value, gate)]
        return jnp.concatenate(columns, axis=1)

    block_in = per_head(w_query, w_key, w_value, w_gate)
    block_out = w_out.T
    block_feed = jnp.concatenate([w_act, w_lin, w_down.T], axis=1)
    pair_blocks = range(0, tensor_size, 2)

    head_first = tensor_own * heads
    head_numbers = (head_first + jnp.arange(heads, dtype=jnp.int32)).astype(f32)
    log_decay = jnp.log(1.0 - jnp.exp2(-5.0 - head_numbers))
    segment, position = sequence_layout(lengths[0], offsets[0], total)
    cosine, sine = rotation(position, KD)
    powers = jnp.exp(
        jnp.arange(total // TILE, dtype=f32)[None, :] * TILE * log_decay[:, None]
    )
    consts = (powers, log_decay, cosine, sine, segment[:, None], segment[None, :])
    ring_places = [(tensor_own - step) % tensor_size for step in range(tensor_size)]

    w_in = gather_step(gather_start(tie(block_in, gains)), 0, "w_in")
    w_in_other = pre = wo = None
    held = [h_attn]

    def beside_attn(step, came):
        nonlocal w_in, w_in_other, cot_came, pre, wo, consts, block_feed, block_out
        if step == 1:
            came, w_in, cot_came, block_feed, block_out = sync(
                came, w_in, cot_came, block_feed, block_out
            )
            w_in = gather_rest(w_in, 1, "w_in")
        if step == 2:
            came, w_in, consts = sync(came, w_in, consts)
            w_in_other = swap(w_in, "dp", 1, "w_in")
            wo = gather_step(gather_start(tie(block_out, w_in)), 0, "w_out")
        if step == tensor_size - 1:
            pre = project(held, (w_in, w_in_other), None, ring_places[:step], tensor_size)
            came, pre, wo = sync(came, pre, wo)
        held.append(came)
        return came

    h_pieces = gather_ring(h_attn, "rows_attn", beside_attn)
    rows_here = h_pieces[-1]
    w_in = (w_in, w_in_other)
    cot_pair = jnp.concatenate([cot, reorder(cot_came, table)], axis=0)

    block_feed, wo = tie((block_feed, wo), rows_here)
    feed_parts = gather_start(block_feed)
    far_feeds = {k: [swap(feed_parts[0], "tensor", k, "w_feed_far")] for k in pair_blocks[1:]}
    near_feed = gather_step(feed_parts, 0, "w_feed_near")
    wo = gather_rest(wo, 1, "w_out")
    pre = project([rows_here], w_in, pre, ring_places[-1:], tensor_size)
    pre, wo = sync(pre, wo)
    wo = (wo, swap(wo, "dp", 1, "w_out"))
    mixed, kept, grouped, scale = retain(pre, consts, heads)
    mixed, near_feed, far_feeds, late_part, cot_pair = sync(
        mixed, near_feed, far_feeds, feed_parts[1], cot_pair
    )
    near_feed = gather_rest(near_feed, 1, "w_feed_near")
    far_feeds = {
        k: v + [swap(late_part, "tensor", k, "w_feed_far")] for k, v in far_feeds.items()
    }

    def beside_out(step, came, _):
        nonlocal near_feed, far_feeds
        if step == 1:
            came, far_feeds = sync(came, far_feeds)
            far_feeds = {k: gather_step(v, 0, "w_feed_far") for k, v in far_feeds.items()}
        if step == 2:
            came, near_feed, far_feeds = sync(came, near_feed, far_feeds)
            near_feed = (near_feed, swap(near_feed, "dp", 1, "w_feed_near"))
            far_feeds = {k: gather_rest(v, 1, "w_feed_far") for k, v in far_feeds.items()}
        return came

    attended = scatter_ring(mixed, wo, rows, "sum_attn", beside_out)

    middle, h_mlp = norm_rows(x_low, attended, gain_two)
    h_came = swap(h_mlp, "tensor", 1, "rows_mlp")
    h_came, far_feeds = sync(h_came, far_feeds)
    far_feeds = {k: (v, swap(v, "dp", 1, "w_feed_far")) for k, v in far_feeds.items()}
    feeds = [near_feed] + [far_feeds[k] for k in pair_blocks[1:]]
    h_pair = jnp.concatenate([h_mlp, h_came], axis=0)
    results, grad_h = [], None
    for weight in feeds:
        *result, grad_h = feed(h_pair, cot_pair, weight, grad_h)
        results.append(result)
    grad_send = grad_h[rows:].astype(low)
    grad_came = swap(grad_send, "tensor", 1, "sum_grad_mlp")

    results, late_rows, late_cot = tie((results, h_pair, cot_pair), grad_send)
    origin = jnp.zeros((), jnp.int32)

    def feed_groups(result):
        hidden, grad_act, grad_lin = result
        return [([late_rows], [origin], [grad_act, grad_lin]), ([late_cot], [origin], [hidden])]

    far = {k: weight_gradient(feed_groups(results[k // 2]), 1) for k in pair_blocks[1:]}
    near_other = weight_gradient(feed_groups(results[0]), 1)
    grad_came, far, near_other = sync(grad_came, far, near_other)
    far_came = {k: swap(other, "dp", 1, "grad_feed_far") for k, other in far.items()}
    near_came = swap(near_other, "dp", 1, "grad_feed_near")
    grad_middle, gain_two_term, grad_mid_low = norm_back_rows(
        middle, cot, gain_two, grad_h[:rows], grad_came
    )

    grad_mixed = out_own = out_send = None
    mid_pieces = [grad_mid_low]

    def beside_mid(step, came):
        nonlocal far, near_came, grad_mixed, out_own, out_send
        if step == 1:
            late = tie(results, grad_mid_low)
            far = {
                k: weight_gradient(feed_groups(late[k // 2]), 0, far_came[k])
                for k in pair_blocks[1:]
            }
            came, far = sync(came, far)
            far = {k: scatter_step(v, 0, "grad_feed_far") for k, v in far.items()}
        if step == 2:
            late, weights = tie((results, feeds), mid_pieces[1])
            sums = [
                jnp.concatenate(
                    [dot_nt(result[0], weight[side][:, 2 * hidden_cols :]) for side in range(2)],
                    axis=1,
                )
                for result, weight in zip(late, weights)
            ]
            out_own, out_send = sum(sums)[:rows], sum(sums)[rows:].astype(low)
            came, out_own, out_send = sync(came, out_own, out_send)
        if step == tensor_size - 1:
            late, late_result = tie((mid_pieces, results[0]), mid_pieces[-1])
            near_came = weight_gradient(feed_groups(late_result), 0, near_came)
            grad_mixed = project(late, wo, None, ring_places[:step], tensor_size)
            came, far, grad_mixed, near_came = sync(came, far, grad_mixed, near_came)
        mid_pieces.append(came)
        return came

    mid_pieces = gather_ring(grad_mid_low, "rows_grad_mid", beside_mid)
    out_came = swap(tie(out_send, mid_pieces[-1]), "tensor", 1, "sum_out")
    far = {k: scatter_rest(v, 1, "grad_feed_far") for k, v in far.items()}

    grad_mixed = project(mid_pieces[-1:], wo, grad_mixed, ring_places[-1:], tensor_size)
    grad_in = retain_back(grad_mixed, pre, kept, grouped, scale, consts, heads)

    grad_in, out_came, far, near = sync(grad_in, out_came, far, near_came)
    far_sent = {k: [part[: part.shape[0] // 2], part[part.shape[0] // 2 :]] for k, part in far.items()}
    far = {k: [swap(part[0], "tensor", k, "grad_feed_far")] for k, part in far_sent.items()}
    near = scatter_step(near, 0, "grad_feed_near")
    in_other = out_other = more = None
    grads_in = grads_out = gain_sum = None

    def gain_total(gain_one_term):
        gain_terms = jnp.concatenate(
            [gain_one_term.reshape(-1, fine), gain_two_term.reshape(-1, fine)], axis=1
        )
        size = gain_terms.shape[0] // 2
        gain_sum = gain_terms[:size] + swap(gain_terms[size:], "dp", 1, "gains")
        sums = [gain_sum[: size // 2], gain_sum[size // 2 :]]
        for bits in reversed(dp_bits(dp_size)):
            size = sums[0].shape[0] // 2
            sums = [
                part[:size] + swap(part[size:], "dp", bit, "gains") for part, bit in zip(sums, bits)
            ]
        gain_sum = jnp.concatenate(sums, axis=0)
        for b in range(tensor_size.bit_length() - 1):
            gain_sum = gain_sum + swap(gain_sum, "tensor", 1 << b, "gains")
        return gain_sum

    def beside_sum(step, came, terms_sum):
        nonlocal near, far, far_sent, in_other, out_other, more, grads_in, grads_out, gain_sum
        if step == 1:
            late, late_mixed = tie((grad_in, mixed), terms_sum)
            in_other = weight_gradient([(h_pieces, ring_places, [late])], 1)
            out_other = weight_gradient([(mid_pieces, ring_places, [late_mixed])], 1)
            came, more, in_other, out_other, far, far_sent, near = sync(
                came, terms_sum, in_other, out_other, far, far_sent, near
            )
            in_other = swap(in_other, "dp", 1, "grad_w_in")
            out_other = swap(out_other, "dp", 1, "grad_w_out")
            far = {
                k: v + [swap(far_sent[k][1], "tensor", k, "grad_feed_far")] for k, v in far.items()
            }
            near = scatter_rest(near, 1, "grad_feed_near")
        if step == 2:
            grads_in = weight_gradient([(h_pieces, ring_places, [grad_in])], 0, in_other)
            grads_out = weight_gradient([(mid_pieces, ring_places, [mixed])], 0, out_other)
            came, grads_in, grads_out, far, near = sync(came, grads_in, grads_out, far, near)
            grads_in = scatter_step(grads_in, 0, "grad_w_in")
            gain_sum = gain_total(more / gain_one)
        if step == tensor_size - 1:
            came, gain_sum = sync(came, gain_sum)
        return came

    grad_hattn = scatter_ring(grad_in, w_in, rows, "sum_grad_attn", beside_sum, h_pieces)
    grad_wo_own = scatter_rest(grads_out, 0, "grad_w_out").astype(f32)
    grad_in_own = scatter_rest(grads_in, 1, "grad_w_in").astype(f32)
    far = [jnp.concatenate(part, axis=0).astype(f32) for part in far.values()]
    grad_feed = near.astype(f32) + sum(far)
    outputs = middle + out_own + out_came.astype(f32)
    (grad_inputs,) = norm_back_rows(x_low, grad_middle, gain_one, grad_hattn)

    def heads_back(first, size):
        stride = 2 * KD + 2 * VD
        return jnp.concatenate(
            [grad_in_own[:, h * stride + first : h * stride + first + size] for h in range(heads)],
            axis=1,
        )

    return (
        reorder(outputs.astype(low), back),
        reorder(grad_inputs, back),
        gain_sum[:, :fine].reshape(-1),
        heads_back(0, KD),
        heads_back(KD, KD),
        heads_back(2 * KD, VD),
        heads_back(2 * KD + VD, VD),
        grad_wo_own.T,
        gain_sum[:, fine:].reshape(-1),
        grad_feed[:, :hidden_cols],
        grad_feed[:, hidden_cols : 2 * hidden_cols],
        grad_feed[:, 2 * hidden_cols :].T,
    )


def solution(mesh):
    return jax.shard_map(
        shards,
        mesh=mesh,
        in_specs=(
            P(("dp", "tensor"), None),
            P("dp"),
            P("dp", "tensor"),
            P("dp", "tensor"),
            P("dp", "tensor"),
            P("dp", "tensor"),
            P("tensor", "dp"),
            P("dp"),
            P("dp", "tensor"),
            P("dp", "tensor"),
            P("tensor", "dp"),
            P(("dp", "tensor"), None),
            P("dp", None),
            P("dp", None),
        ),
        out_specs=(
            P(("dp", "tensor"), None),
            P(("dp", "tensor"), None),
            P("dp"),
            P("dp", "tensor"),
            P("dp", "tensor"),
            P("dp", "tensor"),
            P("dp", "tensor"),
            P("tensor", "dp"),
            P("dp"),
            P("dp", "tensor"),
            P("dp", "tensor"),
            P("tensor", "dp"),
        ),
        check_vma=False,
    )
```

```python
import functools
import math

import jax
import jax.numpy as jnp
from jax import lax
from jax.experimental import pallas as pl
from jax.experimental.pallas import tpu as pltpu
from jax.sharding import PartitionSpec as P

KD = 256
VD = 512
TILE = 256

epsilon = 1e-05
group_floor = 1.0
f32 = jnp.float32
low = jnp.bfloat16
gelu_slope = math.sqrt(2.0 / math.pi)
gelu_cubic = 0.044715


def layer_norm(values, floor_value=epsilon):
    center = values - jnp.mean(values, axis=-1, keepdims=True)
    scale_inv = lax.rsqrt(jnp.mean(center * center, axis=-1, keepdims=True) + floor_value)
    return (center * scale_inv, scale_inv)


def norm_back(grad_norm, normed, scale_inv):
    mean_grad = jnp.mean(grad_norm, axis=-1, keepdims=True)
    mean_cross = jnp.mean(grad_norm * normed, axis=-1, keepdims=True)
    return (grad_norm - mean_grad - normed * mean_cross) * scale_inv


def sequence_layout(lengths, offsets, total):
    places = jnp.arange(total, dtype=jnp.int32)[:, None]
    inside = (places >= offsets[None, :]) & (places < offsets[None, :] + lengths[None, :])
    numbers = jnp.arange(1, offsets.shape[0] + 1, dtype=jnp.int32)
    segment = jnp.sum(jnp.where(inside, numbers[None, :], 0), axis=1) - 1
    position = places[:, 0] - jnp.sum(jnp.where(inside, offsets[None, :], 0), axis=1)
    return (segment, position.astype(f32))


def rotation(position, size):
    half = size // 2
    frequency = jnp.exp(-math.log(10000.0) * jnp.arange(half, dtype=f32) * 2.0 / size)
    angles = position[:, None] * frequency[None, :]
    return (jnp.cos(angles), jnp.sin(angles))


def dot(left, right):
    return jnp.dot(left, right, preferred_element_type=f32)


def dot_nt(left, right):
    return lax.dot_general(left, right, (((1,), (1,)), ((), ())), preferred_element_type=f32)


def dot_tn(left, right):
    return lax.dot_general(left, right, (((0,), (0,)), ((), ())), preferred_element_type=f32)


def swap(values, axis, bits, name="swap"):
    size = lax.axis_size(axis)
    with jax.named_scope(f"{name}_{axis}{bits}"):
        return lax.ppermute(values, axis, [(i, i ^ bits) for i in range(size)])


def shift(values, axis, step, name="shift"):
    size = lax.axis_size(axis)
    with jax.named_scope(name):
        return lax.ppermute(values, axis, [(i, (i + step) % size) for i in range(size)])


def tie(values, token):
    return values if token is None else lax.optimization_barrier((values, token))[0]


def dp_bits(size):
    bits = [1 << b for b in range(1, size.bit_length() - 1)]
    return list(zip(bits, bits[1:] + bits[:1]))


def feature_order(size):
    same = []
    for half in (0, 1):
        held = [0]
        for bits in dp_bits(size):
            held += [k ^ bits[half] for k in held]
        same += [(k, half) for k in held]
    return same + [(k ^ 1, half) for k, half in same]


def gather_step(parts, stage, name, after=None):
    bits = dp_bits(lax.axis_size("dp"))[stage]
    parts = sync(*parts)
    came = tie([swap(part, "dp", bit, name) for part, bit in zip(parts, bits)], after)
    return [join(*pair) for pair in zip(parts, came)]


def gather_rest(parts, stage, name, after=None):
    for step in range(stage, len(dp_bits(lax.axis_size("dp")))):
        parts = gather_step(parts, step, name, after)
    return parts


def gather_core(parts, name):
    return [*parts, *(swap(part, "dp", 1, name) for part in sync(*parts))]


def scatter_step(parts, stage, name, after=None):
    bits = dp_bits(lax.axis_size("dp"))[-1 - stage]
    parts = sync(*parts)
    came = tie([swap(sent, "dp", bit, name) for (_, sent), bit in zip(parts, bits)], after)
    return [add_split(kept, part) for (kept, _), part in zip(parts, came)]


def scatter_rest(parts, stage, name):
    for step in range(stage, len(dp_bits(lax.axis_size("dp")))):
        parts = scatter_step(parts, step, name)
    return [half for part in parts for half in part]


def sync(*values):
    return lax.optimization_barrier(values)


def gather_ring(rows, name, beside):
    pieces = [rows]
    for step in range(1, lax.axis_size("tensor")):
        came = shift(pieces[-1], "tensor", 1, f"{name}_{step}")
        pieces.append(beside(step, came))
    return pieces


def call(kernel, grid, in_specs, out_specs, out_shape, vmem=40, scratch=(), scalars=0, aliases=None):
    return pl.pallas_call(
        kernel,
        grid_spec=pltpu.PrefetchScalarGridSpec(
            num_scalar_prefetch=scalars,
            grid=grid,
            in_specs=in_specs,
            out_specs=out_specs,
            scratch_shapes=scratch,
        ),
        out_shape=out_shape,
        input_output_aliases=aliases or {},
        compiler_params=pltpu.CompilerParams(
            dimension_semantics=("arbitrary",) * len(grid), vmem_limit_bytes=vmem * 1024 * 1024
        ),
        cost_estimate=pl.CostEstimate(flops=0, bytes_accessed=0, transcendentals=0),
    )


def join_kernel(steps, *refs):
    step, first = pl.program_id(0), 0
    for ref, length in zip(refs[:-1], steps):

        @pl.when((step >= first) & (step < first + length))
        def _(ref=ref):
            refs[-1][...] = ref[...]

        first += length


def join(*parts):
    columns = parts[0].shape[1]
    height = min(min(part.shape[0] for part in parts), 256)
    steps, specs, first = [], [], 0
    for part in parts:
        length = part.shape[0] // height
        specs.append(
            pl.BlockSpec(
                (height, columns),
                lambda t, first=first, length=length: (jnp.clip(t - first, 0, length - 1), 0),
            )
        )
        steps.append(length)
        first += length
    return call(
        functools.partial(join_kernel, steps),
        (first,),
        specs,
        pl.BlockSpec((height, columns), lambda t: (t, 0)),
        jax.ShapeDtypeStruct((first * height, columns), parts[0].dtype),
        40,
    )(*parts)


def column_blocks_kernel(places, *refs):
    for ref, (column, first, size) in zip(refs[:-2], places):
        half = ref.shape[0] // 2
        refs[-2][:, first : first + size] = ref[:half, column : column + size]
        refs[-1][:, first : first + size] = ref[half:, column : column + size]


def column_blocks(sources):
    height = sources[0][0].shape[0]
    places, specs, first = [], [], 0
    for array, column, size in sources:
        places.append((column, first, size))
        specs.append(pl.BlockSpec(array.shape, lambda t: (0, 0)))
        first += size
    half = pl.BlockSpec((height // 2, first), lambda t: (0, 0))
    shape = jax.ShapeDtypeStruct((height // 2, first), sources[0][0].dtype)
    return call(
        functools.partial(column_blocks_kernel, places), (1,), specs, [half, half], [shape, shape]
    )(*[array for array, _, _ in sources])


def add_split_kernel(left, right, upper, lower):
    half = upper.shape[0]
    for i, out in enumerate((upper, lower)):
        rows = slice(i * half, (i + 1) * half)
        out[...] = (left[rows, :].astype(f32) + right[rows, :].astype(f32)).astype(low)


def add_split(left, right):
    count, columns = left.shape
    size = columns // 2 if columns % 256 == 0 else columns
    whole = pl.BlockSpec((count, size), lambda t: (0, t))
    half = pl.BlockSpec((count // 2, size), lambda t: (0, t))
    return call(
        add_split_kernel,
        (columns // size,),
        [whole, whole],
        [half, half],
        [jax.ShapeDtypeStruct((count // 2, columns), low)] * 2,
        40,
    )(left, right)


def add_kernel(left, right, out):
    out[...] = (left[...].astype(f32) + right[...].astype(f32)).astype(out.dtype)


def add_rows(left, right, kind):
    count, width = left.shape
    rows = pl.BlockSpec((count // 2, width), lambda i: (i, 0))
    shape = jax.ShapeDtypeStruct((count, width), kind)
    return call(add_kernel, (2,), [rows, rows], rows, shape)(left, right)


def scale_kernel(rows, gain, out):
    out[...] = (rows[...].astype(f32) * gain[...]).astype(low)


def scale_rows(values, gain):
    count, width = values.shape
    rows = pl.BlockSpec((count // 2, width), lambda i: (i, 0))
    line = pl.BlockSpec((1, width), lambda i: (0, 0))
    shape = jax.ShapeDtypeStruct((count, width), low)
    return call(scale_kernel, (2,), [rows, line], rows, shape)(values, gain[None])


def normed_kernel(values, out):
    out[...] = layer_norm(values[...].astype(f32))[0].astype(low)


def normed_rows(values):
    count, width = values.shape
    rows = pl.BlockSpec((count // 2, width), lambda i: (i, 0))
    shape = jax.ShapeDtypeStruct((count, width), low)
    return call(normed_kernel, (2,), [rows], rows, shape)(values)


def reorder_kernel(table, values, out):
    count = table.shape[0]
    width = values.shape[1] // count
    for place in range(count):
        start = pl.multiple_of(table[place] * width, width)
        out[:, place * width : (place + 1) * width] = values[:, pl.ds(start, width)]


def reorder(values, table):
    count, (rows, width) = table.shape[0], values.shape
    size = width // count
    if size % 128:
        blocks = [
            lax.dynamic_slice_in_dim(values, table[i] * size, size, axis=1) for i in range(count)
        ]
        return jnp.concatenate(blocks, axis=1)
    part = min(rows, 64)
    spec = pl.BlockSpec((part, width), lambda i, _: (i, 0))
    return call(
        reorder_kernel,
        (rows // part,),
        [spec],
        spec,
        jax.ShapeDtypeStruct(values.shape, values.dtype),
        40,
        scalars=1,
    )(table, values)


def project_kernel(count, places, *refs):
    weights, out = refs[count : count + 4], refs[-1]
    depth = weights[0].shape[0]
    for i in range(count):
        rows = refs[i]
        size = rows.shape[0]
        start = pl.multiple_of(places[i] * size, size) if out.shape[0] > size else 0
        out[pl.ds(start, size), :] = sum(
            dot(rows[:, q * depth : (q + 1) * depth], weights[q][...]) for q in range(4)
        )


def project(pieces, weight, whole, places, chunks):
    (count, width), columns = pieces[0].shape, weight[0].shape[1]
    size = 512 if columns % 512 == 0 else TILE
    spec = pl.BlockSpec((width // 4, size), lambda j, _: (0, j))
    rows = pl.BlockSpec((count, width), lambda j, _: (0, 0))
    number = len(pieces)
    if whole is None:
        held, out = [], pl.BlockSpec((count * chunks, size), lambda j, _: (0, j))
    else:
        held, out = [whole], pl.BlockSpec((count, size), lambda j, at: (at[0], j))
    return call(
        functools.partial(project_kernel, number),
        (columns // size,),
        [rows] * number + [spec] * 4 + [pl.BlockSpec(memory_space=pl.ANY)] * len(held),
        out,
        jax.ShapeDtypeStruct((count * chunks, columns), f32),
        56,
        scalars=1,
        aliases={number + 5: 0} if held else None,
    )(jnp.stack(places), *pieces, *weight, *held)


def part_specs(shape, steps, column):
    def spec(part):
        def index(i, j, *_):
            return (jnp.where(i == part, j, jnp.where(i < part, 0, steps - 1)), column)

        return pl.BlockSpec(shape, index)

    return [spec(part) for part in range(4)]


def terms_kernel(count, paired, places, *refs):
    weights, outs = refs[count : count + 4], refs[count + 4 :]
    pairs, outs = outs[: count * paired], outs[count * paired :]

    def give(weight):
        sums = 0.0
        for i, rows in enumerate(refs[:count]):
            result = dot_nt(rows[...], weight[...])
            outs[i][...] = result.astype(outs[i].dtype)
            if paired:
                sums = sums + jnp.sum(result * pairs[i][...].astype(f32), axis=0, keepdims=True)
        if paired:
            outs[count][...] = sums

    for part, weight in enumerate(weights):
        pl.when(pl.program_id(0) == part)(functools.partial(give, weight))


def terms(whole, weight, places, size, kinds, pairs):
    quarter, depth = weight[0].shape
    tile = min(quarter, 512 if depth <= 1024 else 256)
    steps = quarter // tile
    number = len(places)
    rows = [
        pl.BlockSpec((size, depth), lambda i, j, at, n=n: (at[n], 0)) for n in range(number)
    ]
    out = lambda height: pl.BlockSpec((height, tile), lambda i, j, _: (0, i * steps + j))
    paired = 1 if pairs else 0
    return call(
        functools.partial(terms_kernel, number, paired),
        (4, steps),
        rows + part_specs((tile, depth), steps, 0) + [out(size)] * (number * paired),
        [out(size)] * number + [out(1)] * paired,
        [jax.ShapeDtypeStruct((size, 4 * quarter), kind) for kind in kinds]
        + [jax.ShapeDtypeStruct((1, 4 * quarter), f32)] * paired,
        56,
        scalars=1,
    )(jnp.stack(places), *([whole] * number), *weight, *(pairs or []))


def scatter_places():
    own, size = lax.axis_index("tensor"), lax.axis_size("tensor")
    return [(own - step) % size for step in range(1, size + 1)]


def scatter_ring(total, rest, name, beside):
    for step, own in enumerate(rest, 1):
        came = shift(total, "tensor", 1, f"{name}_{step}")
        if step == len(rest):
            return beside(step, came), own
        total = beside(step, add_rows(came, own, low))


def norm_kernel(values, came, added, gain, middle, out):
    rows = values[...].astype(f32) + (came[...].astype(f32) + added[...])
    middle[...] = rows
    out[...] = (layer_norm(rows)[0] * gain[...]).astype(low)


def norm_rows(values, came, added, gain):
    count, width = values.shape
    size = min(count, 128)
    rows = pl.BlockSpec((size, width), lambda i: (i, 0))
    return call(
        norm_kernel,
        (count // size,),
        [rows, rows, rows, pl.BlockSpec((1, width), lambda i: (0, 0))],
        [rows, rows],
        [jax.ShapeDtypeStruct((count, width), f32), jax.ShapeDtypeStruct((count, width), low)],
        40,
    )(values, came, added, gain[None])


def norm_back_kernel(values, base, gain, grad, came, out, *more):
    given = grad[...] + came[...].astype(f32)
    normed, scale = layer_norm(values[...].astype(f32))
    result = base[...].astype(f32) + norm_back(given * gain[...], normed, scale)
    out[...] = result
    if not more:
        return
    more[1][...] = result.astype(low)
    term = jnp.sum(given * normed, axis=0, keepdims=True)

    @pl.when(pl.program_id(0) == 0)
    def _():
        more[0][...] = term

    @pl.when(pl.program_id(0) != 0)
    def _():
        more[0][...] += term


def norm_back_rows(values, base, gain, grad, came, more):
    count, width = values.shape
    size = min(count, 128)
    rows = pl.BlockSpec((size, width), lambda i: (i, 0))
    line = pl.BlockSpec((1, width), lambda i: (0, 0))
    shape = lambda height, kind: jax.ShapeDtypeStruct((height, width), kind)
    return call(
        norm_back_kernel,
        (count // size,),
        [rows, rows, line, rows, rows],
        [rows] + [line, rows] * more,
        [shape(count, f32)] + [shape(1, f32), shape(count, low)] * more,
        40,
    )(values, base, gain[None], grad, came)


def place_masks(size):
    row = lax.broadcasted_iota(jnp.int32, (size, size), 0)
    column = lax.broadcasted_iota(jnp.int32, (size, size), 1)
    return row, column


def block_decay(powers, head, apart, base, row, column, after, before):
    kept = (after == before) & (after >= 0)
    if apart == 0:
        kept = kept & (column <= row)
        return jnp.where(kept, base, 0.0)
    return jnp.where(kept, base * powers[head, apart], 0.0)


def retain_kernel(powers, logs, pre, cosine, sine, after, before, mixed, kept, grouped, scale):
    head = pl.program_id(0)
    total = pre.shape[0]
    half = KD // 2
    cos, sin = cosine[...], sine[...]
    for first, factor in ((0, KD ** (-0.5)), (KD, 1.0)):
        a, b = pre[:, first : first + half], pre[:, first + half : first + KD]
        kept[:, first : first + half] = ((a * cos - b * sin) * factor).astype(low)
        kept[:, first + half : first + KD] = ((a * sin + b * cos) * factor).astype(low)
    kept[:, 2 * KD :] = pre[:, 2 * KD : 2 * KD + VD].astype(low)
    row, column = place_masks(TILE)
    base = jnp.exp((row - column).astype(f32) * logs[head])
    for i in range(total // TILE):
        rows = slice(i * TILE, (i + 1) * TILE)
        held = jnp.zeros((TILE, VD), f32)
        for j in range(i + 1):
            past = slice(j * TILE, (j + 1) * TILE)
            decay = block_decay(powers, head, i - j, base, row, column, after[rows, :], before[:, past])
            scores = dot_nt(kept[rows, :KD], kept[past, KD : 2 * KD])
            held = held + dot((decay * scores).astype(low), kept[past, 2 * KD :])
        normed, inverse = layer_norm(held, group_floor)
        grouped[rows, :] = normed
        scale[rows, :] = jnp.broadcast_to(inverse, (TILE, 128))
        gate = pre[rows, 2 * KD + VD :]
        mixed[rows, :] = (gate * jax.nn.sigmoid(gate) * normed).astype(low)


def retain(pre, consts, heads):
    total = pre.shape[0]
    powers, logs, cosine, sine, after, before = consts
    whole = lambda a: pl.BlockSpec(a.shape, lambda h: (0, 0))
    smem = pl.BlockSpec(memory_space=pltpu.SMEM)
    by_head = lambda width: pl.BlockSpec((total, width), lambda h: (0, h))
    shape = lambda width, kind: jax.ShapeDtypeStruct((total, heads * width), kind)
    return call(
        retain_kernel,
        (heads,),
        [smem, smem, by_head(2 * KD + 2 * VD), whole(cosine), whole(sine), whole(after), whole(before)],
        [by_head(VD), by_head(2 * KD + VD), by_head(VD), by_head(128)],
        [shape(VD, low), shape(2 * KD + VD, low), shape(VD, f32), shape(128, f32)],
        56,
    )(*consts[:2], pre, *consts[2:])


def retain_back_kernel(
    powers, logs, grad, gates, kept, grouped, scale, cosine, sine, after, before, out, grad_low, grad_q, grad_k, grad_v
):
    head = pl.program_id(0)
    total = kept.shape[0]
    half = KD // 2
    blocks = total // TILE
    for i in range(blocks):
        rows = slice(i * TILE, (i + 1) * TILE)
        gate, normed, given = gates[rows, :], grouped[rows, :], grad[rows, :]
        sigmoid = jax.nn.sigmoid(gate)
        out[rows, 2 * KD + VD :] = (
            given * normed * sigmoid * (1.0 + gate * (1.0 - sigmoid))
        ).astype(low)
        grad_low[rows, :] = norm_back(given * (gate * sigmoid), normed, scale[rows, :1]).astype(low)
    row, column = place_masks(TILE)
    base = jnp.exp((row - column).astype(f32) * logs[head])
    for i in range(blocks):
        rows = slice(i * TILE, (i + 1) * TILE)
        query, grad_rows = kept[rows, :KD], grad_low[rows, :]
        held = jnp.zeros((TILE, KD), f32)
        for j in range(i + 1):
            past = slice(j * TILE, (j + 1) * TILE)
            decay = block_decay(powers, head, i - j, base, row, column, after[rows, :], before[:, past])
            key, value = kept[past, KD : 2 * KD], kept[past, 2 * KD :]
            weights = (decay * dot_nt(query, key)).astype(low)
            grad_scores = (dot_nt(grad_rows, value) * decay).astype(low)
            held = held + dot(grad_scores, key)
            key_term, value_term = dot_tn(grad_scores, query), dot_tn(weights, grad_rows)
            if i == j:
                grad_k[past, :], grad_v[past, :] = key_term, value_term
            else:
                grad_k[past, :] += key_term
                grad_v[past, :] += value_term
        grad_q[rows, :] = held
    cos, sin = cosine[...], sine[...]
    for first, source, factor in ((0, grad_q, KD ** (-0.5)), (KD, grad_k, 1.0)):
        a, b = source[:, :half] * factor, source[:, half:] * factor
        out[:, first : first + half] = (a * cos + b * sin).astype(low)
        out[:, first + half : first + KD] = (b * cos - a * sin).astype(low)
    out[:, 2 * KD : 2 * KD + VD] = grad_v[...].astype(low)


def retain_back(grad, pre, kept, grouped, scale, consts, heads):
    total = pre.shape[0]
    powers, logs, cosine, sine, after, before = consts
    whole = lambda a: pl.BlockSpec(a.shape, lambda h: (0, 0))
    smem = pl.BlockSpec(memory_space=pltpu.SMEM)
    by_head = lambda width: pl.BlockSpec((total, width), lambda h: (0, h))
    return call(
        retain_back_kernel,
        (heads,),
        [smem, smem, by_head(VD), pl.BlockSpec((total, VD), lambda h: (0, 3 * h + 2))]
        + [by_head(2 * KD + VD), by_head(VD), by_head(128)]
        + [whole(cosine), whole(sine), whole(after), whole(before)],
        by_head(2 * KD + 2 * VD),
        jax.ShapeDtypeStruct((total, heads * (2 * KD + 2 * VD)), low),
        56,
        scratch=[
            pltpu.VMEM((total, VD), low),
            pltpu.VMEM((total, KD), f32),
            pltpu.VMEM((total, KD), f32),
            pltpu.VMEM((total, VD), f32),
        ],
    )(*consts[:2], grad, pre, kept, grouped, scale, *consts[2:])


def feed_kernel(feeds, steps, *refs):
    given, weights = refs[:4], refs[4 : 4 + 4 * feeds]
    outs = refs[4 + 4 * feeds : 4 + 7 * feeds]
    own, sent = refs[4 + 7 * feeds : 6 + 7 * feeds]
    rows, cots, held, grads, total, row_sems, sems = refs[6 + 7 * feeds :]
    count, width = rows.shape
    depth, size = width // 4, held.shape[2] // 3
    step = pl.program_id(0)

    def row_copies():
        places = [(buffer, first) for buffer in (rows, cots) for first in (0, count // 2)]
        return [
            pltpu.make_async_copy(ref, buffer.at[pl.ds(first, count // 2)], row_sems.at[i])
            for i, (ref, (buffer, first)) in enumerate(zip(given, places))
        ]

    def weight_copies(number, tile, slot):
        columns = weights[0].shape[1] // 3
        return [
            pltpu.make_async_copy(
                weights[4 * number + part].at[:, pl.ds(pl.multiple_of(kind * columns + tile * size, size), size)],
                held.at[slot, pl.ds(part * depth, depth), pl.ds(kind * size, size)],
                sems.at[slot, 4 * kind + part],
            )
            for kind in range(3)
            for part in range(4)
        ]

    def for_step(at, act):
        for number in range(feeds):

            @pl.when((at >= number * steps) & (at < (number + 1) * steps))
            def _(number=number):
                for copy in weight_copies(number, at - number * steps, lax.rem(at, 2)):
                    act(copy)

    @pl.when(step == 0)
    def _():
        for copy in row_copies():
            copy.start()
        for_step(step, lambda copy: copy.start())

    for_step(step + 1, lambda copy: copy.start())

    @pl.when(step == 0)
    def _():
        for copy in row_copies():
            copy.wait()

    for_step(step, lambda copy: copy.wait())
    weight = held.at[lax.rem(step, 2)]
    up = weight[:, : 2 * size]
    both, grad_hidden = dot(rows[...], up), dot(cots[...], weight[:, 2 * size :])
    act, lin = both[:, :size], both[:, size:]
    curve = jnp.tanh(gelu_slope * (act + gelu_cubic * act * act * act))
    gelu = 0.5 * act * (1.0 + curve)
    slope = 0.5 * (1.0 + curve) + (0.5 * gelu_slope) * act * (1.0 - curve * curve) * (
        1.0 + (3.0 * gelu_cubic) * act * act
    )
    hidden = (gelu * lin).astype(low)
    grads[:, :size] = (grad_hidden * lin * slope).astype(low)
    grads[:, size:] = (grad_hidden * gelu).astype(low)
    for number in range(feeds):

        @pl.when((step >= number * steps) & (step < (number + 1) * steps))
        def _(number=number):
            outs[3 * number][...] = hidden
            outs[3 * number + 1][...] = grads[:, :size]
            outs[3 * number + 2][...] = grads[:, size:]

    add = dot_nt(grads[...], up)

    @pl.when(step == 0)
    def _():
        total[...] = add

    @pl.when(step != 0)
    def _():
        total[...] += add

    @pl.when(step == pl.num_programs(0) - 1)
    def _():
        own[...] = total[: count // 2, :]
        sent[...] = total[count // 2 :, :].astype(low)


def feed(rows, cots, feeds):
    count, width = rows[0].shape
    columns = feeds[0][0].shape[1] // 3
    size = min(512, columns)
    steps, number = columns // size, len(feeds)
    full = pl.BlockSpec((count, width), lambda t: (0, 0))
    anywhere = pl.BlockSpec(memory_space=pl.ANY)
    tiles = [
        pl.BlockSpec((2 * count, size), lambda t, k=k: (0, jnp.clip(t - k * steps, 0, steps - 1)))
        for k in range(number)
    ]
    shape = jax.ShapeDtypeStruct((2 * count, columns), low)
    outs = call(
        functools.partial(feed_kernel, number, steps),
        (number * steps,),
        [anywhere] * (4 + 4 * number),
        [tile for tile in tiles for _ in range(3)] + [full, full],
        [shape] * (3 * number)
        + [jax.ShapeDtypeStruct((count, width), f32), jax.ShapeDtypeStruct((count, width), low)],
        56,
        scratch=[
            pltpu.VMEM((2 * count, width), low),
            pltpu.VMEM((2 * count, width), low),
            pltpu.VMEM((2, width, 3 * size), low),
            pltpu.VMEM((2 * count, 2 * size), low),
            pltpu.VMEM((2 * count, width), f32),
            pltpu.SemaphoreType.DMA((4,)),
            pltpu.SemaphoreType.DMA((2, 12)),
        ],
    )(*rows, *cots, *[part for weight in feeds for part in weight])
    return [outs[3 * k : 3 * k + 3] for k in range(number)], outs[-2], outs[-1]


def out_kernel(number, *refs):
    hiddens, weights, base = refs[:number], refs[number : 5 * number], refs[5 * number]
    own, sent = refs[5 * number + 1 :]
    half = own.shape[0]

    def give(part):
        total = sum(dot_nt(hiddens[i][...], weights[4 * i + part][...]) for i in range(number))
        own[...] = base[...] + total[:half]
        sent[...] = total[half:].astype(low)

    for part in range(4):
        pl.when(pl.program_id(0) == part)(functools.partial(give, part))


def out_rows(hiddens, feeds, base):
    count, width = base.shape
    columns = hiddens[0].shape[1]
    size = min(256, width // 4)
    steps = width // 4 // size
    tile = pl.BlockSpec((count, size), lambda i, j: (0, i * steps + j))
    return call(
        functools.partial(out_kernel, len(hiddens)),
        (4, steps),
        [pl.BlockSpec((2 * count, columns), lambda i, j: (0, 0))] * len(hiddens)
        + part_specs((size, columns), steps, 2) * len(hiddens)
        + [tile],
        [tile, tile],
        [jax.ShapeDtypeStruct((count, width), f32), jax.ShapeDtypeStruct((count, width), low)],
        56,
    )(*hiddens, *[weight for parts in feeds for weight in parts], base)


def gradient_kernel(plan, added, places, *refs):
    number = sum(pieces for pieces, _, _ in plan)
    lefts, rights = refs[:number], refs[number : number + sum(len(r) for _, r, _ in plan)]
    rest = refs[number + len(rights) :]
    came, outs, turned = rest[:added], rest[added:-1], rest[-1]
    step = pl.program_id(0)
    first = left_at = right_at = 0
    for pieces, lengths, size in plan:

        @pl.when(step == first)
        def _(left_at=left_at, pieces=pieces, size=size):
            for i in range(left_at, left_at + pieces):
                start = pl.multiple_of(places[i] * size, size) if pieces > 1 else 0
                turned[:, pl.ds(start, size)] = lefts[i][...].T

        for length in lengths:

            @pl.when((step >= first) & (step < first + length))
            def _(right=rights[right_at], depth=pieces * size):
                result = dot(turned[:, :depth], right[...])
                if added:
                    result = result + came[0][...].astype(f32)
                height = result.shape[0] // len(outs)
                for i, out in enumerate(outs):
                    out[...] = result[i * height : (i + 1) * height].astype(low)

            first, right_at = first + length, right_at + 1
        left_at += pieces


def weight_gradient(groups, side, came=None, pieces_out=4):
    width = groups[0][0][0].shape[1]
    half = width // 2
    count = max(pieces[0].shape[0] * len(pieces) for pieces, _, _ in groups)
    columns = sum(right.shape[1] for _, _, rights in groups for right in rights)
    size = min(512, min(right.shape[1] for _, _, rights in groups for right in rights))
    plan, lefts, rights, left_specs, right_specs, places, first = [], [], [], [], [], [], 0
    for pieces, at, given in groups:
        plan.append((len(pieces), [right.shape[1] // size for right in given], pieces[0].shape[0]))
        lefts += pieces
        places += at
        left_specs += [pl.BlockSpec((pieces[0].shape[0], half), lambda t, _: (0, side))] * len(pieces)
        for right in given:
            steps = right.shape[1] // size
            right_specs.append(
                pl.BlockSpec(
                    (right.shape[0], size),
                    lambda t, _, first=first, steps=steps: (0, jnp.clip(t - first, 0, steps - 1)),
                )
            )
            rights.append(right)
            first += steps
    parts = 1 if came is None else pieces_out
    tile = lambda height: pl.BlockSpec((height, size), lambda t, _: (0, t))
    more = [] if came is None else [came]
    outs = call(
        functools.partial(gradient_kernel, plan, len(more)),
        (columns // size,),
        left_specs + right_specs + [tile(half)] * len(more),
        [tile(half // parts)] * parts,
        [jax.ShapeDtypeStruct((half // parts, columns), low)] * parts,
        56,
        scratch=[pltpu.VMEM((half, count), low)],
        scalars=1,
    )(jnp.stack(places), *lefts, *rights, *more)
    return outs[0] if came is None else [outs[: parts // 2], outs[parts // 2 :]]


def shards(
    inputs,
    gain_attn,
    w_query,
    w_key,
    w_value,
    w_gate,
    w_out,
    gain_mlp,
    w_act,
    w_lin,
    w_down,
    cotangent,
    lengths,
    offsets,
):
    rows, width = inputs.shape
    dp_size, tensor_size = lax.axis_size("dp"), lax.axis_size("tensor")
    dp_own, tensor_own = lax.axis_index("dp"), lax.axis_index("tensor")
    total = rows * tensor_size
    heads = w_query.shape[1] // KD
    hidden_cols = w_act.shape[1]
    half = width // 2

    order = feature_order(dp_size)
    taken = jnp.array([k for k, _ in order], jnp.int32)
    parts = jnp.array([i for _, i in order], jnp.int32)
    table = (taken ^ dp_own) * 2 + parts
    place = {pair: i for i, pair in enumerate(order)}
    places = jnp.array([[place[k, i] for i in range(2)] for k in range(dp_size)], jnp.int32)
    back = places[jnp.arange(dp_size, dtype=jnp.int32) ^ dp_own].reshape(-1)

    x_low = reorder(inputs, table)
    normed_one = normed_rows(x_low)
    cot = reorder(cotangent, table)

    stride = 2 * KD + 2 * VD
    head_blocks = []
    for h in range(heads):
        head_blocks += [(w_query, h * KD, KD), (w_key, h * KD, KD)]
        head_blocks += [(w_value, h * VD, VD), (w_gate, h * VD, VD)]
    pair_blocks = range(0, tensor_size, 2)

    head_first = tensor_own * heads
    head_numbers = (head_first + jnp.arange(heads, dtype=jnp.int32)).astype(f32)
    log_decay = jnp.log(1.0 - jnp.exp2(-5.0 - head_numbers))
    segment, position = sequence_layout(lengths[0], offsets[0], total)
    cosine, sine = rotation(position, KD)
    powers = jnp.exp(
        jnp.arange(total // TILE, dtype=f32)[None, :] * TILE * log_decay[:, None]
    )
    consts = (powers, log_decay, cosine, sine, segment[:, None], segment[None, :])
    ring_places = [(tensor_own - step) % tensor_size for step in range(tensor_size)]

    gains = jnp.concatenate([gain_attn.reshape(2, -1), gain_mlp.reshape(2, -1)], axis=1)
    parts = [gains[:1], gains[1:]]
    for bits in dp_bits(dp_size):
        parts = [
            jnp.concatenate([part, swap(part, "dp", bit, "gains")], axis=0)
            for part, bit in zip(sync(*parts), bits)
        ]
    gains_same = jnp.concatenate(parts, axis=0)
    gains = jnp.concatenate([gains_same, swap(gains_same, "dp", 1, "gains")], axis=0).astype(f32)
    fine = gains.shape[1] // 2
    gain_one, gain_two = gains[:, :fine].reshape(-1), gains[:, fine:].reshape(-1)

    w_in = gather_step(tie(column_blocks(head_blocks), gains_same), 0, "w_in")
    feed_parts = column_blocks(
        [(w_act, 0, hidden_cols), (w_lin, 0, hidden_cols), (w_down.T, 0, hidden_cols)]
    )
    wo = column_blocks([(w_out.T, 0, w_out.shape[0])])

    def beside_attn(step, came):
        nonlocal w_in, wo, cot, feed_parts, consts
        if step == 1:
            came, w_in, wo, cot, feed_parts, consts = sync(came, w_in, wo, cot, feed_parts, consts)
            w_in = gather_rest(w_in, 1, "w_in", consts)
        return came

    pieces = gather_ring(normed_one, "rows_attn", beside_attn)
    rows_here, w_in, wo = sync(pieces[-1], w_in, wo)
    pieces[-1] = rows_here

    def swap_far(part):
        return {k: swap(part, "tensor", k, "w_feed_far") for k in pair_blocks[1:]}

    cot_came = swap(tie(cotangent, rows_here), "tensor", 1, "rows_cot")
    w_in = gather_core(w_in, "w_in")
    wo = gather_step(wo, 0, "w_out")
    h_pieces = [scale_rows(piece, gain_one) for piece in pieces]
    cot_came, wo, w_in, h_pieces, feed_parts = sync(cot_came, wo, w_in, h_pieces, feed_parts)

    upper = swap_far(feed_parts[0])
    wo = gather_rest(wo, 1, "w_out", upper)
    near_feed = gather_step(feed_parts, 0, "w_feed_near", upper)
    cots = [cot, reorder(cot_came, table)]
    pre = project(h_pieces[:-1], w_in, None, ring_places[:-1], tensor_size)
    pre = project(h_pieces[-1:], w_in, pre, ring_places[-1:], tensor_size)
    pre, upper, wo, near_feed, cots = sync(pre, upper, wo, near_feed, cots)

    lower = swap_far(tie(feed_parts[1], upper))
    wo = gather_core(wo, "w_out")
    near_feed = gather_rest(near_feed, 1, "w_feed_near", lower)
    mixed, kept, grouped, scale = retain(pre, consts, heads)
    sum_places = scatter_places()
    (total_out,) = terms(mixed, wo, sum_places[:1], rows, [low], None)
    rest_out = terms(tie(mixed, total_out), wo, sum_places[1:], rows, [f32] * (tensor_size - 1), None)
    total_out, lower, rest_out, near_feed = sync(total_out, lower, rest_out, near_feed)
    near_feed = gather_core(near_feed, "w_feed_near")
    far_feeds = {k: gather_step([upper[k], lower[k]], 0, "w_feed_far") for k in upper}

    def beside_out(step, total):
        nonlocal far_feeds
        if step == 1:
            total, far_feeds = sync(total, far_feeds)
            far_feeds = {k: gather_rest(v, 1, "w_feed_far") for k, v in far_feeds.items()}
        if step == tensor_size - 1:
            total, far_feeds = sync(total, far_feeds)
            far_feeds = {k: gather_core(v, "w_feed_far") for k, v in far_feeds.items()}
        return total

    attn_came, attn_own = scatter_ring(total_out, rest_out, "sum_attn", beside_out)

    middle, h_mlp = norm_rows(x_low, attn_came, attn_own, gain_two)
    h_came = swap(h_mlp, "tensor", 1, "rows_mlp")
    feeds = [near_feed] + [far_feeds[k] for k in pair_blocks[1:]]
    h_pair = [h_mlp, h_came]
    results, grad_h, grad_send = feed(h_pair, cots, feeds)
    grad_came = swap(grad_send, "tensor", 1, "sum_grad_mlp")

    late, late_rows, late_cots = tie((results, h_pair, cots), grad_send)
    pair_places = [jnp.zeros((), jnp.int32), jnp.ones((), jnp.int32)]

    def feed_groups(result):
        hidden, grad_act, grad_lin = result
        return [
            (late_rows, pair_places, [grad_act, grad_lin]),
            (late_cots, pair_places, [hidden]),
        ]

    far = {k: weight_gradient(feed_groups(late[k // 2]), 1) for k in pair_blocks[1:]}
    near_other = weight_gradient(feed_groups(late[0]), 1)
    grad_came, far, near_other = sync(grad_came, far, near_other)
    far_came = {k: swap(other, "dp", 1, "grad_feed_far") for k, other in far.items()}
    near_came = swap(near_other, "dp", 1, "grad_feed_near")
    grad_middle, gain_two_term, grad_mid_low = norm_back_rows(
        middle, cot, gain_two, grad_h, grad_came, True
    )

    grad_mixed = out_own = out_send = None
    mid_pieces = [grad_mid_low]

    def beside_mid(step, came):
        nonlocal far, near_came, grad_mixed, out_own, out_send
        if step == 1:
            late = tie(results, grad_mid_low)
            far = {
                k: weight_gradient(feed_groups(late[k // 2]), 0, far_came[k])
                for k in pair_blocks[1:]
            }
            came, far = sync(came, far)
            far = {k: scatter_step(v, 0, "grad_feed_far") for k, v in far.items()}
        if step == 2:
            late, weights = tie((results, feeds), mid_pieces[1])
            out_own, out_send = out_rows([result[0] for result in late], weights, middle)
            near_came = weight_gradient(feed_groups(late[0]), 0, near_came)
            came, out_own, out_send, near_came = sync(came, out_own, out_send, near_came)
        if step == tensor_size - 1:
            late = tie(mid_pieces, mid_pieces[-1])
            grad_mixed = project(late, wo, None, ring_places[:step], tensor_size)
            came, far, grad_mixed = sync(came, far, grad_mixed)
        mid_pieces.append(came)
        return came

    mid_pieces = gather_ring(grad_mid_low, "rows_grad_mid", beside_mid)
    out_came = swap(tie(out_send, mid_pieces[-1]), "tensor", 1, "sum_out")
    far = {k: scatter_rest(v, 1, "grad_feed_far") for k, v in far.items()}

    grad_mixed = project(mid_pieces[-1:], wo, grad_mixed, ring_places[-1:], tensor_size)
    grad_in = retain_back(grad_mixed, pre, kept, grouped, scale, consts, heads)

    grad_in, out_came, far, near = sync(grad_in, out_came, far, near_came)
    near = scatter_step(near, 0, "grad_feed_near")
    upper = {k: join(*parts[:2]) for k, parts in far.items()}
    lower = {k: join(*parts[2:]) for k, parts in far.items()}
    gain_places = [jnp.zeros((), jnp.int32)]
    gain_columns = jnp.eye(16, TILE, dtype=low)

    def out_groups(right):
        return [(mid_pieces, ring_places, [right]), ([gain_rows], gain_places, [gain_columns])]

    def swap_grad(parts):
        return {k: swap(part, "tensor", k, "grad_feed_far") for k, part in parts.items()}

    upper, lower_sent = swap_grad(upper), lower
    first_pairs, rest_pairs = h_pieces[1:2], h_pieces[2:] + h_pieces[:1]
    total_in, more = terms(grad_in, w_in, sum_places[:1], rows, [low], first_pairs)
    late_in = tie(grad_in, total_in)
    in_other = weight_gradient([(h_pieces, ring_places, [late_in])], 1)
    total_in, upper, in_other, near, lower_sent = sync(total_in, upper, in_other, near, lower_sent)
    lower = swap_grad(lower_sent)
    in_other = swap(in_other, "dp", 1, "grad_w_in")
    *rest_in, more_rest = terms(
        tie(grad_in, total_in), w_in, sum_places[1:], rows, [f32] * (tensor_size - 1), rest_pairs
    )
    late_in = tie(grad_in, more_rest)
    grads_in = weight_gradient([(h_pieces, ring_places, [late_in])], 0, in_other, 8)
    near = scatter_step(near, 1, "grad_feed_near", grads_in)
    total_in, lower, rest_in, grads_in, near = sync(total_in, lower, rest_in, grads_in, near)
    first_bits = dp_bits(dp_size)[-1]
    sent_on = [
        swap(part[3], "dp", bit, "grad_w_in") for part, bit in zip(grads_in, first_bits)
    ]
    gain_rows = jnp.concatenate(
        [(more + more_rest) / gain_one, gain_two_term, jnp.zeros((14, width), f32)], axis=0
    ).astype(low)
    out_other = weight_gradient(out_groups(tie(mixed, total_in)), 1)
    grads_out = None

    def beside_sum(step, total):
        nonlocal grads_in, grads_out, out_other, sent_on
        if step == 1:
            total, out_other, sent_on = sync(total, out_other, sent_on)
            kept_on = [
                swap(part[2], "dp", bit, "grad_w_in") for part, bit in zip(grads_in, first_bits)
            ]
            out_other = swap(out_other, "dp", 1, "grad_w_out")
            grads_in, sent_on, kept_on = tie((grads_in, sent_on, kept_on), total)
            grads_out = weight_gradient(out_groups(mixed), 0, out_other)
            sent_on = [
                add_rows(part[1], came, low) for part, came in zip(grads_in, sent_on)
            ]
            grads_in = [
                [add_rows(part[0], came, low), sent]
                for part, came, sent in zip(grads_in, kept_on, sent_on)
            ]
        if step == 2:
            total, grads_in, grads_out = sync(total, grads_in, grads_out)
            grads_in = scatter_rest(grads_in, 1, "grad_w_in")
            grads_out = scatter_rest(grads_out, 0, "grad_w_out")
        return total

    hattn_came, hattn_own = scatter_ring(total_in, rest_in, "sum_grad_attn", beside_sum)
    near = scatter_rest(near, 2, "grad_feed_near")
    grad_out_own = jnp.concatenate(grads_out, axis=0).astype(f32)
    columns = w_out.shape[0]
    grad_wo_own, gain_sum = grad_out_own[:, :columns], grad_out_own[:, columns : columns + 128]
    hattn_came, gain_sum = sync(hattn_came, gain_sum)
    for b in range(tensor_size.bit_length() - 1):
        gain_sum = gain_sum + swap(gain_sum, "tensor", 1 << b, "gains")
    grad_in_own = jnp.concatenate(grads_in, axis=0).astype(f32)
    grad_feed = jnp.concatenate(near, axis=0).astype(f32)
    for k in pair_blocks[1:]:
        grad_feed = grad_feed + jnp.concatenate([upper[k], lower[k]], axis=0).astype(f32)
    outputs = out_own + out_came.astype(f32)
    (grad_inputs,) = norm_back_rows(x_low, grad_middle, gain_one, hattn_own, hattn_came, False)

    def heads_back(first, size):
        return jnp.concatenate(
            [grad_in_own[:, h * stride + first : h * stride + first + size] for h in range(heads)],
            axis=1,
        )

    return (
        reorder(outputs.astype(low), back),
        reorder(grad_inputs, back),
        gain_sum[:, 0],
        heads_back(0, KD),
        heads_back(KD, KD),
        heads_back(2 * KD, VD),
        heads_back(2 * KD + VD, VD),
        grad_wo_own.T,
        gain_sum[:, 1],
        grad_feed[:, :hidden_cols],
        grad_feed[:, hidden_cols : 2 * hidden_cols],
        grad_feed[:, 2 * hidden_cols :].T,
    )


def solution(mesh):
    return jax.shard_map(
        shards,
        mesh=mesh,
        in_specs=(
            P(("dp", "tensor"), None),
            P("dp"),
            P("dp", "tensor"),
            P("dp", "tensor"),
            P("dp", "tensor"),
            P("dp", "tensor"),
            P("tensor", "dp"),
            P("dp"),
            P("dp", "tensor"),
            P("dp", "tensor"),
            P("tensor", "dp"),
            P(("dp", "tensor"), None),
            P("dp", None),
            P("dp", None),
        ),
        out_specs=(
            P(("dp", "tensor"), None),
            P(("dp", "tensor"), None),
            P("dp"),
            P("dp", "tensor"),
            P("dp", "tensor"),
            P("dp", "tensor"),
            P("dp", "tensor"),
            P("tensor", "dp"),
            P("dp"),
            P("dp", "tensor"),
            P("dp", "tensor"),
            P("tensor", "dp"),
        ),
        check_vma=False,
    )
```

```python
import functools
import math

import jax
import jax.numpy as jnp
from jax import lax
from jax.experimental import pallas as pl
from jax.experimental.pallas import tpu as pltpu
from jax.sharding import PartitionSpec as P

KD = 256
VD = 512
TILE = 256

epsilon = 1e-05
group_floor = 1.0
f32 = jnp.float32
low = jnp.bfloat16
gelu_slope = math.sqrt(2.0 / math.pi)
gelu_cubic = 0.044715


def layer_norm(values, floor_value=epsilon):
    center = values - jnp.mean(values, axis=-1, keepdims=True)
    scale_inv = lax.rsqrt(jnp.mean(center * center, axis=-1, keepdims=True) + floor_value)
    return (center * scale_inv, scale_inv)


def norm_back(grad_norm, normed, scale_inv):
    mean_grad = jnp.mean(grad_norm, axis=-1, keepdims=True)
    mean_cross = jnp.mean(grad_norm * normed, axis=-1, keepdims=True)
    return (grad_norm - mean_grad - normed * mean_cross) * scale_inv


def sequence_layout(lengths, offsets, total):
    places = jnp.arange(total, dtype=jnp.int32)[:, None]
    inside = (places >= offsets[None, :]) & (places < offsets[None, :] + lengths[None, :])
    numbers = jnp.arange(1, offsets.shape[0] + 1, dtype=jnp.int32)
    segment = jnp.sum(jnp.where(inside, numbers[None, :], 0), axis=1) - 1
    position = places[:, 0] - jnp.sum(jnp.where(inside, offsets[None, :], 0), axis=1)
    return (segment, position.astype(f32))


def rotation(position, size):
    half = size // 2
    frequency = jnp.exp(-math.log(10000.0) * jnp.arange(half, dtype=f32) * 2.0 / size)
    angles = position[:, None] * frequency[None, :]
    return (jnp.cos(angles), jnp.sin(angles))


def dot(left, right):
    return jnp.dot(left, right, preferred_element_type=f32)


def dot_nt(left, right):
    return lax.dot_general(left, right, (((1,), (1,)), ((), ())), preferred_element_type=f32)


def dot_tn(left, right):
    return lax.dot_general(left, right, (((0,), (0,)), ((), ())), preferred_element_type=f32)


def swap(values, axis, bits, name="swap"):
    size = lax.axis_size(axis)
    with jax.named_scope(f"{name}_{axis}{bits}"):
        return lax.ppermute(values, axis, [(i, i ^ bits) for i in range(size)])


def shift(values, axis, step, name="shift"):
    size = lax.axis_size(axis)
    with jax.named_scope(name):
        return lax.ppermute(values, axis, [(i, (i + step) % size) for i in range(size)])


def tie(values, token):
    return values if token is None else lax.optimization_barrier((values, token))[0]


def dp_bits(size):
    bits = [1 << b for b in range(1, size.bit_length() - 1)]
    return list(zip(bits, bits[1:] + bits[:1]))


def feature_order(size):
    same = []
    for half in (0, 1):
        held = [0]
        for bits in dp_bits(size):
            held += [k ^ bits[half] for k in held]
        same += [(k, half) for k in held]
    return same + [(k ^ 1, half) for k, half in same]


def gather_step(parts, stage, name, after=None):
    bits = dp_bits(lax.axis_size("dp"))[stage]
    parts = sync(*parts)
    came = tie([swap(part, "dp", bit, name) for part, bit in zip(parts, bits)], after)
    return [join(*pair) for pair in zip(parts, came)]


def gather_rest(parts, stage, name, after=None):
    for step in range(stage, len(dp_bits(lax.axis_size("dp")))):
        parts = gather_step(parts, step, name, after)
    return parts


def gather_core(parts, name):
    return [*parts, *(swap(part, "dp", 1, name) for part in sync(*parts))]


def scatter_send(parts, stage, name):
    bits = dp_bits(lax.axis_size("dp"))[-1 - stage]
    return [swap(sent, "dp", bit, name) for (_, sent), bit in zip(sync(*parts), bits)]


def scatter_add(parts, came):
    return [add_split(kept, part) for (kept, _), part in zip(parts, came)]


def scatter_step(parts, stage, name, after=None):
    return scatter_add(parts, tie(scatter_send(parts, stage, name), after))


def scatter_rest(parts, stage, name, after=None):
    for step in range(stage, len(dp_bits(lax.axis_size("dp")))):
        parts = scatter_step(parts, step, name, after)
    return [half for part in parts for half in part]


def sync(*values):
    return lax.optimization_barrier(values)


def gather_ring(rows, name, beside):
    pieces = [rows]
    for step in range(1, lax.axis_size("tensor")):
        came = shift(pieces[-1], "tensor", 1, f"{name}_{step}")
        pieces.append(beside(step, came))
    return pieces


def call(kernel, grid, in_specs, out_specs, out_shape, vmem=40, scratch=(), scalars=0, aliases=None):
    return pl.pallas_call(
        kernel,
        grid_spec=pltpu.PrefetchScalarGridSpec(
            num_scalar_prefetch=scalars,
            grid=grid,
            in_specs=in_specs,
            out_specs=out_specs,
            scratch_shapes=scratch,
        ),
        out_shape=out_shape,
        input_output_aliases=aliases or {},
        compiler_params=pltpu.CompilerParams(
            dimension_semantics=("arbitrary",) * len(grid), vmem_limit_bytes=vmem * 1024 * 1024
        ),
        cost_estimate=pl.CostEstimate(flops=0, bytes_accessed=0, transcendentals=0),
    )


def join_kernel(steps, *refs):
    step, first = pl.program_id(0), 0
    for ref, length in zip(refs[:-1], steps):

        @pl.when((step >= first) & (step < first + length))
        def _(ref=ref):
            refs[-1][...] = ref[...]

        first += length


def join(*parts):
    columns = parts[0].shape[1]
    height = min(min(part.shape[0] for part in parts), 256)
    steps, specs, first = [], [], 0
    for part in parts:
        length = part.shape[0] // height
        specs.append(
            pl.BlockSpec(
                (height, columns),
                lambda t, first=first, length=length: (jnp.clip(t - first, 0, length - 1), 0),
            )
        )
        steps.append(length)
        first += length
    return call(
        functools.partial(join_kernel, steps),
        (first,),
        specs,
        pl.BlockSpec((height, columns), lambda t: (t, 0)),
        jax.ShapeDtypeStruct((first * height, columns), parts[0].dtype),
        40,
    )(*parts)


def column_blocks_kernel(places, *refs):
    for ref, (column, first, size) in zip(refs[:-2], places):
        half = ref.shape[0] // 2
        refs[-2][:, first : first + size] = ref[:half, column : column + size]
        refs[-1][:, first : first + size] = ref[half:, column : column + size]


def column_blocks(sources):
    height = sources[0][0].shape[0]
    places, specs, first = [], [], 0
    for array, column, size in sources:
        places.append((column, first, size))
        specs.append(pl.BlockSpec(array.shape, lambda t: (0, 0)))
        first += size
    half = pl.BlockSpec((height // 2, first), lambda t: (0, 0))
    shape = jax.ShapeDtypeStruct((height // 2, first), sources[0][0].dtype)
    return call(
        functools.partial(column_blocks_kernel, places), (1,), specs, [half, half], [shape, shape]
    )(*[array for array, _, _ in sources])


def add_split_kernel(left, right, upper, lower):
    half = upper.shape[0]
    for i, out in enumerate((upper, lower)):
        rows = slice(i * half, (i + 1) * half)
        out[...] = (left[rows, :].astype(f32) + right[rows, :].astype(f32)).astype(low)


def add_split(left, right):
    count, columns = left.shape
    size = columns // 2 if columns % 256 == 0 else columns
    whole = pl.BlockSpec((count, size), lambda t: (0, t))
    half = pl.BlockSpec((count // 2, size), lambda t: (0, t))
    return call(
        add_split_kernel,
        (columns // size,),
        [whole, whole],
        [half, half],
        [jax.ShapeDtypeStruct((count // 2, columns), low)] * 2,
        40,
    )(left, right)


def add_kernel(left, right, out):
    out[...] = (left[...].astype(f32) + right[...].astype(f32)).astype(out.dtype)


def add_rows(left, right, kind):
    count, width = left.shape
    rows = pl.BlockSpec((count // 2, width), lambda i: (i, 0))
    shape = jax.ShapeDtypeStruct((count, width), kind)
    return call(add_kernel, (2,), [rows, rows], rows, shape)(left, right)


def scale_kernel(rows, gain, out):
    out[...] = (rows[...].astype(f32) * gain[...]).astype(low)


def scale_rows(values, gain):
    count, width = values.shape
    rows = pl.BlockSpec((count // 2, width), lambda i: (i, 0))
    line = pl.BlockSpec((1, width), lambda i: (0, 0))
    shape = jax.ShapeDtypeStruct((count, width), low)
    return call(scale_kernel, (2,), [rows, line], rows, shape)(values, gain[None])


def normed_kernel(values, out):
    out[...] = layer_norm(values[...].astype(f32))[0].astype(low)


def normed_rows(values):
    count, width = values.shape
    rows = pl.BlockSpec((count // 2, width), lambda i: (i, 0))
    shape = jax.ShapeDtypeStruct((count, width), low)
    return call(normed_kernel, (2,), [rows], rows, shape)(values)


def reorder_kernel(table, values, out):
    count = table.shape[0]
    width = values.shape[1] // count
    for place in range(count):
        start = pl.multiple_of(table[place] * width, width)
        out[:, place * width : (place + 1) * width] = values[:, pl.ds(start, width)]


def reorder(values, table):
    count, (rows, width) = table.shape[0], values.shape
    size = width // count
    if size % 128:
        blocks = [
            lax.dynamic_slice_in_dim(values, table[i] * size, size, axis=1) for i in range(count)
        ]
        return jnp.concatenate(blocks, axis=1)
    part = min(rows, 64)
    spec = pl.BlockSpec((part, width), lambda i, _: (i, 0))
    return call(
        reorder_kernel,
        (rows // part,),
        [spec],
        spec,
        jax.ShapeDtypeStruct(values.shape, values.dtype),
        40,
        scalars=1,
    )(table, values)


def project_kernel(count, places, *refs):
    weights, out = refs[count : count + 4], refs[-1]
    depth = weights[0].shape[0]
    for i in range(count):
        rows = refs[i]
        size = rows.shape[0]
        start = pl.multiple_of(places[i] * size, size) if out.shape[0] > size else 0
        out[pl.ds(start, size), :] = sum(
            dot(rows[:, q * depth : (q + 1) * depth], weights[q][...]) for q in range(4)
        )


def project(pieces, weight, whole, places, chunks):
    (count, width), columns = pieces[0].shape, weight[0].shape[1]
    size = 512 if columns % 512 == 0 else TILE
    spec = pl.BlockSpec((width // 4, size), lambda j, _: (0, j))
    rows = pl.BlockSpec((count, width), lambda j, _: (0, 0))
    number = len(pieces)
    if whole is None:
        held, out = [], pl.BlockSpec((count * chunks, size), lambda j, _: (0, j))
    else:
        held, out = [whole], pl.BlockSpec((count, size), lambda j, at: (at[0], j))
    return call(
        functools.partial(project_kernel, number),
        (columns // size,),
        [rows] * number + [spec] * 4 + [pl.BlockSpec(memory_space=pl.ANY)] * len(held),
        out,
        jax.ShapeDtypeStruct((count * chunks, columns), f32),
        56,
        scalars=1,
        aliases={number + 5: 0} if held else None,
    )(jnp.stack(places), *pieces, *weight, *held)


def part_specs(shape, steps, column):
    def spec(part):
        def index(i, j, *_):
            return (jnp.where(i == part, j, jnp.where(i < part, 0, steps - 1)), column)

        return pl.BlockSpec(shape, index)

    return [spec(part) for part in range(4)]


def terms_kernel(count, paired, places, *refs):
    weights, outs = refs[count : count + 4], refs[count + 4 :]
    pairs, outs = outs[: count * paired], outs[count * paired :]

    def give(weight):
        sums = 0.0
        for i, rows in enumerate(refs[:count]):
            result = dot_nt(rows[...], weight[...])
            outs[i][...] = result.astype(outs[i].dtype)
            if paired:
                sums = sums + jnp.sum(result * pairs[i][...].astype(f32), axis=0, keepdims=True)
        if paired:
            outs[count][...] = sums

    for part, weight in enumerate(weights):
        pl.when(pl.program_id(0) == part)(functools.partial(give, weight))


def terms(whole, weight, places, size, kinds, pairs):
    quarter, depth = weight[0].shape
    tile = min(quarter, 512 if depth <= 1024 else 256)
    steps = quarter // tile
    number = len(places)
    rows = [
        pl.BlockSpec((size, depth), lambda i, j, at, n=n: (at[n], 0)) for n in range(number)
    ]
    out = lambda height: pl.BlockSpec((height, tile), lambda i, j, _: (0, i * steps + j))
    paired = 1 if pairs else 0
    return call(
        functools.partial(terms_kernel, number, paired),
        (4, steps),
        rows + part_specs((tile, depth), steps, 0) + [out(size)] * (number * paired),
        [out(size)] * number + [out(1)] * paired,
        [jax.ShapeDtypeStruct((size, 4 * quarter), kind) for kind in kinds]
        + [jax.ShapeDtypeStruct((1, 4 * quarter), f32)] * paired,
        56,
        scalars=1,
    )(jnp.stack(places), *([whole] * number), *weight, *(pairs or []))


def scatter_places():
    own, size = lax.axis_index("tensor"), lax.axis_size("tensor")
    return [(own - step) % size for step in range(1, size + 1)]


def scatter_ring(total, rest, name, beside):
    for step, own in enumerate(rest, 1):
        came = shift(total, "tensor", 1, f"{name}_{step}")
        if step == len(rest):
            return beside(step, came), own
        total = beside(step, add_rows(came, own, low))


def norm_kernel(values, came, added, gain, middle, out):
    rows = values[...].astype(f32) + (came[...].astype(f32) + added[...])
    middle[...] = rows
    out[...] = (layer_norm(rows)[0] * gain[...]).astype(low)


def norm_rows(values, came, added, gain):
    count, width = values.shape
    size = min(count, 128)
    rows = pl.BlockSpec((size, width), lambda i: (i, 0))
    return call(
        norm_kernel,
        (count // size,),
        [rows, rows, rows, pl.BlockSpec((1, width), lambda i: (0, 0))],
        [rows, rows],
        [jax.ShapeDtypeStruct((count, width), f32), jax.ShapeDtypeStruct((count, width), low)],
        40,
    )(values, came, added, gain[None])


def norm_back_kernel(values, base, gain, grad, came, out, *more):
    given = grad[...] + came[...].astype(f32)
    normed, scale = layer_norm(values[...].astype(f32))
    result = base[...].astype(f32) + norm_back(given * gain[...], normed, scale)
    out[...] = result
    if not more:
        return
    more[1][...] = result.astype(low)
    term = jnp.sum(given * normed, axis=0, keepdims=True)

    @pl.when(pl.program_id(0) == 0)
    def _():
        more[0][...] = term

    @pl.when(pl.program_id(0) != 0)
    def _():
        more[0][...] += term


def norm_back_rows(values, base, gain, grad, came, more):
    count, width = values.shape
    size = min(count, 128)
    rows = pl.BlockSpec((size, width), lambda i: (i, 0))
    line = pl.BlockSpec((1, width), lambda i: (0, 0))
    shape = lambda height, kind: jax.ShapeDtypeStruct((height, width), kind)
    return call(
        norm_back_kernel,
        (count // size,),
        [rows, rows, line, rows, rows],
        [rows] + [line, rows] * more,
        [shape(count, f32)] + [shape(1, f32), shape(count, low)] * more,
        40,
    )(values, base, gain[None], grad, came)


def place_masks(size):
    row = lax.broadcasted_iota(jnp.int32, (size, size), 0)
    column = lax.broadcasted_iota(jnp.int32, (size, size), 1)
    return row, column


def block_decay(powers, head, apart, base, row, column, after, before):
    kept = (after == before) & (after >= 0)
    if apart == 0:
        kept = kept & (column <= row)
        return jnp.where(kept, base, 0.0)
    return jnp.where(kept, base * powers[head, apart], 0.0)


def retain_kernel(powers, logs, pre, cosine, sine, after, before, mixed, kept, grouped, scale):
    head = pl.program_id(0)
    total = pre.shape[0]
    half = KD // 2
    cos, sin = cosine[...], sine[...]
    for first, factor in ((0, KD ** (-0.5)), (KD, 1.0)):
        a, b = pre[:, first : first + half], pre[:, first + half : first + KD]
        kept[:, first : first + half] = ((a * cos - b * sin) * factor).astype(low)
        kept[:, first + half : first + KD] = ((a * sin + b * cos) * factor).astype(low)
    kept[:, 2 * KD :] = pre[:, 2 * KD : 2 * KD + VD].astype(low)
    row, column = place_masks(TILE)
    base = jnp.exp((row - column).astype(f32) * logs[head])
    for i in range(total // TILE):
        rows = slice(i * TILE, (i + 1) * TILE)
        held = jnp.zeros((TILE, VD), f32)
        for j in range(i + 1):
            past = slice(j * TILE, (j + 1) * TILE)
            decay = block_decay(powers, head, i - j, base, row, column, after[rows, :], before[:, past])
            scores = dot_nt(kept[rows, :KD], kept[past, KD : 2 * KD])
            held = held + dot((decay * scores).astype(low), kept[past, 2 * KD :])
        normed, inverse = layer_norm(held, group_floor)
        grouped[rows, :] = normed
        scale[rows, :] = jnp.broadcast_to(inverse, (TILE, 128))
        gate = pre[rows, 2 * KD + VD :]
        mixed[rows, :] = (gate * jax.nn.sigmoid(gate) * normed).astype(low)


def retain(pre, consts, heads):
    total = pre.shape[0]
    powers, logs, cosine, sine, after, before = consts
    whole = lambda a: pl.BlockSpec(a.shape, lambda h: (0, 0))
    smem = pl.BlockSpec(memory_space=pltpu.SMEM)
    by_head = lambda width: pl.BlockSpec((total, width), lambda h: (0, h))
    shape = lambda width, kind: jax.ShapeDtypeStruct((total, heads * width), kind)
    return call(
        retain_kernel,
        (heads,),
        [smem, smem, by_head(2 * KD + 2 * VD), whole(cosine), whole(sine), whole(after), whole(before)],
        [by_head(VD), by_head(2 * KD + VD), by_head(VD), by_head(128)],
        [shape(VD, low), shape(2 * KD + VD, low), shape(VD, f32), shape(128, f32)],
        56,
    )(*consts[:2], pre, *consts[2:])


def retain_back_kernel(
    powers, logs, grad, gates, kept, grouped, scale, cosine, sine, after, before, out, grad_low, grad_q, grad_k, grad_v
):
    head = pl.program_id(0)
    total = kept.shape[0]
    half = KD // 2
    blocks = total // TILE
    for i in range(blocks):
        rows = slice(i * TILE, (i + 1) * TILE)
        gate, normed, given = gates[rows, :], grouped[rows, :], grad[rows, :]
        sigmoid = jax.nn.sigmoid(gate)
        out[rows, 2 * KD + VD :] = (
            given * normed * sigmoid * (1.0 + gate * (1.0 - sigmoid))
        ).astype(low)
        grad_low[rows, :] = norm_back(given * (gate * sigmoid), normed, scale[rows, :1]).astype(low)
    row, column = place_masks(TILE)
    base = jnp.exp((row - column).astype(f32) * logs[head])
    for i in range(blocks):
        rows = slice(i * TILE, (i + 1) * TILE)
        query, grad_rows = kept[rows, :KD], grad_low[rows, :]
        held = jnp.zeros((TILE, KD), f32)
        for j in range(i + 1):
            past = slice(j * TILE, (j + 1) * TILE)
            decay = block_decay(powers, head, i - j, base, row, column, after[rows, :], before[:, past])
            key, value = kept[past, KD : 2 * KD], kept[past, 2 * KD :]
            weights = (decay * dot_nt(query, key)).astype(low)
            grad_scores = (dot_nt(grad_rows, value) * decay).astype(low)
            held = held + dot(grad_scores, key)
            key_term, value_term = dot_tn(grad_scores, query), dot_tn(weights, grad_rows)
            if i == j:
                grad_k[past, :], grad_v[past, :] = key_term, value_term
            else:
                grad_k[past, :] += key_term
                grad_v[past, :] += value_term
        grad_q[rows, :] = held
    cos, sin = cosine[...], sine[...]
    for first, source, factor in ((0, grad_q, KD ** (-0.5)), (KD, grad_k, 1.0)):
        a, b = source[:, :half] * factor, source[:, half:] * factor
        out[:, first : first + half] = (a * cos + b * sin).astype(low)
        out[:, first + half : first + KD] = (b * cos - a * sin).astype(low)
    out[:, 2 * KD : 2 * KD + VD] = grad_v[...].astype(low)


def retain_back(grad, pre, kept, grouped, scale, consts, heads):
    total = pre.shape[0]
    powers, logs, cosine, sine, after, before = consts
    whole = lambda a: pl.BlockSpec(a.shape, lambda h: (0, 0))
    smem = pl.BlockSpec(memory_space=pltpu.SMEM)
    by_head = lambda width: pl.BlockSpec((total, width), lambda h: (0, h))
    return call(
        retain_back_kernel,
        (heads,),
        [smem, smem, by_head(VD), pl.BlockSpec((total, VD), lambda h: (0, 3 * h + 2))]
        + [by_head(2 * KD + VD), by_head(VD), by_head(128)]
        + [whole(cosine), whole(sine), whole(after), whole(before)],
        by_head(2 * KD + 2 * VD),
        jax.ShapeDtypeStruct((total, heads * (2 * KD + 2 * VD)), low),
        56,
        scratch=[
            pltpu.VMEM((total, VD), low),
            pltpu.VMEM((total, KD), f32),
            pltpu.VMEM((total, KD), f32),
            pltpu.VMEM((total, VD), f32),
        ],
    )(*consts[:2], grad, pre, kept, grouped, scale, *consts[2:])


def feed_kernel(feeds, steps, *refs):
    given, weights = refs[:4], refs[4 : 4 + 4 * feeds]
    outs = refs[4 + 4 * feeds : 4 + 7 * feeds]
    own, sent = refs[4 + 7 * feeds : 6 + 7 * feeds]
    rows, cots, held, grads, total, row_sems, sems = refs[6 + 7 * feeds :]
    count, width = rows.shape
    depth, size = width // 4, held.shape[2] // 3
    step = pl.program_id(0)

    def row_copies():
        places = [(buffer, first) for buffer in (rows, cots) for first in (0, count // 2)]
        return [
            pltpu.make_async_copy(ref, buffer.at[pl.ds(first, count // 2)], row_sems.at[i])
            for i, (ref, (buffer, first)) in enumerate(zip(given, places))
        ]

    def weight_copies(number, tile, slot):
        columns = weights[0].shape[1] // 3
        return [
            pltpu.make_async_copy(
                weights[4 * number + part].at[:, pl.ds(pl.multiple_of(kind * columns + tile * size, size), size)],
                held.at[slot, pl.ds(part * depth, depth), pl.ds(kind * size, size)],
                sems.at[slot, 4 * kind + part],
            )
            for kind in range(3)
            for part in range(4)
        ]

    def for_step(at, act):
        for number in range(feeds):

            @pl.when((at >= number * steps) & (at < (number + 1) * steps))
            def _(number=number):
                for copy in weight_copies(number, at - number * steps, lax.rem(at, 2)):
                    act(copy)

    @pl.when(step == 0)
    def _():
        for copy in row_copies():
            copy.start()
        for_step(step, lambda copy: copy.start())

    for_step(step + 1, lambda copy: copy.start())

    @pl.when(step == 0)
    def _():
        for copy in row_copies():
            copy.wait()

    for_step(step, lambda copy: copy.wait())
    weight = held.at[lax.rem(step, 2)]
    up = weight[:, : 2 * size]
    both, grad_hidden = dot(rows[...], up), dot(cots[...], weight[:, 2 * size :])
    act, lin = both[:, :size], both[:, size:]
    curve = jnp.tanh(gelu_slope * (act + gelu_cubic * act * act * act))
    gelu = 0.5 * act * (1.0 + curve)
    slope = 0.5 * (1.0 + curve) + (0.5 * gelu_slope) * act * (1.0 - curve * curve) * (
        1.0 + (3.0 * gelu_cubic) * act * act
    )
    hidden = (gelu * lin).astype(low)
    grads[:, :size] = (grad_hidden * lin * slope).astype(low)
    grads[:, size:] = (grad_hidden * gelu).astype(low)
    for number in range(feeds):

        @pl.when((step >= number * steps) & (step < (number + 1) * steps))
        def _(number=number):
            outs[3 * number][...] = hidden
            outs[3 * number + 1][...] = grads[:, :size]
            outs[3 * number + 2][...] = grads[:, size:]

    add = dot_nt(grads[...], up)

    @pl.when(step == 0)
    def _():
        total[...] = add

    @pl.when(step != 0)
    def _():
        total[...] += add

    @pl.when(step == pl.num_programs(0) - 1)
    def _():
        own[...] = total[: count // 2, :]
        sent[...] = total[count // 2 :, :].astype(low)


def feed(rows, cots, feeds):
    count, width = rows[0].shape
    columns = feeds[0][0].shape[1] // 3
    size = min(512, columns)
    steps, number = columns // size, len(feeds)
    full = pl.BlockSpec((count, width), lambda t: (0, 0))
    anywhere = pl.BlockSpec(memory_space=pl.ANY)
    tiles = [
        pl.BlockSpec((2 * count, size), lambda t, k=k: (0, jnp.clip(t - k * steps, 0, steps - 1)))
        for k in range(number)
    ]
    shape = jax.ShapeDtypeStruct((2 * count, columns), low)
    outs = call(
        functools.partial(feed_kernel, number, steps),
        (number * steps,),
        [anywhere] * (4 + 4 * number),
        [tile for tile in tiles for _ in range(3)] + [full, full],
        [shape] * (3 * number)
        + [jax.ShapeDtypeStruct((count, width), f32), jax.ShapeDtypeStruct((count, width), low)],
        56,
        scratch=[
            pltpu.VMEM((2 * count, width), low),
            pltpu.VMEM((2 * count, width), low),
            pltpu.VMEM((2, width, 3 * size), low),
            pltpu.VMEM((2 * count, 2 * size), low),
            pltpu.VMEM((2 * count, width), f32),
            pltpu.SemaphoreType.DMA((4,)),
            pltpu.SemaphoreType.DMA((2, 12)),
        ],
    )(*rows, *cots, *[part for weight in feeds for part in weight])
    return [outs[3 * k : 3 * k + 3] for k in range(number)], outs[-2], outs[-1]


def out_kernel(number, *refs):
    hiddens, weights, base = refs[:number], refs[number : 5 * number], refs[5 * number]
    own, sent = refs[5 * number + 1 :]
    half = own.shape[0]

    def give(part):
        total = sum(dot_nt(hiddens[i][...], weights[4 * i + part][...]) for i in range(number))
        own[...] = base[...] + total[:half]
        sent[...] = total[half:].astype(low)

    for part in range(4):
        pl.when(pl.program_id(0) == part)(functools.partial(give, part))


def out_rows(hiddens, feeds, base):
    count, width = base.shape
    columns = hiddens[0].shape[1]
    size = min(256, width // 4)
    steps = width // 4 // size
    tile = pl.BlockSpec((count, size), lambda i, j: (0, i * steps + j))
    return call(
        functools.partial(out_kernel, len(hiddens)),
        (4, steps),
        [pl.BlockSpec((2 * count, columns), lambda i, j: (0, 0))] * len(hiddens)
        + part_specs((size, columns), steps, 2) * len(hiddens)
        + [tile],
        [tile, tile],
        [jax.ShapeDtypeStruct((count, width), f32), jax.ShapeDtypeStruct((count, width), low)],
        56,
    )(*hiddens, *[weight for parts in feeds for weight in parts], base)


def gradient_kernel(plan, added, came_steps, places, *refs):
    number = sum(pieces for pieces, _, _ in plan)
    lefts, rights = refs[:number], refs[number : number + sum(len(r) for _, r, _ in plan)]
    rest = refs[number + len(rights) :]
    came, outs, turned = rest[:added], rest[added:-1], rest[-1]
    step = pl.program_id(0)
    first = left_at = right_at = 0
    for pieces, lengths, size in plan:

        @pl.when(step == first)
        def _(left_at=left_at, pieces=pieces, size=size):
            for i in range(left_at, left_at + pieces):
                start = pl.multiple_of(places[i] * size, size) if pieces > 1 else 0
                turned[:, pl.ds(start, size)] = lefts[i][...].T

        for length in lengths:

            @pl.when((step >= first) & (step < first + length))
            def _(right=rights[right_at], depth=pieces * size):
                result = dot(turned[:, :depth], right[...])
                if added:
                    result = result + jnp.where(step < came_steps, came[0][...].astype(f32), 0.0)
                height = result.shape[0] // len(outs)
                for i, out in enumerate(outs):
                    out[...] = result[i * height : (i + 1) * height].astype(low)

            first, right_at = first + length, right_at + 1
        left_at += pieces


def weight_gradient(groups, side, came=None, pieces_out=4):
    width = groups[0][0][0].shape[1]
    half = width // 2
    count = max(pieces[0].shape[0] * len(pieces) for pieces, _, _ in groups)
    columns = sum(right.shape[1] for _, _, rights in groups for right in rights)
    size = min(512, min(right.shape[1] for _, _, rights in groups for right in rights))
    plan, lefts, rights, left_specs, right_specs, places, first = [], [], [], [], [], [], 0
    for pieces, at, given in groups:
        plan.append((len(pieces), [right.shape[1] // size for right in given], pieces[0].shape[0]))
        lefts += pieces
        places += at
        whole = pieces[0].shape[1] == width
        spec = pl.BlockSpec((pieces[0].shape[0], half), lambda t, _, whole=whole: (0, side if whole else 0))
        left_specs += [spec] * len(pieces)
        for right in given:
            steps = right.shape[1] // size
            right_specs.append(
                pl.BlockSpec(
                    (right.shape[0], size),
                    lambda t, _, first=first, steps=steps: (0, jnp.clip(t - first, 0, steps - 1)),
                )
            )
            rights.append(right)
            first += steps
    parts = 1 if came is None else pieces_out
    tile = lambda height: pl.BlockSpec((height, size), lambda t, _: (0, t))
    more = [] if came is None else [came]
    came_steps = 0 if came is None else came.shape[1] // size
    came_specs = [pl.BlockSpec((half, size), lambda t, _: (0, jnp.minimum(t, came_steps - 1)))] * len(more)
    outs = call(
        functools.partial(gradient_kernel, plan, len(more), came_steps),
        (columns // size,),
        left_specs + right_specs + came_specs,
        [tile(half // parts)] * parts,
        [jax.ShapeDtypeStruct((half // parts, columns), low)] * parts,
        56,
        scratch=[pltpu.VMEM((half, count), low)],
        scalars=1,
    )(jnp.stack(places), *lefts, *rights, *more)
    return outs[0] if came is None else [outs[: parts // 2], outs[parts // 2 :]]


def shards(
    inputs,
    gain_attn,
    w_query,
    w_key,
    w_value,
    w_gate,
    w_out,
    gain_mlp,
    w_act,
    w_lin,
    w_down,
    cotangent,
    lengths,
    offsets,
):
    rows, width = inputs.shape
    dp_size, tensor_size = lax.axis_size("dp"), lax.axis_size("tensor")
    dp_own, tensor_own = lax.axis_index("dp"), lax.axis_index("tensor")
    total = rows * tensor_size
    heads = w_query.shape[1] // KD
    hidden_cols = w_act.shape[1]
    half = width // 2

    order = feature_order(dp_size)
    taken = jnp.array([k for k, _ in order], jnp.int32)
    parts = jnp.array([i for _, i in order], jnp.int32)
    table = (taken ^ dp_own) * 2 + parts
    place = {pair: i for i, pair in enumerate(order)}
    places = jnp.array([[place[k, i] for i in range(2)] for k in range(dp_size)], jnp.int32)
    back = places[jnp.arange(dp_size, dtype=jnp.int32) ^ dp_own].reshape(-1)

    x_low = reorder(inputs, table)
    normed_one = normed_rows(x_low)
    stride = 2 * KD + 2 * VD
    head_blocks = []
    for h in range(heads):
        head_blocks += [(w_query, h * KD, KD), (w_key, h * KD, KD)]
        head_blocks += [(w_value, h * VD, VD), (w_gate, h * VD, VD)]
    pair_blocks = range(0, tensor_size, 2)

    head_first = tensor_own * heads
    head_numbers = (head_first + jnp.arange(heads, dtype=jnp.int32)).astype(f32)
    log_decay = jnp.log(1.0 - jnp.exp2(-5.0 - head_numbers))
    segment, position = sequence_layout(lengths[0], offsets[0], total)
    cosine, sine = rotation(position, KD)
    powers = jnp.exp(
        jnp.arange(total // TILE, dtype=f32)[None, :] * TILE * log_decay[:, None]
    )
    consts = (powers, log_decay, cosine, sine, segment[:, None], segment[None, :])
    ring_places = [(tensor_own - step) % tensor_size for step in range(tensor_size)]

    gains = jnp.concatenate([gain_attn.reshape(2, -1), gain_mlp.reshape(2, -1)], axis=1)
    parts = [gains[:1], gains[1:]]
    for bits in dp_bits(dp_size):
        parts = [
            jnp.concatenate([part, swap(part, "dp", bit, "gains")], axis=0)
            for part, bit in zip(sync(*parts), bits)
        ]
    gains_same = jnp.concatenate(parts, axis=0)
    gains = jnp.concatenate([gains_same, swap(gains_same, "dp", 1, "gains")], axis=0).astype(f32)
    fine = gains.shape[1] // 2
    gain_one, gain_two = gains[:, :fine].reshape(-1), gains[:, fine:].reshape(-1)

    w_in = gather_step(column_blocks(head_blocks), 0, "w_in")
    late_act, late_lin, late_down, late_out, late_cot = tie(
        (w_act, w_lin, w_down, w_out, cotangent), normed_one
    )
    feed_parts = column_blocks(
        [(late_act, 0, hidden_cols), (late_lin, 0, hidden_cols), (late_down.T, 0, hidden_cols)]
    )
    wo = column_blocks([(late_out.T, 0, w_out.shape[0])])
    cot = reorder(late_cot, table)

    def beside_attn(step, came):
        nonlocal w_in, wo, cot, feed_parts, consts
        if step == 1:
            came, w_in, wo, cot, feed_parts, consts = sync(came, w_in, wo, cot, feed_parts, consts)
            w_in = gather_rest(w_in, 1, "w_in", consts)
            wo = gather_step(tie(wo, w_in), 0, "w_out")
        return came

    pieces = gather_ring(normed_one, "rows_attn", beside_attn)
    rows_here, w_in, wo, feed_parts, gain_one, gain_two = sync(
        pieces[-1], w_in, wo, feed_parts, gain_one, gain_two
    )
    pieces[-1] = rows_here

    def swap_far(part):
        return {k: swap(part, "tensor", k, "w_feed_far") for k in pair_blocks[1:]}

    cot_came = swap(tie(cotangent, rows_here), "tensor", 1, "rows_cot")
    upper = swap_far(feed_parts[0])
    w_in = gather_core(w_in, "w_in")
    h_pieces = [scale_rows(piece, gain_one) for piece in pieces]
    pre = project(h_pieces[:-1], w_in, None, ring_places[:-1], tensor_size)
    wo = gather_rest(wo, 1, "w_out", pre)
    pre, cot_came, upper, wo, feed_parts = sync(pre, cot_came, upper, wo, feed_parts)
    wo = gather_core(wo, "w_out")

    lower = swap_far(tie(feed_parts[1], upper))
    pre = project(h_pieces[-1:], w_in, pre, ring_places[-1:], tensor_size)
    mixed, kept, grouped, scale = retain(pre, consts, heads)
    near_feed = gather_step(feed_parts, 0, "w_feed_near", mixed)
    near_feed = gather_rest(near_feed, 1, "w_feed_near")
    sum_places = scatter_places()
    (total_out,) = terms(mixed, wo, sum_places[:1], rows, [low], None)
    rest_out = terms(tie(mixed, total_out), wo, sum_places[1:], rows, [f32] * (tensor_size - 1), None)
    cots = [cot, reorder(tie(cot_came, total_out), table)]
    total_out, lower, cots = sync(total_out, lower, cots)
    far_feeds = {k: gather_step([upper[k], lower[k]], 0, "w_feed_far") for k in upper}

    def beside_out(step, total):
        nonlocal far_feeds, near_feed
        if step == 1:
            total, far_feeds = sync(total, far_feeds)
            far_feeds = {k: gather_rest(v, 1, "w_feed_far") for k, v in far_feeds.items()}
        if step == 2:
            total, near_feed = sync(total, near_feed)
            near_feed = gather_core(near_feed, "w_feed_near")
        if step == tensor_size - 1:
            total, far_feeds = sync(total, far_feeds)
            far_feeds = {k: gather_core(v, "w_feed_far") for k, v in far_feeds.items()}
        return total

    attn_came, attn_own = scatter_ring(total_out, rest_out, "sum_attn", beside_out)

    middle, h_mlp = norm_rows(x_low, attn_came, attn_own, gain_two)
    h_came = swap(h_mlp, "tensor", 1, "rows_mlp")
    feeds = [near_feed] + [far_feeds[k] for k in pair_blocks[1:]]
    h_pair = [h_mlp, h_came]
    results, grad_h, grad_send = feed(h_pair, cots, feeds)
    grad_came = swap(grad_send, "tensor", 1, "sum_grad_mlp")

    late, late_rows, late_cots = tie((results, h_pair, cots), grad_send)
    pair_places = [jnp.zeros((), jnp.int32), jnp.ones((), jnp.int32)]

    def feed_groups(result):
        hidden, grad_act, grad_lin = result
        return [
            (late_rows, pair_places, [grad_act, grad_lin]),
            (late_cots, pair_places, [hidden]),
        ]

    far = {k: weight_gradient(feed_groups(late[k // 2]), 1) for k in pair_blocks[1:]}
    near_other = weight_gradient(feed_groups(late[0]), 1)
    grad_came, far, near_other = sync(grad_came, far, near_other)
    far_came = {k: swap(other, "dp", 1, "grad_feed_far") for k, other in far.items()}
    near_came = None
    grad_middle, gain_two_term, grad_mid_low = norm_back_rows(
        middle, cot, gain_two, grad_h, grad_came, True
    )

    grad_mixed = out_own = out_send = None
    mid_pieces = [grad_mid_low]

    def beside_mid(step, came):
        nonlocal far, near_came, grad_mixed, out_own, out_send
        if step == 1:
            late = tie(results, grad_mid_low)
            far = {
                k: weight_gradient(feed_groups(late[k // 2]), 0, far_came[k])
                for k in pair_blocks[1:]
            }
            came, far, near_last = sync(came, far, near_other)
            near_came = swap(near_last, "dp", 1, "grad_feed_near")
            far = {k: scatter_step(v, 0, "grad_feed_far") for k, v in far.items()}
        if step == 2:
            late, weights = tie((results, feeds), mid_pieces[1])
            out_own, out_send = out_rows([result[0] for result in late], weights, middle)
            near_came = weight_gradient(feed_groups(late[0]), 0, near_came)
            came, out_own, out_send, near_came = sync(came, out_own, out_send, near_came)
        if step == tensor_size - 1:
            late = tie(mid_pieces, mid_pieces[-1])
            grad_mixed = project(late, wo, None, ring_places[:step], tensor_size)
            came, far, grad_mixed = sync(came, far, grad_mixed)
        mid_pieces.append(came)
        return came

    mid_pieces = gather_ring(grad_mid_low, "rows_grad_mid", beside_mid)
    out_came = swap(tie(out_send, mid_pieces[-1]), "tensor", 1, "sum_out")
    far = {k: scatter_rest(v, 1, "grad_feed_far") for k, v in far.items()}

    grad_mixed = project(mid_pieces[-1:], wo, grad_mixed, ring_places[-1:], tensor_size)
    grad_in = retain_back(grad_mixed, pre, kept, grouped, scale, consts, heads)

    grad_in, out_came, far, near = sync(grad_in, out_came, far, near_came)
    near = scatter_step(near, 0, "grad_feed_near")
    upper = {k: join(*parts[:2]) for k, parts in far.items()}
    lower = {k: join(*parts[2:]) for k, parts in far.items()}
    gain_places = [jnp.zeros((), jnp.int32)]
    gain_columns = jnp.eye(16, TILE, dtype=low)

    def out_groups(right):
        return [(mid_pieces, ring_places, [right])]

    def swap_grad(parts):
        return {k: swap(part, "tensor", k, "grad_feed_far") for k, part in parts.items()}

    upper, lower_sent = swap_grad(upper), lower
    first_pairs, rest_pairs = h_pieces[1:2], h_pieces[2:] + h_pieces[:1]
    total_in, more = terms(grad_in, w_in, sum_places[:1], rows, [low], first_pairs)
    late_in = tie(grad_in, total_in)
    in_other = weight_gradient([(h_pieces, ring_places, [late_in])], 1)
    out_other = weight_gradient(out_groups(tie(mixed, in_other)), 1)
    total_in, upper, in_other, out_other, near, lower_sent = sync(
        total_in, upper, in_other, out_other, near, lower_sent
    )
    lower = swap_grad(lower_sent)
    in_other = swap(in_other, "dp", 1, "grad_w_in")
    out_other = swap(out_other, "dp", 1, "grad_w_out")
    *rest_in, more_rest = terms(
        tie(grad_in, total_in), w_in, sum_places[1:], rows, [f32] * (tensor_size - 1), rest_pairs
    )
    late_in = tie(grad_in, more_rest)
    grads_in = weight_gradient([(h_pieces, ring_places, [late_in])], 0, in_other, 8)
    near = scatter_step(near, 1, "grad_feed_near", grads_in)
    total_in, lower, rest_in, grads_in, near, out_other = sync(
        total_in, lower, rest_in, grads_in, near, out_other
    )
    first_bits = dp_bits(dp_size)[-1]
    sent_on = [
        swap(part[3], "dp", bit, "grad_w_in") for part, bit in zip(grads_in, first_bits)
    ]
    gain_rows = jnp.concatenate([(more + more_rest) / gain_one, gain_two_term], axis=0)
    gain_rows = gain_rows[:, :half] + swap(gain_rows[:, half:], "dp", 1, "gains")
    gain_rows = jnp.concatenate([gain_rows, jnp.zeros((14, half), f32)], axis=0).astype(low)
    grads_out = weight_gradient(
        out_groups(tie(mixed, total_in)) + [([gain_rows], gain_places, [gain_columns])], 0, out_other
    )
    out_sent = scatter_send(grads_out, 0, "grad_w_out")

    def beside_sum(step, total):
        nonlocal grads_in, grads_out, sent_on
        if step == 1:
            total, sent_on, grads_out = sync(total, sent_on, grads_out)
            kept_on = [
                swap(part[2], "dp", bit, "grad_w_in") for part, bit in zip(grads_in, first_bits)
            ]
            grads_in, sent_on = tie((grads_in, sent_on), total)
            sent_on = [
                add_rows(part[1], came, low) for part, came in zip(grads_in, sent_on)
            ]
            grads_in = [
                [add_rows(part[0], came, low), sent]
                for part, came, sent in zip(grads_in, kept_on, sent_on)
            ]
            grads_out = scatter_add(grads_out, tie(out_sent, total))
        return total

    hattn_came, hattn_own = scatter_ring(total_in, rest_in, "sum_grad_attn", beside_sum)
    (grad_inputs,) = norm_back_rows(x_low, grad_middle, gain_one, hattn_own, hattn_came, False)
    grad_inputs = reorder(grad_inputs, back)
    grads_out = scatter_rest(grads_out, 1, "grad_w_out")
    grads_in = scatter_rest(tie(grads_in, grads_out), 1, "grad_w_in", grad_inputs)
    near = scatter_rest(near, 2, "grad_feed_near")
    grad_out_own = jnp.concatenate(grads_out, axis=0).astype(f32)
    columns = w_out.shape[0]
    grad_wo_own, gain_sum = grad_out_own[:, :columns], grad_out_own[:, columns : columns + 2].T
    gain_sums = [gain_sum] + [swap(gain_sum, "tensor", k, "gains") for k in range(1, tensor_size)]
    while len(gain_sums) > 1:
        gain_sums = [a + b for a, b in zip(gain_sums[::2], gain_sums[1::2])]
    gain_sum = gain_sums[0]
    grad_in_own = jnp.concatenate(grads_in, axis=0).astype(f32)
    grad_feed = jnp.concatenate(near, axis=0).astype(f32)
    for k in pair_blocks[1:]:
        grad_feed = grad_feed + jnp.concatenate([upper[k], lower[k]], axis=0).astype(f32)
    outputs = out_own + out_came.astype(f32)

    def heads_back(first, size):
        return jnp.concatenate(
            [grad_in_own[:, h * stride + first : h * stride + first + size] for h in range(heads)],
            axis=1,
        )

    return (
        reorder(outputs.astype(low), back),
        grad_inputs,
        gain_sum[0],
        heads_back(0, KD),
        heads_back(KD, KD),
        heads_back(2 * KD, VD),
        heads_back(2 * KD + VD, VD),
        grad_wo_own.T,
        gain_sum[1],
        grad_feed[:, :hidden_cols],
        grad_feed[:, hidden_cols : 2 * hidden_cols],
        grad_feed[:, 2 * hidden_cols :].T,
    )


def solution(mesh):
    return jax.shard_map(
        shards,
        mesh=mesh,
        in_specs=(
            P(("dp", "tensor"), None),
            P("dp"),
            P("dp", "tensor"),
            P("dp", "tensor"),
            P("dp", "tensor"),
            P("dp", "tensor"),
            P("tensor", "dp"),
            P("dp"),
            P("dp", "tensor"),
            P("dp", "tensor"),
            P("tensor", "dp"),
            P(("dp", "tensor"), None),
            P("dp", None),
            P("dp", None),
        ),
        out_specs=(
            P(("dp", "tensor"), None),
            P(("dp", "tensor"), None),
            P("dp"),
            P("dp", "tensor"),
            P("dp", "tensor"),
            P("dp", "tensor"),
            P("dp", "tensor"),
            P("tensor", "dp"),
            P("dp"),
            P("dp", "tensor"),
            P("dp", "tensor"),
            P("tensor", "dp"),
        ),
        check_vma=False,
    )
```

```python
import functools
import math

import jax
import jax.numpy as jnp
from jax import lax
from jax.experimental import pallas as pl
from jax.experimental.pallas import tpu as pltpu
from jax.sharding import PartitionSpec as P

KD = 256
VD = 512
TILE = 256

epsilon = 1e-05
group_floor = 1.0
f32 = jnp.float32
low = jnp.bfloat16
gelu_slope = math.sqrt(2.0 / math.pi)
gelu_cubic = 0.044715


def layer_norm(values, floor_value=epsilon):
    center = values - jnp.mean(values, axis=-1, keepdims=True)
    scale_inv = lax.rsqrt(jnp.mean(center * center, axis=-1, keepdims=True) + floor_value)
    return (center * scale_inv, scale_inv)


def norm_back(grad_norm, normed, scale_inv):
    mean_grad = jnp.mean(grad_norm, axis=-1, keepdims=True)
    mean_cross = jnp.mean(grad_norm * normed, axis=-1, keepdims=True)
    return (grad_norm - mean_grad - normed * mean_cross) * scale_inv


def sequence_layout(lengths, offsets, total):
    places = jnp.arange(total, dtype=jnp.int32)[:, None]
    inside = (places >= offsets[None, :]) & (places < offsets[None, :] + lengths[None, :])
    numbers = jnp.arange(1, offsets.shape[0] + 1, dtype=jnp.int32)
    segment = jnp.sum(jnp.where(inside, numbers[None, :], 0), axis=1) - 1
    position = places[:, 0] - jnp.sum(jnp.where(inside, offsets[None, :], 0), axis=1)
    return (segment, position.astype(f32))


def rotation(position, size):
    half = size // 2
    frequency = jnp.exp(-math.log(10000.0) * jnp.arange(half, dtype=f32) * 2.0 / size)
    angles = position[:, None] * frequency[None, :]
    return (jnp.cos(angles), jnp.sin(angles))


def dot(left, right):
    return jnp.dot(left, right, preferred_element_type=f32)


def dot_nt(left, right):
    return lax.dot_general(left, right, (((1,), (1,)), ((), ())), preferred_element_type=f32)


def dot_tn(left, right):
    return lax.dot_general(left, right, (((0,), (0,)), ((), ())), preferred_element_type=f32)


def swap(values, axis, bits, name="swap"):
    size = lax.axis_size(axis)
    with jax.named_scope(f"{name}_{axis}{bits}"):
        return lax.ppermute(values, axis, [(i, i ^ bits) for i in range(size)])


def shift(values, axis, step, name="shift"):
    size = lax.axis_size(axis)
    with jax.named_scope(name):
        return lax.ppermute(values, axis, [(i, (i + step) % size) for i in range(size)])


def tie(values, token):
    return values if token is None else lax.optimization_barrier((values, token))[0]


def dp_bits(size):
    bits = [1 << b for b in range(1, size.bit_length() - 1)]
    return list(zip(bits, bits[1:] + bits[:1]))


def feature_order(size):
    same = []
    for half in (0, 1):
        held = [0]
        for bits in dp_bits(size):
            held += [k ^ bits[half] for k in held]
        same += [(k, half) for k in held]
    return same + [(k ^ 1, half) for k, half in same]


def gather_step(parts, stage, name, after=None):
    bits = dp_bits(lax.axis_size("dp"))[stage]
    parts = sync(*parts)
    came = tie([swap(part, "dp", bit, name) for part, bit in zip(parts, bits)], after)
    return [join(*pair) for pair in zip(parts, came)]


def gather_rest(parts, stage, name, after=None):
    for step in range(stage, len(dp_bits(lax.axis_size("dp")))):
        parts = gather_step(parts, step, name, after)
    return parts


def gather_core(parts, name):
    return [*parts, *(swap(part, "dp", 1, name) for part in sync(*parts))]


def scatter_send(parts, stage, name):
    bits = dp_bits(lax.axis_size("dp"))[-1 - stage]
    return [swap(sent, "dp", bit, name) for (_, sent), bit in zip(sync(*parts), bits)]


def scatter_add(parts, came):
    return [add_split(kept, part) for (kept, _), part in zip(parts, came)]


def scatter_step(parts, stage, name, after=None):
    return scatter_add(parts, tie(scatter_send(parts, stage, name), after))


def scatter_rest(parts, stage, name, after=None):
    for step in range(stage, len(dp_bits(lax.axis_size("dp")))):
        parts = scatter_step(parts, step, name, after)
    return [half for part in parts for half in part]


def sync(*values):
    return lax.optimization_barrier(values)


def gather_ring(rows, name, beside):
    pieces = [rows]
    for step in range(1, lax.axis_size("tensor")):
        came = shift(pieces[-1], "tensor", 1, f"{name}_{step}")
        pieces.append(beside(step, came))
    return pieces


def call(kernel, grid, in_specs, out_specs, out_shape, vmem=40, scratch=(), scalars=0, aliases=None):
    return pl.pallas_call(
        kernel,
        grid_spec=pltpu.PrefetchScalarGridSpec(
            num_scalar_prefetch=scalars,
            grid=grid,
            in_specs=in_specs,
            out_specs=out_specs,
            scratch_shapes=scratch,
        ),
        out_shape=out_shape,
        input_output_aliases=aliases or {},
        compiler_params=pltpu.CompilerParams(
            dimension_semantics=("arbitrary",) * len(grid), vmem_limit_bytes=vmem * 1024 * 1024
        ),
        cost_estimate=pl.CostEstimate(flops=0, bytes_accessed=0, transcendentals=0),
    )


def join_kernel(steps, *refs):
    step, first = pl.program_id(0), 0
    for ref, length in zip(refs[:-1], steps):

        @pl.when((step >= first) & (step < first + length))
        def _(ref=ref):
            refs[-1][...] = ref[...]

        first += length


def join(*parts):
    columns = parts[0].shape[1]
    height = min(min(part.shape[0] for part in parts), 256)
    steps, specs, first = [], [], 0
    for part in parts:
        length = part.shape[0] // height
        specs.append(
            pl.BlockSpec(
                (height, columns),
                lambda t, first=first, length=length: (jnp.clip(t - first, 0, length - 1), 0),
            )
        )
        steps.append(length)
        first += length
    return call(
        functools.partial(join_kernel, steps),
        (first,),
        specs,
        pl.BlockSpec((height, columns), lambda t: (t, 0)),
        jax.ShapeDtypeStruct((first * height, columns), parts[0].dtype),
        40,
    )(*parts)


def column_blocks_kernel(places, *refs):
    for ref, (column, first, size) in zip(refs[:-2], places):
        half = ref.shape[0] // 2
        refs[-2][:, first : first + size] = ref[:half, column : column + size]
        refs[-1][:, first : first + size] = ref[half:, column : column + size]


def column_blocks(sources):
    height = sources[0][0].shape[0]
    places, specs, first = [], [], 0
    for array, column, size in sources:
        places.append((column, first, size))
        specs.append(pl.BlockSpec(array.shape, lambda t: (0, 0)))
        first += size
    half = pl.BlockSpec((height // 2, first), lambda t: (0, 0))
    shape = jax.ShapeDtypeStruct((height // 2, first), sources[0][0].dtype)
    return call(
        functools.partial(column_blocks_kernel, places), (1,), specs, [half, half], [shape, shape]
    )(*[array for array, _, _ in sources])


def add_split_kernel(left, right, upper, lower):
    half = upper.shape[0]
    for i, out in enumerate((upper, lower)):
        rows = slice(i * half, (i + 1) * half)
        out[...] = (left[rows, :].astype(f32) + right[rows, :].astype(f32)).astype(low)


def add_split(left, right):
    count, columns = left.shape
    size = columns // 2 if columns % 256 == 0 else columns
    whole = pl.BlockSpec((count, size), lambda t: (0, t))
    half = pl.BlockSpec((count // 2, size), lambda t: (0, t))
    return call(
        add_split_kernel,
        (columns // size,),
        [whole, whole],
        [half, half],
        [jax.ShapeDtypeStruct((count // 2, columns), low)] * 2,
        40,
    )(left, right)


def add_kernel(left, right, out):
    out[...] = (left[...].astype(f32) + right[...].astype(f32)).astype(out.dtype)


def add_rows(left, right, kind):
    count, width = left.shape
    rows = pl.BlockSpec((count // 2, width), lambda i: (i, 0))
    shape = jax.ShapeDtypeStruct((count, width), kind)
    return call(add_kernel, (2,), [rows, rows], rows, shape)(left, right)


def scale_kernel(rows, gain, out):
    out[...] = (rows[...].astype(f32) * gain[...]).astype(low)


def scale_rows(values, gain):
    count, width = values.shape
    rows = pl.BlockSpec((count // 2, width), lambda i: (i, 0))
    line = pl.BlockSpec((1, width), lambda i: (0, 0))
    shape = jax.ShapeDtypeStruct((count, width), low)
    return call(scale_kernel, (2,), [rows, line], rows, shape)(values, gain[None])


def normed_kernel(values, out):
    out[...] = layer_norm(values[...].astype(f32))[0].astype(low)


def normed_rows(values):
    count, width = values.shape
    rows = pl.BlockSpec((count // 2, width), lambda i: (i, 0))
    shape = jax.ShapeDtypeStruct((count, width), low)
    return call(normed_kernel, (2,), [rows], rows, shape)(values)


def reorder_kernel(table, values, out):
    count = table.shape[0]
    width = values.shape[1] // count
    for place in range(count):
        start = pl.multiple_of(table[place] * width, width)
        out[:, place * width : (place + 1) * width] = values[:, pl.ds(start, width)]


def reorder(values, table):
    count, (rows, width) = table.shape[0], values.shape
    size = width // count
    if size % 128:
        blocks = [
            lax.dynamic_slice_in_dim(values, table[i] * size, size, axis=1) for i in range(count)
        ]
        return jnp.concatenate(blocks, axis=1)
    part = min(rows, 64)
    spec = pl.BlockSpec((part, width), lambda i, _: (i, 0))
    return call(
        reorder_kernel,
        (rows // part,),
        [spec],
        spec,
        jax.ShapeDtypeStruct(values.shape, values.dtype),
        40,
        scalars=1,
    )(table, values)


def project_kernel(count, places, *refs):
    weights, out = refs[count : count + 4], refs[-1]
    depth = weights[0].shape[0]
    for i in range(count):
        rows = refs[i]
        size = rows.shape[0]
        start = pl.multiple_of(places[i] * size, size) if out.shape[0] > size else 0
        out[pl.ds(start, size), :] = sum(
            dot(rows[:, q * depth : (q + 1) * depth], weights[q][...]) for q in range(4)
        )


def project(pieces, weight, whole, places, chunks):
    (count, width), columns = pieces[0].shape, weight[0].shape[1]
    size = 512 if columns % 512 == 0 else TILE
    spec = pl.BlockSpec((width // 4, size), lambda j, _: (0, j))
    rows = pl.BlockSpec((count, width), lambda j, _: (0, 0))
    number = len(pieces)
    if whole is None:
        held, out = [], pl.BlockSpec((count * chunks, size), lambda j, _: (0, j))
    else:
        held, out = [whole], pl.BlockSpec((count, size), lambda j, at: (at[0], j))
    return call(
        functools.partial(project_kernel, number),
        (columns // size,),
        [rows] * number + [spec] * 4 + [pl.BlockSpec(memory_space=pl.ANY)] * len(held),
        out,
        jax.ShapeDtypeStruct((count * chunks, columns), f32),
        56,
        scalars=1,
        aliases={number + 5: 0} if held else None,
    )(jnp.stack(places), *pieces, *weight, *held)


def part_specs(shape, steps, column):
    def spec(part):
        def index(i, j, *_):
            return (jnp.where(i == part, j, jnp.where(i < part, 0, steps - 1)), column)

        return pl.BlockSpec(shape, index)

    return [spec(part) for part in range(4)]


def terms_kernel(count, paired, places, *refs):
    weights, outs = refs[count : count + 4], refs[count + 4 :]
    pairs, outs = outs[: count * paired], outs[count * paired :]

    def give(weight):
        sums = 0.0
        for i, rows in enumerate(refs[:count]):
            result = dot_nt(rows[...], weight[...])
            outs[i][...] = result.astype(outs[i].dtype)
            if paired:
                sums = sums + jnp.sum(result * pairs[i][...].astype(f32), axis=0, keepdims=True)
        if paired:
            outs[count][...] = sums

    for part, weight in enumerate(weights):
        pl.when(pl.program_id(0) == part)(functools.partial(give, weight))


def terms(whole, weight, places, size, kinds, pairs):
    quarter, depth = weight[0].shape
    tile = min(quarter, 512 if depth <= 1024 else 256)
    steps = quarter // tile
    number = len(places)
    rows = [
        pl.BlockSpec((size, depth), lambda i, j, at, n=n: (at[n], 0)) for n in range(number)
    ]
    out = lambda height: pl.BlockSpec((height, tile), lambda i, j, _: (0, i * steps + j))
    paired = 1 if pairs else 0
    return call(
        functools.partial(terms_kernel, number, paired),
        (4, steps),
        rows + part_specs((tile, depth), steps, 0) + [out(size)] * (number * paired),
        [out(size)] * number + [out(1)] * paired,
        [jax.ShapeDtypeStruct((size, 4 * quarter), kind) for kind in kinds]
        + [jax.ShapeDtypeStruct((1, 4 * quarter), f32)] * paired,
        56,
        scalars=1,
    )(jnp.stack(places), *([whole] * number), *weight, *(pairs or []))


def scatter_places():
    own, size = lax.axis_index("tensor"), lax.axis_size("tensor")
    return [(own - step) % size for step in range(1, size + 1)]


def scatter_ring(total, rest, name, beside):
    for step, own in enumerate(rest, 1):
        came = shift(total, "tensor", 1, f"{name}_{step}")
        if step == len(rest):
            return beside(step, came), own
        total = beside(step, add_rows(came, own, low))


def norm_kernel(values, came, added, gain, middle, out):
    rows = values[...].astype(f32) + (came[...].astype(f32) + added[...])
    middle[...] = rows
    out[...] = (layer_norm(rows)[0] * gain[...]).astype(low)


def norm_rows(values, came, added, gain):
    count, width = values.shape
    size = min(count, 128)
    rows = pl.BlockSpec((size, width), lambda i: (i, 0))
    return call(
        norm_kernel,
        (count // size,),
        [rows, rows, rows, pl.BlockSpec((1, width), lambda i: (0, 0))],
        [rows, rows],
        [jax.ShapeDtypeStruct((count, width), f32), jax.ShapeDtypeStruct((count, width), low)],
        40,
    )(values, came, added, gain[None])


def norm_back_kernel(values, base, gain, grad, came, out, *more):
    given = grad[...] + came[...].astype(f32)
    normed, scale = layer_norm(values[...].astype(f32))
    result = base[...].astype(f32) + norm_back(given * gain[...], normed, scale)
    out[...] = result
    if not more:
        return
    more[1][...] = result.astype(low)
    term = jnp.sum(given * normed, axis=0, keepdims=True)

    @pl.when(pl.program_id(0) == 0)
    def _():
        more[0][...] = term

    @pl.when(pl.program_id(0) != 0)
    def _():
        more[0][...] += term


def norm_back_rows(values, base, gain, grad, came, more):
    count, width = values.shape
    size = min(count, 128)
    rows = pl.BlockSpec((size, width), lambda i: (i, 0))
    line = pl.BlockSpec((1, width), lambda i: (0, 0))
    shape = lambda height, kind: jax.ShapeDtypeStruct((height, width), kind)
    return call(
        norm_back_kernel,
        (count // size,),
        [rows, rows, line, rows, rows],
        [rows] + [line, rows] * more,
        [shape(count, f32)] + [shape(1, f32), shape(count, low)] * more,
        40,
    )(values, base, gain[None], grad, came)


def place_masks(size):
    row = lax.broadcasted_iota(jnp.int32, (size, size), 0)
    column = lax.broadcasted_iota(jnp.int32, (size, size), 1)
    return row, column


def block_decay(powers, head, apart, base, row, column, after, before):
    kept = (after == before) & (after >= 0)
    if apart == 0:
        kept = kept & (column <= row)
        return jnp.where(kept, base, 0.0)
    return jnp.where(kept, base * powers[head, apart], 0.0)


def retain_kernel(powers, logs, pre, cosine, sine, after, before, mixed, kept, grouped, scale):
    head = pl.program_id(0)
    total = pre.shape[0]
    half = KD // 2
    cos, sin = cosine[...], sine[...]
    for first, factor in ((0, KD ** (-0.5)), (KD, 1.0)):
        a, b = pre[:, first : first + half], pre[:, first + half : first + KD]
        kept[:, first : first + half] = ((a * cos - b * sin) * factor).astype(low)
        kept[:, first + half : first + KD] = ((a * sin + b * cos) * factor).astype(low)
    kept[:, 2 * KD :] = pre[:, 2 * KD : 2 * KD + VD].astype(low)
    row, column = place_masks(TILE)
    base = jnp.exp((row - column).astype(f32) * logs[head])
    for i in range(total // TILE):
        rows = slice(i * TILE, (i + 1) * TILE)
        held = jnp.zeros((TILE, VD), f32)
        for j in range(i + 1):
            past = slice(j * TILE, (j + 1) * TILE)
            decay = block_decay(powers, head, i - j, base, row, column, after[rows, :], before[:, past])
            scores = dot_nt(kept[rows, :KD], kept[past, KD : 2 * KD])
            held = held + dot((decay * scores).astype(low), kept[past, 2 * KD :])
        normed, inverse = layer_norm(held, group_floor)
        grouped[rows, :] = normed
        scale[rows, :] = jnp.broadcast_to(inverse, (TILE, 128))
        gate = pre[rows, 2 * KD + VD :]
        mixed[rows, :] = (gate * jax.nn.sigmoid(gate) * normed).astype(low)


def retain(pre, consts, heads):
    total = pre.shape[0]
    powers, logs, cosine, sine, after, before = consts
    whole = lambda a: pl.BlockSpec(a.shape, lambda h: (0, 0))
    smem = pl.BlockSpec(memory_space=pltpu.SMEM)
    by_head = lambda width: pl.BlockSpec((total, width), lambda h: (0, h))
    shape = lambda width, kind: jax.ShapeDtypeStruct((total, heads * width), kind)
    return call(
        retain_kernel,
        (heads,),
        [smem, smem, by_head(2 * KD + 2 * VD), whole(cosine), whole(sine), whole(after), whole(before)],
        [by_head(VD), by_head(2 * KD + VD), by_head(VD), by_head(128)],
        [shape(VD, low), shape(2 * KD + VD, low), shape(VD, f32), shape(128, f32)],
        56,
    )(*consts[:2], pre, *consts[2:])


def retain_back_kernel(
    powers, logs, grad, gates, kept, grouped, scale, cosine, sine, after, before, out, grad_low, grad_q, grad_k, grad_v
):
    head = pl.program_id(0)
    total = kept.shape[0]
    half = KD // 2
    blocks = total // TILE
    for i in range(blocks):
        rows = slice(i * TILE, (i + 1) * TILE)
        gate, normed, given = gates[rows, :], grouped[rows, :], grad[rows, :]
        sigmoid = jax.nn.sigmoid(gate)
        out[rows, 2 * KD + VD :] = (
            given * normed * sigmoid * (1.0 + gate * (1.0 - sigmoid))
        ).astype(low)
        grad_low[rows, :] = norm_back(given * (gate * sigmoid), normed, scale[rows, :1]).astype(low)
    row, column = place_masks(TILE)
    base = jnp.exp((row - column).astype(f32) * logs[head])
    for i in range(blocks):
        rows = slice(i * TILE, (i + 1) * TILE)
        query, grad_rows = kept[rows, :KD], grad_low[rows, :]
        held = jnp.zeros((TILE, KD), f32)
        for j in range(i + 1):
            past = slice(j * TILE, (j + 1) * TILE)
            decay = block_decay(powers, head, i - j, base, row, column, after[rows, :], before[:, past])
            key, value = kept[past, KD : 2 * KD], kept[past, 2 * KD :]
            weights = (decay * dot_nt(query, key)).astype(low)
            grad_scores = (dot_nt(grad_rows, value) * decay).astype(low)
            held = held + dot(grad_scores, key)
            key_term, value_term = dot_tn(grad_scores, query), dot_tn(weights, grad_rows)
            if i == j:
                grad_k[past, :], grad_v[past, :] = key_term, value_term
            else:
                grad_k[past, :] += key_term
                grad_v[past, :] += value_term
        grad_q[rows, :] = held
    cos, sin = cosine[...], sine[...]
    for first, source, factor in ((0, grad_q, KD ** (-0.5)), (KD, grad_k, 1.0)):
        a, b = source[:, :half] * factor, source[:, half:] * factor
        out[:, first : first + half] = (a * cos + b * sin).astype(low)
        out[:, first + half : first + KD] = (b * cos - a * sin).astype(low)
    out[:, 2 * KD : 2 * KD + VD] = grad_v[...].astype(low)


def retain_back(grad, pre, kept, grouped, scale, consts, heads):
    total = pre.shape[0]
    powers, logs, cosine, sine, after, before = consts
    whole = lambda a: pl.BlockSpec(a.shape, lambda h: (0, 0))
    smem = pl.BlockSpec(memory_space=pltpu.SMEM)
    by_head = lambda width: pl.BlockSpec((total, width), lambda h: (0, h))
    return call(
        retain_back_kernel,
        (heads,),
        [smem, smem, by_head(VD), pl.BlockSpec((total, VD), lambda h: (0, 3 * h + 2))]
        + [by_head(2 * KD + VD), by_head(VD), by_head(128)]
        + [whole(cosine), whole(sine), whole(after), whole(before)],
        by_head(2 * KD + 2 * VD),
        jax.ShapeDtypeStruct((total, heads * (2 * KD + 2 * VD)), low),
        56,
        scratch=[
            pltpu.VMEM((total, VD), low),
            pltpu.VMEM((total, KD), f32),
            pltpu.VMEM((total, KD), f32),
            pltpu.VMEM((total, VD), f32),
        ],
    )(*consts[:2], grad, pre, kept, grouped, scale, *consts[2:])


def feed_kernel(feeds, steps, *refs):
    given, weights = refs[:4], refs[4 : 4 + 4 * feeds]
    outs = refs[4 + 4 * feeds : 4 + 7 * feeds]
    own, sent = refs[4 + 7 * feeds : 6 + 7 * feeds]
    rows, cots, held, grads, total, row_sems, sems = refs[6 + 7 * feeds :]
    count, width = rows.shape
    depth, size = width // 4, held.shape[2] // 3
    step = pl.program_id(0)

    def row_copies():
        places = [(buffer, first) for buffer in (rows, cots) for first in (0, count // 2)]
        return [
            pltpu.make_async_copy(ref, buffer.at[pl.ds(first, count // 2)], row_sems.at[i])
            for i, (ref, (buffer, first)) in enumerate(zip(given, places))
        ]

    def weight_copies(number, tile, slot):
        columns = weights[0].shape[1] // 3
        return [
            pltpu.make_async_copy(
                weights[4 * number + part].at[:, pl.ds(pl.multiple_of(kind * columns + tile * size, size), size)],
                held.at[slot, pl.ds(part * depth, depth), pl.ds(kind * size, size)],
                sems.at[slot, 4 * kind + part],
            )
            for kind in range(3)
            for part in range(4)
        ]

    def for_step(at, act):
        for number in range(feeds):

            @pl.when((at >= number * steps) & (at < (number + 1) * steps))
            def _(number=number):
                for copy in weight_copies(number, at - number * steps, lax.rem(at, 2)):
                    act(copy)

    @pl.when(step == 0)
    def _():
        for copy in row_copies():
            copy.start()
        for_step(step, lambda copy: copy.start())

    for_step(step + 1, lambda copy: copy.start())

    @pl.when(step == 0)
    def _():
        for copy in row_copies():
            copy.wait()

    for_step(step, lambda copy: copy.wait())
    weight = held.at[lax.rem(step, 2)]
    up = weight[:, : 2 * size]
    both, grad_hidden = dot(rows[...], up), dot(cots[...], weight[:, 2 * size :])
    act, lin = both[:, :size], both[:, size:]
    curve = jnp.tanh(gelu_slope * (act + gelu_cubic * act * act * act))
    gelu = 0.5 * act * (1.0 + curve)
    slope = 0.5 * (1.0 + curve) + (0.5 * gelu_slope) * act * (1.0 - curve * curve) * (
        1.0 + (3.0 * gelu_cubic) * act * act
    )
    hidden = (gelu * lin).astype(low)
    grads[:, :size] = (grad_hidden * lin * slope).astype(low)
    grads[:, size:] = (grad_hidden * gelu).astype(low)
    for number in range(feeds):

        @pl.when((step >= number * steps) & (step < (number + 1) * steps))
        def _(number=number):
            outs[3 * number][...] = hidden
            outs[3 * number + 1][...] = grads[:, :size]
            outs[3 * number + 2][...] = grads[:, size:]

    add = dot_nt(grads[...], up)

    @pl.when(step == 0)
    def _():
        total[...] = add

    @pl.when(step != 0)
    def _():
        total[...] += add

    @pl.when(step == pl.num_programs(0) - 1)
    def _():
        own[...] = total[: count // 2, :]
        sent[...] = total[count // 2 :, :].astype(low)


def feed(rows, cots, feeds):
    count, width = rows[0].shape
    columns = feeds[0][0].shape[1] // 3
    size = min(512, columns)
    steps, number = columns // size, len(feeds)
    full = pl.BlockSpec((count, width), lambda t: (0, 0))
    anywhere = pl.BlockSpec(memory_space=pl.ANY)
    tiles = [
        pl.BlockSpec((2 * count, size), lambda t, k=k: (0, jnp.clip(t - k * steps, 0, steps - 1)))
        for k in range(number)
    ]
    shape = jax.ShapeDtypeStruct((2 * count, columns), low)
    outs = call(
        functools.partial(feed_kernel, number, steps),
        (number * steps,),
        [anywhere] * (4 + 4 * number),
        [tile for tile in tiles for _ in range(3)] + [full, full],
        [shape] * (3 * number)
        + [jax.ShapeDtypeStruct((count, width), f32), jax.ShapeDtypeStruct((count, width), low)],
        56,
        scratch=[
            pltpu.VMEM((2 * count, width), low),
            pltpu.VMEM((2 * count, width), low),
            pltpu.VMEM((2, width, 3 * size), low),
            pltpu.VMEM((2 * count, 2 * size), low),
            pltpu.VMEM((2 * count, width), f32),
            pltpu.SemaphoreType.DMA((4,)),
            pltpu.SemaphoreType.DMA((2, 12)),
        ],
    )(*rows, *cots, *[part for weight in feeds for part in weight])
    return [outs[3 * k : 3 * k + 3] for k in range(number)], outs[-2], outs[-1]


def out_kernel(number, *refs):
    hiddens, weights, base = refs[:number], refs[number : 5 * number], refs[5 * number]
    own, sent = refs[5 * number + 1 :]
    half = own.shape[0]

    def give(part):
        total = sum(dot_nt(hiddens[i][...], weights[4 * i + part][...]) for i in range(number))
        own[...] = base[...] + total[:half]
        sent[...] = total[half:].astype(low)

    for part in range(4):
        pl.when(pl.program_id(0) == part)(functools.partial(give, part))


def out_rows(hiddens, feeds, base):
    count, width = base.shape
    columns = hiddens[0].shape[1]
    size = min(256, width // 4)
    steps = width // 4 // size
    tile = pl.BlockSpec((count, size), lambda i, j: (0, i * steps + j))
    return call(
        functools.partial(out_kernel, len(hiddens)),
        (4, steps),
        [pl.BlockSpec((2 * count, columns), lambda i, j: (0, 0))] * len(hiddens)
        + part_specs((size, columns), steps, 2) * len(hiddens)
        + [tile],
        [tile, tile],
        [jax.ShapeDtypeStruct((count, width), f32), jax.ShapeDtypeStruct((count, width), low)],
        56,
    )(*hiddens, *[weight for parts in feeds for weight in parts], base)


def gradient_kernel(plan, added, came_steps, places, *refs):
    number = sum(pieces for pieces, _, _ in plan)
    lefts, rights = refs[:number], refs[number : number + sum(len(r) for _, r, _ in plan)]
    rest = refs[number + len(rights) :]
    came, outs, turned = rest[:added], rest[added:-1], rest[-1]
    step = pl.program_id(0)
    first = left_at = right_at = 0
    for pieces, lengths, size in plan:

        @pl.when(step == first)
        def _(left_at=left_at, pieces=pieces, size=size):
            for i in range(left_at, left_at + pieces):
                start = pl.multiple_of(places[i] * size, size) if pieces > 1 else 0
                turned[:, pl.ds(start, size)] = lefts[i][...].T

        for length in lengths:

            @pl.when((step >= first) & (step < first + length))
            def _(right=rights[right_at], depth=pieces * size):
                result = dot(turned[:, :depth], right[...])
                if added:
                    result = result + jnp.where(step < came_steps, came[0][...].astype(f32), 0.0)
                height = result.shape[0] // len(outs)
                for i, out in enumerate(outs):
                    out[...] = result[i * height : (i + 1) * height].astype(low)

            first, right_at = first + length, right_at + 1
        left_at += pieces


def weight_gradient(groups, side, came=None, pieces_out=4):
    width = groups[0][0][0].shape[1]
    half = width // 2
    count = max(pieces[0].shape[0] * len(pieces) for pieces, _, _ in groups)
    columns = sum(right.shape[1] for _, _, rights in groups for right in rights)
    size = min(512, min(right.shape[1] for _, _, rights in groups for right in rights))
    plan, lefts, rights, left_specs, right_specs, places, first = [], [], [], [], [], [], 0
    for pieces, at, given in groups:
        plan.append((len(pieces), [right.shape[1] // size for right in given], pieces[0].shape[0]))
        lefts += pieces
        places += at
        whole = pieces[0].shape[1] == width
        spec = pl.BlockSpec((pieces[0].shape[0], half), lambda t, _, whole=whole: (0, side if whole else 0))
        left_specs += [spec] * len(pieces)
        for right in given:
            steps = right.shape[1] // size
            right_specs.append(
                pl.BlockSpec(
                    (right.shape[0], size),
                    lambda t, _, first=first, steps=steps: (0, jnp.clip(t - first, 0, steps - 1)),
                )
            )
            rights.append(right)
            first += steps
    parts = 1 if came is None else pieces_out
    tile = lambda height: pl.BlockSpec((height, size), lambda t, _: (0, t))
    more = [] if came is None else [came]
    came_steps = 0 if came is None else came.shape[1] // size
    came_specs = [pl.BlockSpec((half, size), lambda t, _: (0, jnp.minimum(t, came_steps - 1)))] * len(more)
    outs = call(
        functools.partial(gradient_kernel, plan, len(more), came_steps),
        (columns // size,),
        left_specs + right_specs + came_specs,
        [tile(half // parts)] * parts,
        [jax.ShapeDtypeStruct((half // parts, columns), low)] * parts,
        56,
        scratch=[pltpu.VMEM((half, count), low)],
        scalars=1,
    )(jnp.stack(places), *lefts, *rights, *more)
    return outs[0] if came is None else [outs[: parts // 2], outs[parts // 2 :]]


def shards(
    inputs,
    gain_attn,
    w_query,
    w_key,
    w_value,
    w_gate,
    w_out,
    gain_mlp,
    w_act,
    w_lin,
    w_down,
    cotangent,
    lengths,
    offsets,
):
    rows, width = inputs.shape
    dp_size, tensor_size = lax.axis_size("dp"), lax.axis_size("tensor")
    dp_own, tensor_own = lax.axis_index("dp"), lax.axis_index("tensor")
    total = rows * tensor_size
    heads = w_query.shape[1] // KD
    hidden_cols = w_act.shape[1]
    half = width // 2

    order = feature_order(dp_size)
    taken = jnp.array([k for k, _ in order], jnp.int32)
    parts = jnp.array([i for _, i in order], jnp.int32)
    table = (taken ^ dp_own) * 2 + parts
    place = {pair: i for i, pair in enumerate(order)}
    places = jnp.array([[place[k, i] for i in range(2)] for k in range(dp_size)], jnp.int32)
    back = places[jnp.arange(dp_size, dtype=jnp.int32) ^ dp_own].reshape(-1)

    x_low = reorder(inputs, table)
    normed_one = normed_rows(x_low)
    stride = 2 * KD + 2 * VD
    head_blocks = []
    for h in range(heads):
        head_blocks += [(w_query, h * KD, KD), (w_key, h * KD, KD)]
        head_blocks += [(w_value, h * VD, VD), (w_gate, h * VD, VD)]
    pair_blocks = range(0, tensor_size, 2)

    head_first = tensor_own * heads
    head_numbers = (head_first + jnp.arange(heads, dtype=jnp.int32)).astype(f32)
    log_decay = jnp.log(1.0 - jnp.exp2(-5.0 - head_numbers))
    segment, position = sequence_layout(lengths[0], offsets[0], total)
    cosine, sine = rotation(position, KD)
    powers = jnp.exp(
        jnp.arange(total // TILE, dtype=f32)[None, :] * TILE * log_decay[:, None]
    )
    consts = (powers, log_decay, cosine, sine, segment[:, None], segment[None, :])
    ring_places = [(tensor_own - step) % tensor_size for step in range(tensor_size)]

    gains = jnp.concatenate([gain_attn.reshape(2, -1), gain_mlp.reshape(2, -1)], axis=1)
    parts = [gains[:1], gains[1:]]
    for bits in dp_bits(dp_size):
        parts = [
            jnp.concatenate([part, swap(part, "dp", bit, "gains")], axis=0)
            for part, bit in zip(sync(*parts), bits)
        ]
    gains_same = jnp.concatenate(parts, axis=0)
    gains = jnp.concatenate([gains_same, swap(gains_same, "dp", 1, "gains")], axis=0).astype(f32)
    fine = gains.shape[1] // 2
    gain_one, gain_two = gains[:, :fine].reshape(-1), gains[:, fine:].reshape(-1)

    w_in = gather_step(column_blocks(head_blocks), 0, "w_in")
    late_act, late_lin, late_down, late_out, late_cot = tie(
        (w_act, w_lin, w_down, w_out, cotangent), normed_one
    )
    feed_parts = column_blocks(
        [(late_act, 0, hidden_cols), (late_lin, 0, hidden_cols), (late_down.T, 0, hidden_cols)]
    )
    wo = column_blocks([(late_out.T, 0, w_out.shape[0])])
    cot = reorder(late_cot, table)

    def beside_attn(step, came):
        nonlocal w_in, wo, cot, feed_parts, consts
        if step == 1:
            came, w_in, wo, cot, feed_parts, consts = sync(came, w_in, wo, cot, feed_parts, consts)
            w_in = gather_rest(w_in, 1, "w_in", consts)
            wo = gather_step(tie(wo, w_in), 0, "w_out")
        return came

    pieces = gather_ring(normed_one, "rows_attn", beside_attn)
    rows_here, w_in, wo, feed_parts, gain_one, gain_two = sync(
        pieces[-1], w_in, wo, feed_parts, gain_one, gain_two
    )
    pieces[-1] = rows_here

    def swap_far(part):
        return {k: swap(part, "tensor", k, "w_feed_far") for k in pair_blocks[1:]}

    cot_came = swap(tie(cotangent, rows_here), "tensor", 1, "rows_cot")
    upper = swap_far(feed_parts[0])
    w_in = gather_core(w_in, "w_in")
    h_pieces = [scale_rows(piece, gain_one) for piece in pieces]
    pre = project(h_pieces[:-1], w_in, None, ring_places[:-1], tensor_size)
    wo = gather_rest(wo, 1, "w_out", pre)
    pre, cot_came, upper, wo, feed_parts = sync(pre, cot_came, upper, wo, feed_parts)
    wo = gather_core(wo, "w_out")

    lower = swap_far(tie(feed_parts[1], upper))
    pre = project(h_pieces[-1:], w_in, pre, ring_places[-1:], tensor_size)
    mixed, kept, grouped, scale = retain(pre, consts, heads)
    near_feed = gather_step(feed_parts, 0, "w_feed_near", mixed)
    near_feed = gather_rest(near_feed, 1, "w_feed_near")
    sum_places = scatter_places()
    (total_out,) = terms(mixed, wo, sum_places[:1], rows, [low], None)
    rest_out = terms(tie(mixed, total_out), wo, sum_places[1:], rows, [f32] * (tensor_size - 1), None)
    cots = [cot, reorder(tie(cot_came, total_out), table)]
    total_out, lower, cots = sync(total_out, lower, cots)
    far_feeds = {k: gather_step([upper[k], lower[k]], 0, "w_feed_far") for k in upper}

    def beside_out(step, total):
        nonlocal far_feeds, near_feed
        if step == 1:
            total, far_feeds = sync(total, far_feeds)
            far_feeds = {k: gather_rest(v, 1, "w_feed_far") for k, v in far_feeds.items()}
        if step == 2:
            total, near_feed = sync(total, near_feed)
            near_feed = gather_core(near_feed, "w_feed_near")
        if step == tensor_size - 1:
            total, far_feeds = sync(total, far_feeds)
            far_feeds = {k: gather_core(v, "w_feed_far") for k, v in far_feeds.items()}
        return total

    attn_came, attn_own = scatter_ring(total_out, rest_out, "sum_attn", beside_out)

    middle, h_mlp = norm_rows(x_low, attn_came, attn_own, gain_two)
    h_came = swap(h_mlp, "tensor", 1, "rows_mlp")
    feeds = [near_feed] + [far_feeds[k] for k in pair_blocks[1:]]
    h_pair = [h_mlp, h_came]
    results, grad_h, grad_send = feed(h_pair, cots, feeds)
    grad_came = swap(grad_send, "tensor", 1, "sum_grad_mlp")

    late, late_rows, late_cots = tie((results, h_pair, cots), grad_send)
    pair_places = [jnp.zeros((), jnp.int32), jnp.ones((), jnp.int32)]

    def feed_groups(result):
        hidden, grad_act, grad_lin = result
        return [
            (late_rows, pair_places, [grad_act, grad_lin]),
            (late_cots, pair_places, [hidden]),
        ]

    far = {k: weight_gradient(feed_groups(late[k // 2]), 1) for k in pair_blocks[1:]}
    near_other = weight_gradient(feed_groups(late[0]), 1)
    grad_came, far, near_other = sync(grad_came, far, near_other)
    far_came = {k: swap(other, "dp", 1, "grad_feed_far") for k, other in far.items()}
    near_came = None
    grad_middle, gain_two_term, grad_mid_low = norm_back_rows(
        middle, cot, gain_two, grad_h, grad_came, True
    )

    grad_mixed = out_own = out_send = None
    mid_pieces = [grad_mid_low]

    def beside_mid(step, came):
        nonlocal far, near_came, grad_mixed, out_own, out_send
        if step == 1:
            late = tie(results, grad_mid_low)
            far = {
                k: weight_gradient(feed_groups(late[k // 2]), 0, far_came[k])
                for k in pair_blocks[1:]
            }
            came, far, near_last = sync(came, far, near_other)
            near_came = swap(near_last, "dp", 1, "grad_feed_near")
            far = {k: scatter_step(v, 0, "grad_feed_far") for k, v in far.items()}
        if step == 2:
            late, weights = tie((results, feeds), mid_pieces[1])
            out_own, out_send = out_rows([result[0] for result in late], weights, middle)
            near_came = weight_gradient(feed_groups(late[0]), 0, near_came)
            came, out_own, out_send, near_came = sync(came, out_own, out_send, near_came)
        if step == tensor_size - 1:
            late = tie(mid_pieces, mid_pieces[-1])
            grad_mixed = project(late, wo, None, ring_places[:step], tensor_size)
            came, far, grad_mixed = sync(came, far, grad_mixed)
        mid_pieces.append(came)
        return came

    mid_pieces = gather_ring(grad_mid_low, "rows_grad_mid", beside_mid)
    out_came = swap(tie(out_send, mid_pieces[-1]), "tensor", 1, "sum_out")
    far = {k: scatter_rest(v, 1, "grad_feed_far") for k, v in far.items()}

    grad_mixed = project(mid_pieces[-1:], wo, grad_mixed, ring_places[-1:], tensor_size)
    grad_in = retain_back(grad_mixed, pre, kept, grouped, scale, consts, heads)

    grad_in, out_came, far, near = sync(grad_in, out_came, far, near_came)
    near = scatter_step(near, 0, "grad_feed_near")
    upper = {k: join(*parts[:2]) for k, parts in far.items()}
    lower = {k: join(*parts[2:]) for k, parts in far.items()}
    gain_places = [jnp.zeros((), jnp.int32)]
    gain_columns = jnp.eye(16, TILE, dtype=low)

    def out_groups(right):
        return [(mid_pieces, ring_places, [right])]

    def swap_grad(parts):
        return {k: swap(part, "tensor", k, "grad_feed_far") for k, part in parts.items()}

    upper, lower_sent = swap_grad(upper), lower
    first_pairs, rest_pairs = h_pieces[1:2], h_pieces[2:] + h_pieces[:1]
    total_in, more = terms(grad_in, w_in, sum_places[:1], rows, [low], first_pairs)
    late_in = tie(grad_in, total_in)
    in_other = weight_gradient([(h_pieces, ring_places, [late_in])], 1)
    out_other = weight_gradient(out_groups(tie(mixed, in_other)), 1)
    total_in, upper, in_other, out_other, near, lower_sent = sync(
        total_in, upper, in_other, out_other, near, lower_sent
    )
    lower = swap_grad(lower_sent)
    in_other = swap(in_other, "dp", 1, "grad_w_in")
    out_other = swap(out_other, "dp", 1, "grad_w_out")
    *rest_in, more_rest = terms(
        tie(grad_in, total_in), w_in, sum_places[1:], rows, [f32] * (tensor_size - 1), rest_pairs
    )
    late_in = tie(grad_in, more_rest)
    grads_in = weight_gradient([(h_pieces, ring_places, [late_in])], 0, in_other, 8)
    near = scatter_step(near, 1, "grad_feed_near", grads_in)
    total_in, lower, rest_in, grads_in, near, out_other = sync(
        total_in, lower, rest_in, grads_in, near, out_other
    )
    first_bits = dp_bits(dp_size)[-1]
    sent_on = [
        swap(part[3], "dp", bit, "grad_w_in") for part, bit in zip(grads_in, first_bits)
    ]
    gain_rows = jnp.concatenate([(more + more_rest) / gain_one, gain_two_term], axis=0)
    gain_rows = gain_rows[:, :half] + swap(gain_rows[:, half:], "dp", 1, "gains")
    gain_rows = jnp.concatenate([gain_rows, jnp.zeros((14, half), f32)], axis=0).astype(low)
    grads_out = weight_gradient(
        out_groups(tie(mixed, total_in)) + [([gain_rows], gain_places, [gain_columns])], 0, out_other
    )
    out_sent = scatter_send(grads_out, 0, "grad_w_out")

    def beside_sum(step, total):
        nonlocal grads_in, grads_out, sent_on
        if step == 1:
            total, sent_on, grads_out = sync(total, sent_on, grads_out)
            kept_on = [
                swap(part[2], "dp", bit, "grad_w_in") for part, bit in zip(grads_in, first_bits)
            ]
            grads_in, sent_on = tie((grads_in, sent_on), total)
            sent_on = [
                add_rows(part[1], came, low) for part, came in zip(grads_in, sent_on)
            ]
            grads_in = [
                [add_rows(part[0], came, low), sent]
                for part, came, sent in zip(grads_in, kept_on, sent_on)
            ]
            grads_out = scatter_add(grads_out, tie(out_sent, total))
        return total

    hattn_came, hattn_own = scatter_ring(total_in, rest_in, "sum_grad_attn", beside_sum)
    (grad_inputs,) = norm_back_rows(x_low, grad_middle, gain_one, hattn_own, hattn_came, False)
    grad_inputs = reorder(grad_inputs, back)
    grads_out = scatter_rest(grads_out, 1, "grad_w_out")
    grads_in = scatter_rest(tie(grads_in, grads_out), 1, "grad_w_in", grad_inputs)
    near = scatter_rest(near, 2, "grad_feed_near")
    grad_out_own = jnp.concatenate(grads_out, axis=0).astype(f32)
    columns = w_out.shape[0]
    grad_wo_own, gain_sum = grad_out_own[:, :columns], grad_out_own[:, columns : columns + 2].T
    gain_came = [swap(gain_sum, "tensor", k, "gains") for k in range(1, tensor_size)]
    gain_sums = [gain_sum] + tie(gain_came, grad_inputs)
    while len(gain_sums) > 1:
        gain_sums = [a + b for a, b in zip(gain_sums[::2], gain_sums[1::2])]
    gain_sum = gain_sums[0]
    grad_in_own = jnp.concatenate(grads_in, axis=0).astype(f32)
    grad_feed = jnp.concatenate(near, axis=0).astype(f32)
    for k in pair_blocks[1:]:
        grad_feed = grad_feed + jnp.concatenate([upper[k], lower[k]], axis=0).astype(f32)
    outputs = out_own + out_came.astype(f32)

    def heads_back(first, size):
        return jnp.concatenate(
            [grad_in_own[:, h * stride + first : h * stride + first + size] for h in range(heads)],
            axis=1,
        )

    return (
        reorder(outputs.astype(low), back),
        grad_inputs,
        gain_sum[0],
        heads_back(0, KD),
        heads_back(KD, KD),
        heads_back(2 * KD, VD),
        heads_back(2 * KD + VD, VD),
        grad_wo_own.T,
        gain_sum[1],
        grad_feed[:, :hidden_cols],
        grad_feed[:, hidden_cols : 2 * hidden_cols],
        grad_feed[:, 2 * hidden_cols :].T,
    )


def solution(mesh):
    return jax.shard_map(
        shards,
        mesh=mesh,
        in_specs=(
            P(("dp", "tensor"), None),
            P("dp"),
            P("dp", "tensor"),
            P("dp", "tensor"),
            P("dp", "tensor"),
            P("dp", "tensor"),
            P("tensor", "dp"),
            P("dp"),
            P("dp", "tensor"),
            P("dp", "tensor"),
            P("tensor", "dp"),
            P(("dp", "tensor"), None),
            P("dp", None),
            P("dp", None),
        ),
        out_specs=(
            P(("dp", "tensor"), None),
            P(("dp", "tensor"), None),
            P("dp"),
            P("dp", "tensor"),
            P("dp", "tensor"),
            P("dp", "tensor"),
            P("dp", "tensor"),
            P("tensor", "dp"),
            P("dp"),
            P("dp", "tensor"),
            P("dp", "tensor"),
            P("tensor", "dp"),
        ),
        check_vma=False,
    )
```

```python
import functools
import math

import jax
import jax.numpy as jnp
from jax import lax
from jax.experimental import pallas as pl
from jax.experimental.pallas import tpu as pltpu
from jax.sharding import PartitionSpec as P

KD = 256
VD = 512
TILE = 256

epsilon = 1e-05
group_floor = 1.0
f32 = jnp.float32
low = jnp.bfloat16
gelu_slope = math.sqrt(2.0 / math.pi)
gelu_cubic = 0.044715


def layer_norm(values, floor_value=epsilon):
    center = values - jnp.mean(values, axis=-1, keepdims=True)
    scale_inv = lax.rsqrt(jnp.mean(center * center, axis=-1, keepdims=True) + floor_value)
    return (center * scale_inv, scale_inv)


def norm_back(grad_norm, normed, scale_inv):
    mean_grad = jnp.mean(grad_norm, axis=-1, keepdims=True)
    mean_cross = jnp.mean(grad_norm * normed, axis=-1, keepdims=True)
    return (grad_norm - mean_grad - normed * mean_cross) * scale_inv


def sequence_layout(lengths, offsets, total):
    places = jnp.arange(total, dtype=jnp.int32)[:, None]
    inside = (places >= offsets[None, :]) & (places < offsets[None, :] + lengths[None, :])
    numbers = jnp.arange(1, offsets.shape[0] + 1, dtype=jnp.int32)
    segment = jnp.sum(jnp.where(inside, numbers[None, :], 0), axis=1) - 1
    position = places[:, 0] - jnp.sum(jnp.where(inside, offsets[None, :], 0), axis=1)
    return (segment, position.astype(f32))


def rotation(position, size):
    half = size // 2
    frequency = jnp.exp(-math.log(10000.0) * jnp.arange(half, dtype=f32) * 2.0 / size)
    angles = position[:, None] * frequency[None, :]
    return (jnp.cos(angles), jnp.sin(angles))


def dot(left, right):
    return jnp.dot(left, right, preferred_element_type=f32)


def dot_nt(left, right):
    return lax.dot_general(left, right, (((1,), (1,)), ((), ())), preferred_element_type=f32)


def dot_tn(left, right):
    return lax.dot_general(left, right, (((0,), (0,)), ((), ())), preferred_element_type=f32)


def swap(values, axis, bits, name="swap"):
    size = lax.axis_size(axis)
    with jax.named_scope(f"{name}_{axis}{bits}"):
        return lax.ppermute(values, axis, [(i, i ^ bits) for i in range(size)])


def shift(values, axis, step, name="shift"):
    size = lax.axis_size(axis)
    with jax.named_scope(name):
        return lax.ppermute(values, axis, [(i, (i + step) % size) for i in range(size)])


def tie(values, token):
    return values if token is None else lax.optimization_barrier((values, token))[0]


def dp_bits(size):
    bits = [1 << b for b in range(1, size.bit_length() - 1)]
    return list(zip(bits, bits[1:] + bits[:1]))


def feature_order(size):
    same = []
    for half in (0, 1):
        held = [0]
        for bits in dp_bits(size):
            held += [k ^ bits[half] for k in held]
        same += [(k, half) for k in held]
    return same + [(k ^ 1, half) for k, half in same]


def gather_step(parts, stage, name, after=None):
    bits = dp_bits(lax.axis_size("dp"))[stage]
    parts = sync(*parts)
    came = tie([swap(part, "dp", bit, name) for part, bit in zip(parts, bits)], after)
    return [join(*pair) for pair in zip(parts, came)]


def gather_rest(parts, stage, name, after=None):
    for step in range(stage, len(dp_bits(lax.axis_size("dp")))):
        parts = gather_step(parts, step, name, after)
    return parts


def gather_core(parts, name):
    return [*parts, *(swap(part, "dp", 1, name) for part in sync(*parts))]


def scatter_send(parts, stage, name):
    bits = dp_bits(lax.axis_size("dp"))[-1 - stage]
    return [swap(sent, "dp", bit, name) for (_, sent), bit in zip(sync(*parts), bits)]


def scatter_add(parts, came):
    return [add_split(kept, part) for (kept, _), part in zip(parts, came)]


def scatter_step(parts, stage, name, after=None):
    return scatter_add(parts, tie(scatter_send(parts, stage, name), after))


def scatter_rest(parts, stage, name, after=None):
    for step in range(stage, len(dp_bits(lax.axis_size("dp")))):
        parts = scatter_step(parts, step, name, after)
    return [half for part in parts for half in part]


def sync(*values):
    return lax.optimization_barrier(values)


def gather_ring(rows, name, beside):
    pieces = [rows]
    for step in range(1, lax.axis_size("tensor")):
        came = shift(pieces[-1], "tensor", 1, f"{name}_{step}")
        pieces.append(beside(step, came))
    return pieces


def call(kernel, grid, in_specs, out_specs, out_shape, vmem=32, scratch=(), scalars=0, aliases=None):
    return pl.pallas_call(
        kernel,
        grid_spec=pltpu.PrefetchScalarGridSpec(
            num_scalar_prefetch=scalars,
            grid=grid,
            in_specs=in_specs,
            out_specs=out_specs,
            scratch_shapes=scratch,
        ),
        out_shape=out_shape,
        input_output_aliases=aliases or {},
        compiler_params=pltpu.CompilerParams(
            dimension_semantics=("arbitrary",) * len(grid), vmem_limit_bytes=vmem * 1024 * 1024
        ),
        cost_estimate=pl.CostEstimate(flops=0, bytes_accessed=0, transcendentals=0),
    )


def join_kernel(steps, *refs):
    step, first = pl.program_id(0), 0
    for ref, length in zip(refs[:-1], steps):

        @pl.when((step >= first) & (step < first + length))
        def _(ref=ref):
            refs[-1][...] = ref[...]

        first += length


def join(*parts):
    columns = parts[0].shape[1]
    height = min(min(part.shape[0] for part in parts), 256)
    steps, specs, first = [], [], 0
    for part in parts:
        length = part.shape[0] // height
        specs.append(
            pl.BlockSpec(
                (height, columns),
                lambda t, first=first, length=length: (jnp.clip(t - first, 0, length - 1), 0),
            )
        )
        steps.append(length)
        first += length
    return call(
        functools.partial(join_kernel, steps),
        (first,),
        specs,
        pl.BlockSpec((height, columns), lambda t: (t, 0)),
        jax.ShapeDtypeStruct((first * height, columns), parts[0].dtype),
        32,
    )(*parts)


def column_blocks_kernel(places, *refs):
    for ref, (column, first, size) in zip(refs[:-2], places):
        half = ref.shape[0] // 2
        refs[-2][:, first : first + size] = ref[:half, column : column + size]
        refs[-1][:, first : first + size] = ref[half:, column : column + size]


def column_blocks(sources):
    height = sources[0][0].shape[0]
    places, specs, first = [], [], 0
    for array, column, size in sources:
        places.append((column, first, size))
        specs.append(pl.BlockSpec(array.shape, lambda t: (0, 0)))
        first += size
    half = pl.BlockSpec((height // 2, first), lambda t: (0, 0))
    shape = jax.ShapeDtypeStruct((height // 2, first), sources[0][0].dtype)
    return call(
        functools.partial(column_blocks_kernel, places), (1,), specs, [half, half], [shape, shape]
    )(*[array for array, _, _ in sources])


def add_split_kernel(left, right, upper, lower):
    half = upper.shape[0]
    for i, out in enumerate((upper, lower)):
        rows = slice(i * half, (i + 1) * half)
        out[...] = (left[rows, :].astype(f32) + right[rows, :].astype(f32)).astype(low)


def add_split(left, right):
    count, columns = left.shape
    size = columns // 2 if columns % 256 == 0 else columns
    whole = pl.BlockSpec((count, size), lambda t: (0, t))
    half = pl.BlockSpec((count // 2, size), lambda t: (0, t))
    return call(
        add_split_kernel,
        (columns // size,),
        [whole, whole],
        [half, half],
        [jax.ShapeDtypeStruct((count // 2, columns), low)] * 2,
        32,
    )(left, right)


def add_kernel(left, right, out):
    out[...] = (left[...].astype(f32) + right[...].astype(f32)).astype(out.dtype)


def add_rows(left, right, kind):
    count, width = left.shape
    rows = pl.BlockSpec((count // 2, width), lambda i: (i, 0))
    shape = jax.ShapeDtypeStruct((count, width), kind)
    return call(add_kernel, (2,), [rows, rows], rows, shape)(left, right)


def scale_kernel(rows, gain, out):
    out[...] = (rows[...].astype(f32) * gain[...]).astype(low)


def scale_rows(values, gain):
    count, width = values.shape
    rows = pl.BlockSpec((count // 2, width), lambda i: (i, 0))
    line = pl.BlockSpec((1, width), lambda i: (0, 0))
    shape = jax.ShapeDtypeStruct((count, width), low)
    return call(scale_kernel, (2,), [rows, line], rows, shape)(values, gain[None])


def normed_kernel(values, out):
    out[...] = layer_norm(values[...].astype(f32))[0].astype(low)


def normed_rows(values):
    count, width = values.shape
    rows = pl.BlockSpec((count // 2, width), lambda i: (i, 0))
    shape = jax.ShapeDtypeStruct((count, width), low)
    return call(normed_kernel, (2,), [rows], rows, shape)(values)


def reorder_kernel(table, values, out):
    count = table.shape[0]
    width = values.shape[1] // count
    for place in range(count):
        start = pl.multiple_of(table[place] * width, width)
        out[:, place * width : (place + 1) * width] = values[:, pl.ds(start, width)]


def reorder(values, table):
    count, (rows, width) = table.shape[0], values.shape
    size = width // count
    if size % 128:
        blocks = [
            lax.dynamic_slice_in_dim(values, table[i] * size, size, axis=1) for i in range(count)
        ]
        return jnp.concatenate(blocks, axis=1)
    part = min(rows, 64)
    spec = pl.BlockSpec((part, width), lambda i, _: (i, 0))
    return call(
        reorder_kernel,
        (rows // part,),
        [spec],
        spec,
        jax.ShapeDtypeStruct(values.shape, values.dtype),
        32,
        scalars=1,
    )(table, values)


def project_kernel(count, places, *refs):
    weights, out = refs[count : count + 4], refs[-1]
    depth = weights[0].shape[0]
    for i in range(count):
        rows = refs[i]
        size = rows.shape[0]
        start = pl.multiple_of(places[i] * size, size) if out.shape[0] > size else 0
        out[pl.ds(start, size), :] = sum(
            dot(rows[:, q * depth : (q + 1) * depth], weights[q][...]) for q in range(4)
        )


def project(pieces, weight, whole, places, chunks):
    (count, width), columns = pieces[0].shape, weight[0].shape[1]
    size = 512 if columns % 512 == 0 else TILE
    spec = pl.BlockSpec((width // 4, size), lambda j, _: (0, j))
    rows = pl.BlockSpec((count, width), lambda j, _: (0, 0))
    number = len(pieces)
    if whole is None:
        held, out = [], pl.BlockSpec((count * chunks, size), lambda j, _: (0, j))
    else:
        held, out = [whole], pl.BlockSpec((count, size), lambda j, at: (at[0], j))
    return call(
        functools.partial(project_kernel, number),
        (columns // size,),
        [rows] * number + [spec] * 4 + [pl.BlockSpec(memory_space=pl.ANY)] * len(held),
        out,
        jax.ShapeDtypeStruct((count * chunks, columns), f32),
        56,
        scalars=1,
        aliases={number + 5: 0} if held else None,
    )(jnp.stack(places), *pieces, *weight, *held)


def part_specs(shape, steps, column):
    def spec(part):
        def index(i, j, *_):
            return (jnp.where(i == part, j, jnp.where(i < part, 0, steps - 1)), column)

        return pl.BlockSpec(shape, index)

    return [spec(part) for part in range(4)]


def terms_kernel(count, paired, places, *refs):
    weights, outs = refs[count : count + 4], refs[count + 4 :]
    pairs, outs = outs[: count * paired], outs[count * paired :]

    def give(weight):
        sums = 0.0
        for i, rows in enumerate(refs[:count]):
            result = dot_nt(rows[...], weight[...])
            outs[i][...] = result.astype(outs[i].dtype)
            if paired:
                sums = sums + jnp.sum(result * pairs[i][...].astype(f32), axis=0, keepdims=True)
        if paired:
            outs[count][...] = sums

    for part, weight in enumerate(weights):
        pl.when(pl.program_id(0) == part)(functools.partial(give, weight))


def terms(whole, weight, places, size, kinds, pairs):
    quarter, depth = weight[0].shape
    tile = min(quarter, 512 if depth <= 1024 else 256)
    steps = quarter // tile
    number = len(places)
    rows = [
        pl.BlockSpec((size, depth), lambda i, j, at, n=n: (at[n], 0)) for n in range(number)
    ]
    out = lambda height: pl.BlockSpec((height, tile), lambda i, j, _: (0, i * steps + j))
    paired = 1 if pairs else 0
    return call(
        functools.partial(terms_kernel, number, paired),
        (4, steps),
        rows + part_specs((tile, depth), steps, 0) + [out(size)] * (number * paired),
        [out(size)] * number + [out(1)] * paired,
        [jax.ShapeDtypeStruct((size, 4 * quarter), kind) for kind in kinds]
        + [jax.ShapeDtypeStruct((1, 4 * quarter), f32)] * paired,
        56,
        scalars=1,
    )(jnp.stack(places), *([whole] * number), *weight, *(pairs or []))


def scatter_places():
    own, size = lax.axis_index("tensor"), lax.axis_size("tensor")
    return [(own - step) % size for step in range(1, size + 1)]


def scatter_ring(total, rest, name, beside):
    for step, own in enumerate(rest, 1):
        came = shift(total, "tensor", 1, f"{name}_{step}")
        if step == len(rest):
            return beside(step, came), own
        total = beside(step, add_rows(came, own, low))


def norm_kernel(values, came, added, gain, middle, out):
    rows = values[...].astype(f32) + (came[...].astype(f32) + added[...])
    middle[...] = rows
    out[...] = (layer_norm(rows)[0] * gain[...]).astype(low)


def norm_rows(values, came, added, gain):
    count, width = values.shape
    size = min(count, 128)
    rows = pl.BlockSpec((size, width), lambda i: (i, 0))
    return call(
        norm_kernel,
        (count // size,),
        [rows, rows, rows, pl.BlockSpec((1, width), lambda i: (0, 0))],
        [rows, rows],
        [jax.ShapeDtypeStruct((count, width), f32), jax.ShapeDtypeStruct((count, width), low)],
        32,
    )(values, came, added, gain[None])


def norm_back_kernel(values, base, gain, grad, came, out, *more):
    given = grad[...] + came[...].astype(f32)
    normed, scale = layer_norm(values[...].astype(f32))
    result = base[...].astype(f32) + norm_back(given * gain[...], normed, scale)
    out[...] = result
    if not more:
        return
    more[1][...] = result.astype(low)
    term = jnp.sum(given * normed, axis=0, keepdims=True)

    @pl.when(pl.program_id(0) == 0)
    def _():
        more[0][...] = term

    @pl.when(pl.program_id(0) != 0)
    def _():
        more[0][...] += term


def norm_back_rows(values, base, gain, grad, came, more):
    count, width = values.shape
    size = min(count, 128)
    rows = pl.BlockSpec((size, width), lambda i: (i, 0))
    line = pl.BlockSpec((1, width), lambda i: (0, 0))
    shape = lambda height, kind: jax.ShapeDtypeStruct((height, width), kind)
    return call(
        norm_back_kernel,
        (count // size,),
        [rows, rows, line, rows, rows],
        [rows] + [line, rows] * more,
        [shape(count, f32)] + [shape(1, f32), shape(count, low)] * more,
        32,
    )(values, base, gain[None], grad, came)


def place_masks(size):
    row = lax.broadcasted_iota(jnp.int32, (size, size), 0)
    column = lax.broadcasted_iota(jnp.int32, (size, size), 1)
    return row, column


def block_decay(powers, head, apart, base, row, column, after, before):
    kept = (after == before) & (after >= 0)
    if apart == 0:
        kept = kept & (column <= row)
        return jnp.where(kept, base, 0.0)
    return jnp.where(kept, base * powers[head, apart], 0.0)


def retain_kernel(powers, logs, pre, cosine, sine, after, before, mixed, kept, grouped, scale):
    head = pl.program_id(0)
    total = pre.shape[0]
    half = KD // 2
    cos, sin = cosine[...], sine[...]
    for first, factor in ((0, KD ** (-0.5)), (KD, 1.0)):
        a, b = pre[:, first : first + half], pre[:, first + half : first + KD]
        kept[:, first : first + half] = ((a * cos - b * sin) * factor).astype(low)
        kept[:, first + half : first + KD] = ((a * sin + b * cos) * factor).astype(low)
    kept[:, 2 * KD :] = pre[:, 2 * KD : 2 * KD + VD].astype(low)
    row, column = place_masks(TILE)
    base = jnp.exp((row - column).astype(f32) * logs[head])
    for i in range(total // TILE):
        rows = slice(i * TILE, (i + 1) * TILE)
        held = jnp.zeros((TILE, VD), f32)
        for j in range(i + 1):
            past = slice(j * TILE, (j + 1) * TILE)
            decay = block_decay(powers, head, i - j, base, row, column, after[rows, :], before[:, past])
            scores = dot_nt(kept[rows, :KD], kept[past, KD : 2 * KD])
            held = held + dot((decay * scores).astype(low), kept[past, 2 * KD :])
        normed, inverse = layer_norm(held, group_floor)
        grouped[rows, :] = normed
        scale[rows, :] = jnp.broadcast_to(inverse, (TILE, 128))
        gate = pre[rows, 2 * KD + VD :]
        mixed[rows, :] = (gate * jax.nn.sigmoid(gate) * normed).astype(low)


def retain(pre, consts, heads):
    total = pre.shape[0]
    powers, logs, cosine, sine, after, before = consts
    whole = lambda a: pl.BlockSpec(a.shape, lambda h: (0, 0))
    smem = pl.BlockSpec(memory_space=pltpu.SMEM)
    by_head = lambda width: pl.BlockSpec((total, width), lambda h: (0, h))
    shape = lambda width, kind: jax.ShapeDtypeStruct((total, heads * width), kind)
    return call(
        retain_kernel,
        (heads,),
        [smem, smem, by_head(2 * KD + 2 * VD), whole(cosine), whole(sine), whole(after), whole(before)],
        [by_head(VD), by_head(2 * KD + VD), by_head(VD), by_head(128)],
        [shape(VD, low), shape(2 * KD + VD, low), shape(VD, f32), shape(128, f32)],
        56,
    )(*consts[:2], pre, *consts[2:])


def retain_back_kernel(
    powers, logs, grad, gates, kept, grouped, scale, cosine, sine, after, before, out, grad_low, grad_q, grad_k, grad_v
):
    head = pl.program_id(0)
    total = kept.shape[0]
    half = KD // 2
    blocks = total // TILE
    for i in range(blocks):
        rows = slice(i * TILE, (i + 1) * TILE)
        gate, normed, given = gates[rows, :], grouped[rows, :], grad[rows, :]
        sigmoid = jax.nn.sigmoid(gate)
        out[rows, 2 * KD + VD :] = (
            given * normed * sigmoid * (1.0 + gate * (1.0 - sigmoid))
        ).astype(low)
        grad_low[rows, :] = norm_back(given * (gate * sigmoid), normed, scale[rows, :1]).astype(low)
    row, column = place_masks(TILE)
    base = jnp.exp((row - column).astype(f32) * logs[head])
    for i in range(blocks):
        rows = slice(i * TILE, (i + 1) * TILE)
        query, grad_rows = kept[rows, :KD], grad_low[rows, :]
        held = jnp.zeros((TILE, KD), f32)
        for j in range(i + 1):
            past = slice(j * TILE, (j + 1) * TILE)
            decay = block_decay(powers, head, i - j, base, row, column, after[rows, :], before[:, past])
            key, value = kept[past, KD : 2 * KD], kept[past, 2 * KD :]
            weights = (decay * dot_nt(query, key)).astype(low)
            grad_scores = (dot_nt(grad_rows, value) * decay).astype(low)
            held = held + dot(grad_scores, key)
            key_term, value_term = dot_tn(grad_scores, query), dot_tn(weights, grad_rows)
            if i == j:
                grad_k[past, :], grad_v[past, :] = key_term, value_term
            else:
                grad_k[past, :] += key_term
                grad_v[past, :] += value_term
        grad_q[rows, :] = held
    cos, sin = cosine[...], sine[...]
    for first, source, factor in ((0, grad_q, KD ** (-0.5)), (KD, grad_k, 1.0)):
        a, b = source[:, :half] * factor, source[:, half:] * factor
        out[:, first : first + half] = (a * cos + b * sin).astype(low)
        out[:, first + half : first + KD] = (b * cos - a * sin).astype(low)
    out[:, 2 * KD : 2 * KD + VD] = grad_v[...].astype(low)


def retain_back(grad, pre, kept, grouped, scale, consts, heads):
    total = pre.shape[0]
    powers, logs, cosine, sine, after, before = consts
    whole = lambda a: pl.BlockSpec(a.shape, lambda h: (0, 0))
    smem = pl.BlockSpec(memory_space=pltpu.SMEM)
    by_head = lambda width: pl.BlockSpec((total, width), lambda h: (0, h))
    return call(
        retain_back_kernel,
        (heads,),
        [smem, smem, by_head(VD), pl.BlockSpec((total, VD), lambda h: (0, 3 * h + 2))]
        + [by_head(2 * KD + VD), by_head(VD), by_head(128)]
        + [whole(cosine), whole(sine), whole(after), whole(before)],
        by_head(2 * KD + 2 * VD),
        jax.ShapeDtypeStruct((total, heads * (2 * KD + 2 * VD)), low),
        56,
        scratch=[
            pltpu.VMEM((total, VD), low),
            pltpu.VMEM((total, KD), f32),
            pltpu.VMEM((total, KD), f32),
            pltpu.VMEM((total, VD), f32),
        ],
    )(*consts[:2], grad, pre, kept, grouped, scale, *consts[2:])


def feed_kernel(feeds, steps, *refs):
    given, weights = refs[:4], refs[4 : 4 + 4 * feeds]
    outs = refs[4 + 4 * feeds : 4 + 7 * feeds]
    own, sent = refs[4 + 7 * feeds : 6 + 7 * feeds]
    rows, cots, held, grads, total, row_sems, sems = refs[6 + 7 * feeds :]
    count, width = rows.shape
    depth, size = width // 4, held.shape[2] // 3
    step = pl.program_id(0)

    def row_copies():
        places = [(buffer, first) for buffer in (rows, cots) for first in (0, count // 2)]
        return [
            pltpu.make_async_copy(ref, buffer.at[pl.ds(first, count // 2)], row_sems.at[i])
            for i, (ref, (buffer, first)) in enumerate(zip(given, places))
        ]

    def weight_copies(number, tile, slot):
        columns = weights[0].shape[1] // 3
        return [
            pltpu.make_async_copy(
                weights[4 * number + part].at[:, pl.ds(pl.multiple_of(kind * columns + tile * size, size), size)],
                held.at[slot, pl.ds(part * depth, depth), pl.ds(kind * size, size)],
                sems.at[slot, 4 * kind + part],
            )
            for kind in range(3)
            for part in range(4)
        ]

    def for_step(at, act):
        for number in range(feeds):

            @pl.when((at >= number * steps) & (at < (number + 1) * steps))
            def _(number=number):
                for copy in weight_copies(number, at - number * steps, lax.rem(at, 2)):
                    act(copy)

    @pl.when(step == 0)
    def _():
        for copy in row_copies():
            copy.start()
        for_step(step, lambda copy: copy.start())

    for_step(step + 1, lambda copy: copy.start())

    @pl.when(step == 0)
    def _():
        for copy in row_copies():
            copy.wait()

    for_step(step, lambda copy: copy.wait())
    weight = held.at[lax.rem(step, 2)]
    up = weight[:, : 2 * size]
    both, grad_hidden = dot(rows[...], up), dot(cots[...], weight[:, 2 * size :])
    act, lin = both[:, :size], both[:, size:]
    curve = jnp.tanh(gelu_slope * (act + gelu_cubic * act * act * act))
    gelu = 0.5 * act * (1.0 + curve)
    slope = 0.5 * (1.0 + curve) + (0.5 * gelu_slope) * act * (1.0 - curve * curve) * (
        1.0 + (3.0 * gelu_cubic) * act * act
    )
    hidden = (gelu * lin).astype(low)
    grads[:, :size] = (grad_hidden * lin * slope).astype(low)
    grads[:, size:] = (grad_hidden * gelu).astype(low)
    for number in range(feeds):

        @pl.when((step >= number * steps) & (step < (number + 1) * steps))
        def _(number=number):
            outs[3 * number][...] = hidden
            outs[3 * number + 1][...] = grads[:, :size]
            outs[3 * number + 2][...] = grads[:, size:]

    add = dot_nt(grads[...], up)

    @pl.when(step == 0)
    def _():
        total[...] = add

    @pl.when(step != 0)
    def _():
        total[...] += add

    @pl.when(step == pl.num_programs(0) - 1)
    def _():
        own[...] = total[: count // 2, :]
        sent[...] = total[count // 2 :, :].astype(low)


def feed(rows, cots, feeds):
    count, width = rows[0].shape
    columns = feeds[0][0].shape[1] // 3
    size = min(512, columns)
    steps, number = columns // size, len(feeds)
    full = pl.BlockSpec((count, width), lambda t: (0, 0))
    anywhere = pl.BlockSpec(memory_space=pl.ANY)
    tiles = [
        pl.BlockSpec((2 * count, size), lambda t, k=k: (0, jnp.clip(t - k * steps, 0, steps - 1)))
        for k in range(number)
    ]
    shape = jax.ShapeDtypeStruct((2 * count, columns), low)
    outs = call(
        functools.partial(feed_kernel, number, steps),
        (number * steps,),
        [anywhere] * (4 + 4 * number),
        [tile for tile in tiles for _ in range(3)] + [full, full],
        [shape] * (3 * number)
        + [jax.ShapeDtypeStruct((count, width), f32), jax.ShapeDtypeStruct((count, width), low)],
        56,
        scratch=[
            pltpu.VMEM((2 * count, width), low),
            pltpu.VMEM((2 * count, width), low),
            pltpu.VMEM((2, width, 3 * size), low),
            pltpu.VMEM((2 * count, 2 * size), low),
            pltpu.VMEM((2 * count, width), f32),
            pltpu.SemaphoreType.DMA((4,)),
            pltpu.SemaphoreType.DMA((2, 12)),
        ],
    )(*rows, *cots, *[part for weight in feeds for part in weight])
    return [outs[3 * k : 3 * k + 3] for k in range(number)], outs[-2], outs[-1]


def out_kernel(number, *refs):
    hiddens, weights, base = refs[:number], refs[number : 5 * number], refs[5 * number]
    own, sent = refs[5 * number + 1 :]
    half = own.shape[0]

    def give(part):
        total = sum(dot_nt(hiddens[i][...], weights[4 * i + part][...]) for i in range(number))
        own[...] = base[...] + total[:half]
        sent[...] = total[half:].astype(low)

    for part in range(4):
        pl.when(pl.program_id(0) == part)(functools.partial(give, part))


def out_rows(hiddens, feeds, base):
    count, width = base.shape
    columns = hiddens[0].shape[1]
    size = min(256, width // 4)
    steps = width // 4 // size
    tile = pl.BlockSpec((count, size), lambda i, j: (0, i * steps + j))
    return call(
        functools.partial(out_kernel, len(hiddens)),
        (4, steps),
        [pl.BlockSpec((2 * count, columns), lambda i, j: (0, 0))] * len(hiddens)
        + part_specs((size, columns), steps, 2) * len(hiddens)
        + [tile],
        [tile, tile],
        [jax.ShapeDtypeStruct((count, width), f32), jax.ShapeDtypeStruct((count, width), low)],
        56,
    )(*hiddens, *[weight for parts in feeds for weight in parts], base)


def gradient_kernel(plan, added, came_steps, places, *refs):
    number = sum(pieces for pieces, _, _ in plan)
    lefts, rights = refs[:number], refs[number : number + sum(len(r) for _, r, _ in plan)]
    rest = refs[number + len(rights) :]
    came, outs, turned = rest[:added], rest[added:-1], rest[-1]
    step = pl.program_id(0)
    first = left_at = right_at = 0
    for pieces, lengths, size in plan:

        @pl.when(step == first)
        def _(left_at=left_at, pieces=pieces, size=size):
            for i in range(left_at, left_at + pieces):
                start = pl.multiple_of(places[i] * size, size) if pieces > 1 else 0
                turned[:, pl.ds(start, size)] = lefts[i][...].T

        for length in lengths:

            @pl.when((step >= first) & (step < first + length))
            def _(right=rights[right_at], depth=pieces * size):
                result = dot(turned[:, :depth], right[...])
                if added:
                    result = result + jnp.where(step < came_steps, came[0][...].astype(f32), 0.0)
                height = result.shape[0] // len(outs)
                for i, out in enumerate(outs):
                    out[...] = result[i * height : (i + 1) * height].astype(low)

            first, right_at = first + length, right_at + 1
        left_at += pieces


def weight_gradient(groups, side, came=None, pieces_out=4):
    width = groups[0][0][0].shape[1]
    half = width // 2
    count = max(pieces[0].shape[0] * len(pieces) for pieces, _, _ in groups)
    columns = sum(right.shape[1] for _, _, rights in groups for right in rights)
    size = min(512, min(right.shape[1] for _, _, rights in groups for right in rights))
    plan, lefts, rights, left_specs, right_specs, places, first = [], [], [], [], [], [], 0
    for pieces, at, given in groups:
        plan.append((len(pieces), [right.shape[1] // size for right in given], pieces[0].shape[0]))
        lefts += pieces
        places += at
        whole = pieces[0].shape[1] == width
        spec = pl.BlockSpec((pieces[0].shape[0], half), lambda t, _, whole=whole: (0, side if whole else 0))
        left_specs += [spec] * len(pieces)
        for right in given:
            steps = right.shape[1] // size
            right_specs.append(
                pl.BlockSpec(
                    (right.shape[0], size),
                    lambda t, _, first=first, steps=steps: (0, jnp.clip(t - first, 0, steps - 1)),
                )
            )
            rights.append(right)
            first += steps
    parts = 1 if came is None else pieces_out
    tile = lambda height: pl.BlockSpec((height, size), lambda t, _: (0, t))
    more = [] if came is None else [came]
    came_steps = 0 if came is None else came.shape[1] // size
    came_specs = [pl.BlockSpec((half, size), lambda t, _: (0, jnp.minimum(t, came_steps - 1)))] * len(more)
    outs = call(
        functools.partial(gradient_kernel, plan, len(more), came_steps),
        (columns // size,),
        left_specs + right_specs + came_specs,
        [tile(half // parts)] * parts,
        [jax.ShapeDtypeStruct((half // parts, columns), low)] * parts,
        56,
        scratch=[pltpu.VMEM((half, count), low)],
        scalars=1,
    )(jnp.stack(places), *lefts, *rights, *more)
    return outs[0] if came is None else [outs[: parts // 2], outs[parts // 2 :]]


def shards(
    inputs,
    gain_attn,
    w_query,
    w_key,
    w_value,
    w_gate,
    w_out,
    gain_mlp,
    w_act,
    w_lin,
    w_down,
    cotangent,
    lengths,
    offsets,
):
    rows, width = inputs.shape
    dp_size, tensor_size = lax.axis_size("dp"), lax.axis_size("tensor")
    dp_own, tensor_own = lax.axis_index("dp"), lax.axis_index("tensor")
    total = rows * tensor_size
    heads = w_query.shape[1] // KD
    hidden_cols = w_act.shape[1]
    half = width // 2

    order = feature_order(dp_size)
    taken = jnp.array([k for k, _ in order], jnp.int32)
    parts = jnp.array([i for _, i in order], jnp.int32)
    table = (taken ^ dp_own) * 2 + parts
    place = {pair: i for i, pair in enumerate(order)}
    places = jnp.array([[place[k, i] for i in range(2)] for k in range(dp_size)], jnp.int32)
    back = places[jnp.arange(dp_size, dtype=jnp.int32) ^ dp_own].reshape(-1)

    x_low = reorder(inputs, table)
    normed_one = normed_rows(x_low)
    stride = 2 * KD + 2 * VD
    head_blocks = []
    for h in range(heads):
        head_blocks += [(w_query, h * KD, KD), (w_key, h * KD, KD)]
        head_blocks += [(w_value, h * VD, VD), (w_gate, h * VD, VD)]
    pair_blocks = range(0, tensor_size, 2)

    head_first = tensor_own * heads
    head_numbers = (head_first + jnp.arange(heads, dtype=jnp.int32)).astype(f32)
    log_decay = jnp.log(1.0 - jnp.exp2(-5.0 - head_numbers))
    segment, position = sequence_layout(lengths[0], offsets[0], total)
    cosine, sine = rotation(position, KD)
    powers = jnp.exp(
        jnp.arange(total // TILE, dtype=f32)[None, :] * TILE * log_decay[:, None]
    )
    consts = (powers, log_decay, cosine, sine, segment[:, None], segment[None, :])
    ring_places = [(tensor_own - step) % tensor_size for step in range(tensor_size)]

    gains = jnp.concatenate([gain_attn.reshape(2, -1), gain_mlp.reshape(2, -1)], axis=1)
    parts = [gains[:1], gains[1:]]
    for bits in dp_bits(dp_size):
        parts = [
            jnp.concatenate([part, swap(part, "dp", bit, "gains")], axis=0)
            for part, bit in zip(sync(*parts), bits)
        ]
    gains_same = jnp.concatenate(parts, axis=0)
    gains = jnp.concatenate([gains_same, swap(gains_same, "dp", 1, "gains")], axis=0).astype(f32)
    fine = gains.shape[1] // 2
    gain_one, gain_two = gains[:, :fine].reshape(-1), gains[:, fine:].reshape(-1)

    w_in = gather_step(column_blocks(head_blocks), 0, "w_in")
    late_act, late_lin, late_down, late_out, late_cot = tie(
        (w_act, w_lin, w_down, w_out, cotangent), normed_one
    )
    feed_parts = column_blocks(
        [(late_act, 0, hidden_cols), (late_lin, 0, hidden_cols), (late_down.T, 0, hidden_cols)]
    )
    wo = column_blocks([(late_out.T, 0, w_out.shape[0])])
    cot = reorder(late_cot, table)

    def beside_attn(step, came):
        nonlocal w_in, wo, cot, feed_parts, consts
        if step == 1:
            came, w_in, wo, cot, feed_parts, consts = sync(came, w_in, wo, cot, feed_parts, consts)
            w_in = gather_rest(w_in, 1, "w_in", consts)
            wo = gather_step(tie(wo, w_in), 0, "w_out")
        return came

    pieces = gather_ring(normed_one, "rows_attn", beside_attn)
    rows_here, w_in, wo, feed_parts, gain_one, gain_two = sync(
        pieces[-1], w_in, wo, feed_parts, gain_one, gain_two
    )
    pieces[-1] = rows_here

    def swap_far(part):
        return {k: swap(part, "tensor", k, "w_feed_far") for k in pair_blocks[1:]}

    cot_came = swap(tie(cotangent, rows_here), "tensor", 1, "rows_cot")
    upper = swap_far(feed_parts[0])
    w_in = gather_core(w_in, "w_in")
    h_pieces = [scale_rows(piece, gain_one) for piece in pieces]
    pre = project(h_pieces[:-1], w_in, None, ring_places[:-1], tensor_size)
    wo = gather_rest(wo, 1, "w_out", pre)
    pre, cot_came, upper, wo, feed_parts = sync(pre, cot_came, upper, wo, feed_parts)
    wo = gather_core(wo, "w_out")

    lower = swap_far(tie(feed_parts[1], upper))
    pre = project(h_pieces[-1:], w_in, pre, ring_places[-1:], tensor_size)
    mixed, kept, grouped, scale = retain(pre, consts, heads)
    near_feed = gather_step(feed_parts, 0, "w_feed_near", mixed)
    near_feed = gather_rest(near_feed, 1, "w_feed_near")
    sum_places = scatter_places()
    (total_out,) = terms(mixed, wo, sum_places[:1], rows, [low], None)
    rest_out = terms(tie(mixed, total_out), wo, sum_places[1:], rows, [f32] * (tensor_size - 1), None)
    cots = [cot, reorder(tie(cot_came, total_out), table)]
    total_out, lower, cots = sync(total_out, lower, cots)
    far_feeds = {k: gather_step([upper[k], lower[k]], 0, "w_feed_far") for k in upper}

    def beside_out(step, total):
        nonlocal far_feeds, near_feed
        if step == 1:
            total, far_feeds = sync(total, far_feeds)
            far_feeds = {k: gather_rest(v, 1, "w_feed_far") for k, v in far_feeds.items()}
        if step == 2:
            total, near_feed = sync(total, near_feed)
            near_feed = gather_core(near_feed, "w_feed_near")
        if step == tensor_size - 1:
            total, far_feeds = sync(total, far_feeds)
            far_feeds = {k: gather_core(v, "w_feed_far") for k, v in far_feeds.items()}
        return total

    attn_came, attn_own = scatter_ring(total_out, rest_out, "sum_attn", beside_out)

    middle, h_mlp = norm_rows(x_low, attn_came, attn_own, gain_two)
    h_came = swap(h_mlp, "tensor", 1, "rows_mlp")
    feeds = [near_feed] + [far_feeds[k] for k in pair_blocks[1:]]
    h_pair = [h_mlp, h_came]
    results, grad_h, grad_send = feed(h_pair, cots, feeds)
    grad_came = swap(grad_send, "tensor", 1, "sum_grad_mlp")

    late, late_rows, late_cots = tie((results, h_pair, cots), grad_send)
    pair_places = [jnp.zeros((), jnp.int32), jnp.ones((), jnp.int32)]

    def feed_groups(result):
        hidden, grad_act, grad_lin = result
        return [
            (late_rows, pair_places, [grad_act, grad_lin]),
            (late_cots, pair_places, [hidden]),
        ]

    far = {k: weight_gradient(feed_groups(late[k // 2]), 1) for k in pair_blocks[1:]}
    near_other = weight_gradient(feed_groups(late[0]), 1)
    grad_came, far, near_other = sync(grad_came, far, near_other)
    far_came = {k: swap(other, "dp", 1, "grad_feed_far") for k, other in far.items()}
    near_came = None
    grad_middle, gain_two_term, grad_mid_low = norm_back_rows(
        middle, cot, gain_two, grad_h, grad_came, True
    )

    grad_mixed = out_own = out_send = None
    mid_pieces = [grad_mid_low]

    def beside_mid(step, came):
        nonlocal far, near_came, grad_mixed, out_own, out_send
        if step == 1:
            late = tie(results, grad_mid_low)
            far = {
                k: weight_gradient(feed_groups(late[k // 2]), 0, far_came[k])
                for k in pair_blocks[1:]
            }
            came, far, near_last = sync(came, far, near_other)
            near_came = swap(near_last, "dp", 1, "grad_feed_near")
            far = {k: scatter_step(v, 0, "grad_feed_far") for k, v in far.items()}
        if step == 2:
            late, weights = tie((results, feeds), mid_pieces[1])
            out_own, out_send = out_rows([result[0] for result in late], weights, middle)
            near_came = weight_gradient(feed_groups(late[0]), 0, near_came)
            came, out_own, out_send, near_came = sync(came, out_own, out_send, near_came)
        if step == tensor_size - 1:
            late = tie(mid_pieces, mid_pieces[-1])
            grad_mixed = project(late, wo, None, ring_places[:step], tensor_size)
            came, far, grad_mixed = sync(came, far, grad_mixed)
        mid_pieces.append(came)
        return came

    mid_pieces = gather_ring(grad_mid_low, "rows_grad_mid", beside_mid)
    out_came = swap(tie(out_send, mid_pieces[-1]), "tensor", 1, "sum_out")
    far = {k: scatter_rest(v, 1, "grad_feed_far") for k, v in far.items()}

    grad_mixed = project(mid_pieces[-1:], wo, grad_mixed, ring_places[-1:], tensor_size)
    grad_in = retain_back(grad_mixed, pre, kept, grouped, scale, consts, heads)

    grad_in, out_came, far, near = sync(grad_in, out_came, far, near_came)
    near = scatter_step(near, 0, "grad_feed_near")
    upper = {k: join(*parts[:2]) for k, parts in far.items()}
    lower = {k: join(*parts[2:]) for k, parts in far.items()}
    gain_places = [jnp.zeros((), jnp.int32)]
    gain_columns = jnp.eye(16, TILE, dtype=low)

    def out_groups(right):
        return [(mid_pieces, ring_places, [right])]

    def swap_grad(parts):
        return {k: swap(part, "tensor", k, "grad_feed_far") for k, part in parts.items()}

    upper, lower_sent = swap_grad(upper), lower
    first_pairs, rest_pairs = h_pieces[1:2], h_pieces[2:] + h_pieces[:1]
    total_in, more = terms(grad_in, w_in, sum_places[:1], rows, [low], first_pairs)
    late_in = tie(grad_in, total_in)
    in_other = weight_gradient([(h_pieces, ring_places, [late_in])], 1)
    out_other = weight_gradient(out_groups(tie(mixed, in_other)), 1)
    total_in, upper, in_other, out_other, near, lower_sent = sync(
        total_in, upper, in_other, out_other, near, lower_sent
    )
    lower = swap_grad(lower_sent)
    in_other = swap(in_other, "dp", 1, "grad_w_in")
    out_other = swap(out_other, "dp", 1, "grad_w_out")
    *rest_in, more_rest = terms(
        tie(grad_in, total_in), w_in, sum_places[1:], rows, [f32] * (tensor_size - 1), rest_pairs
    )
    late_in = tie(grad_in, more_rest)
    grads_in = weight_gradient([(h_pieces, ring_places, [late_in])], 0, in_other, 8)
    near = scatter_step(near, 1, "grad_feed_near", grads_in)
    total_in, lower, rest_in, grads_in, near, out_other = sync(
        total_in, lower, rest_in, grads_in, near, out_other
    )
    first_bits = dp_bits(dp_size)[-1]
    sent_on = [
        swap(part[3], "dp", bit, "grad_w_in") for part, bit in zip(grads_in, first_bits)
    ]
    gain_rows = jnp.concatenate([(more + more_rest) / gain_one, gain_two_term], axis=0)
    gain_rows = gain_rows[:, :half] + swap(gain_rows[:, half:], "dp", 1, "gains")
    gain_rows = jnp.concatenate([gain_rows, jnp.zeros((14, half), f32)], axis=0).astype(low)
    grads_out = weight_gradient(
        out_groups(tie(mixed, total_in)) + [([gain_rows], gain_places, [gain_columns])], 0, out_other
    )
    out_sent = scatter_send(grads_out, 0, "grad_w_out")

    def beside_sum(step, total):
        nonlocal grads_in, grads_out, sent_on
        if step == 1:
            total, sent_on, grads_out = sync(total, sent_on, grads_out)
            kept_on = [
                swap(part[2], "dp", bit, "grad_w_in") for part, bit in zip(grads_in, first_bits)
            ]
            grads_in, sent_on = tie((grads_in, sent_on), total)
            sent_on = [
                add_rows(part[1], came, low) for part, came in zip(grads_in, sent_on)
            ]
            grads_in = [
                [add_rows(part[0], came, low), sent]
                for part, came, sent in zip(grads_in, kept_on, sent_on)
            ]
            grads_out = scatter_add(grads_out, tie(out_sent, total))
        return total

    hattn_came, hattn_own = scatter_ring(total_in, rest_in, "sum_grad_attn", beside_sum)
    (grad_inputs,) = norm_back_rows(x_low, grad_middle, gain_one, hattn_own, hattn_came, False)
    grad_inputs = reorder(grad_inputs, back)
    grads_out = scatter_rest(grads_out, 1, "grad_w_out")
    grads_in = scatter_rest(tie(grads_in, grads_out), 1, "grad_w_in", grad_inputs)
    near = scatter_rest(near, 2, "grad_feed_near")
    grad_out_own = jnp.concatenate(grads_out, axis=0).astype(f32)
    columns = w_out.shape[0]
    grad_wo_own, gain_sum = grad_out_own[:, :columns], grad_out_own[:, columns : columns + 2].T
    gain_came = [swap(gain_sum, "tensor", k, "gains") for k in range(1, tensor_size)]
    gain_sums = [gain_sum] + tie(gain_came, grad_inputs)
    while len(gain_sums) > 1:
        gain_sums = [a + b for a, b in zip(gain_sums[::2], gain_sums[1::2])]
    gain_sum = gain_sums[0]
    grad_in_own = jnp.concatenate(grads_in, axis=0).astype(f32)
    grad_feed = jnp.concatenate(near, axis=0).astype(f32)
    for k in pair_blocks[1:]:
        grad_feed = grad_feed + jnp.concatenate([upper[k], lower[k]], axis=0).astype(f32)
    outputs = out_own + out_came.astype(f32)

    def heads_back(first, size):
        return jnp.concatenate(
            [grad_in_own[:, h * stride + first : h * stride + first + size] for h in range(heads)],
            axis=1,
        )

    return (
        reorder(outputs.astype(low), back),
        grad_inputs,
        gain_sum[0],
        heads_back(0, KD),
        heads_back(KD, KD),
        heads_back(2 * KD, VD),
        heads_back(2 * KD + VD, VD),
        grad_wo_own.T,
        gain_sum[1],
        grad_feed[:, :hidden_cols],
        grad_feed[:, hidden_cols : 2 * hidden_cols],
        grad_feed[:, 2 * hidden_cols :].T,
    )


def solution(mesh):
    return jax.shard_map(
        shards,
        mesh=mesh,
        in_specs=(
            P(("dp", "tensor"), None),
            P("dp"),
            P("dp", "tensor"),
            P("dp", "tensor"),
            P("dp", "tensor"),
            P("dp", "tensor"),
            P("tensor", "dp"),
            P("dp"),
            P("dp", "tensor"),
            P("dp", "tensor"),
            P("tensor", "dp"),
            P(("dp", "tensor"), None),
            P("dp", None),
            P("dp", None),
        ),
        out_specs=(
            P(("dp", "tensor"), None),
            P(("dp", "tensor"), None),
            P("dp"),
            P("dp", "tensor"),
            P("dp", "tensor"),
            P("dp", "tensor"),
            P("dp", "tensor"),
            P("tensor", "dp"),
            P("dp"),
            P("dp", "tensor"),
            P("dp", "tensor"),
            P("tensor", "dp"),
        ),
        check_vma=False,
    )
```
